32 devices in a mesh: stu: 4 (over y, x), que: 8 (over z, core).
Axes of the slice: x: 2, y: 2, z: 4, core: 2. Of those that a mesh axis runs over, the one named last changes fastest.
Arguments:
- codes: int32 [1024, 1024], P('stu', 'que'), may hold values from 0 to 2
- theta: float32 [1024, 64], P(('stu', 'que')), may hold values from -6 to 6
- disc: float32 [1024, 64], P(('que', 'stu')), may hold values from -0.75 to 0.75
- intercept: float32 [1024], P(('que', 'stu')), may hold values from -5 to 5
Outputs:
- step_abilities: float32 [1024, 64], P(('stu', 'que'))
- step_disc: float32 [1024, 64], P(('que', 'stu'))
- step_intercept: float32 [1024], P(('que', 'stu'))
The draws below stay inside these ranges and needn't reach their ends.
All inputs are finite; a program needn't handle non-finite values.
Results may differ from the reference program's by a relative error of at most 0.0003.
Values sent between devices are 32-bit elements; how exact they have to be, the bound alone decides.
No kernel may reach another device: no remote copies, remote signals or barrier semaphores. Data moves between devices by JAX's collectives and lax.ppermute only.
A program may use at most 64 MiB of HBM per device.

```python
import jax
import jax.numpy as jnp
from jax import lax

K = 64
TILE_S = 256
ITERS = 2
STUDENTS = 1024
QUESTIONS = 1024
N_STU = 4


def with_ends(entries, stream_key, least, high):
    dims = entries.shape
    index_at = [jax.random.randint(jax.random.fold_in(stream_key, axis), (), 0, dims[axis]) for axis in range(len(dims))]
    entries = entries.at[tuple(index_at)].set(least)
    longest = dims.index(max(dims))
    index_at[longest] = (index_at[longest] + 1) % dims[longest]
    return entries.at[tuple(index_at)].set(high)


def levels(stream_key, extent, cuts, least, high):
    gain = 1.0
    for position, shards_of in cuts:
        steps = jax.random.uniform(jax.random.fold_in(jax.random.fold_in(stream_key, 6), position), (shards_of,), jnp.float32, least / len(cuts), high / len(cuts))
        gain = gain * jnp.repeat(jnp.exp(steps), extent[position] // shards_of).reshape((-1,) + (1,) * (len(extent) - 1 - position))
    return gain


def normal_values(stream_key, extent, scale, limit, cuts=(), dtype=jnp.bfloat16):
    values = scale * jax.random.normal(stream_key, extent, jnp.float32)
    if cuts:
        values = values * levels(stream_key, extent, cuts, -0.22, 0.18)
    return jnp.clip(values, -limit, limit).astype(dtype)


def setup_inputs(seed: int = 0) -> dict:
    splits = jax.random.split(jax.random.key(seed), 5)
    return {
        "codes": with_ends(jax.random.randint(splits[0], (STUDENTS, QUESTIONS), 0, 3), jax.random.fold_in(splits[0], 1), 0, 2).astype(jnp.int32),
        "theta": normal_values(splits[1], (STUDENTS, K), 1.0, 6.0, ((0, 32),), jnp.float32),
        "disc": normal_values(splits[2], (QUESTIONS, K), K ** -0.5, 0.75, ((0, 32),), jnp.float32),
        "intercept": normal_values(splits[3], (QUESTIONS,), 1.0, 5.0, ((0, 32),), jnp.float32),
    }


HIGH = lax.Precision.HIGHEST

def matmul(left, right):
    return jnp.dot(left, right, precision=HIGH, preferred_element_type=jnp.float32)

def contract_rows(left, right):
    return lax.dot_general(left, right, (((0,), (0,)), ((), ())), precision=HIGH, preferred_element_type=jnp.float32)

def block_terms(code_blk, theta_blk, disc, intercept):
    logit = matmul(theta_blk, disc.T) + intercept[None, :]
    prob = jax.nn.sigmoid(logit)
    observed = (code_blk > 0).astype(jnp.float32)
    correct = (code_blk == 2).astype(jnp.float32)
    return (observed * (prob - correct), observed * prob * (1.0 - prob))

def reference(codes, theta, disc, intercept):
    blocks = codes.reshape(N_STU, TILE_S, QUESTIONS)
    theta_blocks = theta.reshape(N_STU, TILE_S, K)
    zero_cols = (jnp.zeros((QUESTIONS, K), jnp.float32), jnp.zeros((QUESTIONS, K), jnp.float32), jnp.zeros((QUESTIONS,), jnp.float32), jnp.zeros((QUESTIONS,), jnp.float32))

    def grad_step(carry, item):
        code_blk, theta_blk = item
        resid, weight = block_terms(code_blk, theta_blk, disc, intercept)
        rows = (matmul(resid, disc), matmul(weight, disc * disc))
        cols = (contract_rows(resid, theta_blk), contract_rows(weight, theta_blk * theta_blk), lax.optimization_barrier(jnp.sum(resid, 0)), lax.optimization_barrier(jnp.sum(weight, 0)))
        return (jax.tree.map(lambda u, v: u + v, carry, cols), rows)
    cols, rows = lax.scan(grad_step, zero_cols, (blocks, theta_blocks))
    grad = (rows[0].reshape(STUDENTS, K) + theta, cols[0] + disc, cols[2] + intercept)
    diag = (rows[1].reshape(STUDENTS, K) + 1.0, cols[1] + 1.0, cols[3] + 1.0)

    def apply_hessian(vec):
        vt_blocks = vec[0].reshape(N_STU, TILE_S, K)

        def hess_step(carry, item):
            code_blk, theta_blk, vt_blk = item
            resid, weight = block_terms(code_blk, theta_blk, disc, intercept)
            change = matmul(vt_blk, disc.T) + matmul(theta_blk, vec[1].T) + vec[2][None, :]
            scaled = weight * change
            cols_now = (contract_rows(scaled, theta_blk), lax.optimization_barrier(jnp.sum(scaled, 0)))
            return ((carry[0] + cols_now[0], carry[1] + cols_now[1]), matmul(scaled, disc))
        start = (jnp.zeros((QUESTIONS, K), jnp.float32), jnp.zeros((QUESTIONS,), jnp.float32))
        col_part, row_part = lax.scan(hess_step, start, (blocks, theta_blocks, vt_blocks))
        return (row_part.reshape(STUDENTS, K) + vec[0], col_part[0] + vec[1], col_part[1] + vec[2])

    def inner(left, right):
        return jnp.sum(left[0] * right[0]) + jnp.sum(left[1] * right[1]) + jnp.sum(left[2] * right[2])
    solution = jax.tree.map(jnp.zeros_like, grad)
    residual = jax.tree.map(lambda u: -u, grad)
    precond = jax.tree.map(lambda u, d: u / d, residual, diag)
    direction = precond
    norm_now = inner(residual, precond)
    for step in range(ITERS):
        image = apply_hessian(direction)
        alpha = norm_now / inner(direction, image)
        solution = jax.tree.map(lambda u, v: u + alpha * v, solution, direction)
        residual = jax.tree.map(lambda u, v: u - alpha * v, residual, image)
        if step + 1 < ITERS:
            precond = jax.tree.map(lambda u, d: u / d, residual, diag)
            norm_next = inner(residual, precond)
            ratio = norm_next / norm_now
            direction = jax.tree.map(lambda u, v: u + ratio * v, precond, direction)
            norm_now = norm_next
    result = jax.tree.map(lambda u, d: u * jnp.sqrt(d), solution, diag)
    return (result[0], result[1], result[2])
```

```python
import functools

import jax
import jax.numpy as jnp
from jax import lax
from jax.experimental import pallas as pl
from jax.experimental.pallas import tpu as pltpu
from jax.sharding import PartitionSpec as P

HIGH = lax.Precision.HIGHEST
AXES = ("stu", "que")
LANES = 128
BIAS = 8


def dot_nt(left, right):
    return lax.dot_general(
        left, right, (((1,), (1,)), ((), ())), precision=HIGH, preferred_element_type=jnp.float32
    )


def dot_nn(left, right):
    return jnp.dot(left, right, precision=HIGH, preferred_element_type=jnp.float32)


def position():
    que = lax.axis_index("que")
    return lax.rem(que, 2), que // 2, lax.axis_index("stu")


def block_of(side, core, line, plane, group):
    return jnp.where(side == 0, line * 2 + core, core * group + plane)


def low_lanes(shape):
    return lax.broadcasted_iota(jnp.int32, shape, 1) < LANES // 2


def turn(value):
    return pltpu.roll(value, LANES // 2, 1)


def pack(value):
    half = value.shape[0] // 2
    low = low_lanes((half, LANES))
    return jnp.where(low, value[:half], turn(value[half:]))


def bias_rows(lanes, mine):
    return jnp.where(mine, jnp.concatenate([lanes[0:1, :LANES], lanes[0:1, LANES:]], 0), 0.0)


def column(rows):
    wide = jnp.concatenate([rows, jnp.zeros((LANES - 2, LANES), jnp.float32)], 0)
    tall = wide.T
    return jnp.concatenate([tall[:, 0:1], tall[:, 1:2]], 0)


def arrange_kernel(own_ref, peer_ref, out_ref):
    core, _, _ = position()
    cols = own_ref.shape[1]

    @pl.when(core == 0)
    def _():
        out_ref[:, :cols] = own_ref[...].astype(jnp.float32)
        out_ref[:, cols:] = peer_ref[...].astype(jnp.float32)

    @pl.when(core == 1)
    def _():
        out_ref[:cols, :] = peer_ref[...].astype(jnp.float32).T
        out_ref[cols:, :] = own_ref[...].astype(jnp.float32).T


def place(src_ref, dst_ref, side, core, line, plane, group):
    rows = src_ref.shape[0] // (2 * group)
    for k in range(group):
        for j in range(2):
            at = block_of(side, core ^ j, line ^ k, plane ^ k, group) * rows
            first = (k * 2 + j) * rows
            dst_ref[pl.ds(pl.multiple_of(at, rows), rows), :] = src_ref[first : first + rows, :]


def gradient_kernel(group, mine_ref, other_ref, code_ref, sums_ref, left_ref, right_ref, weight_ref, icpt_ref):
    core, line, plane = position()
    place(mine_ref, left_ref, core, core, line, plane, group)
    place(other_ref, right_ref, 1 - core, 1 - core, line, plane, group)
    left = left_ref[...]
    right = right_ref[...]
    prob = 1.0 / (1.0 + jnp.exp(-dot_nt(left, right)))
    code = code_ref[...]
    seen = code > 0.0
    resid = jnp.where(seen, prob - jnp.where(code == 2.0, 1.0, 0.0), 0.0)
    weight = jnp.where(seen, prob * (1.0 - prob), 0.0)
    weight_ref[...] = weight
    rows = left.shape[0]
    grad = dot_nn(resid, right)
    diag = dot_nn(weight, right * right)
    sums_ref[:rows, :] = jnp.where(low_lanes((rows, LANES)), grad, turn(diag))
    ones = jnp.ones((8, rows), jnp.float32)
    mine = core == 1
    sums_ref[rows:, :] = jnp.concatenate(
        [
            bias_rows(dot_nt(ones, resid), mine),
            bias_rows(dot_nt(ones, weight), mine),
            jnp.zeros((BIAS - 4, LANES), jnp.float32),
        ],
        0,
    )
    pick = (lax.broadcasted_iota(jnp.int32, (8, LANES), 1) == LANES // 2).astype(jnp.float32)
    icpt = bias_rows(dot_nt(pick, left), mine)
    icpt_ref[...] = jnp.concatenate([icpt, jnp.zeros((BIAS - 2, LANES), jnp.float32)], 0)


def start_kernel(group, parts, *refs):
    sum_refs, (left_ref, icpt_ref, send_ref, diag_ref, root_ref) = refs[:parts], refs[parts:]
    core, line, plane = position()
    total = sum_refs[0][...]
    for ref in sum_refs[1:]:
        total = total + ref[...]
    rows = left_ref.shape[0]
    half = rows // 2
    low = low_lanes((rows, LANES))
    main = total[:rows]
    diag = jnp.where(low, turn(main) + 1.0, 1.0)
    first = jnp.where(low, -(main + left_ref[...]) / diag, 0.0)
    grad_b = total[rows : rows + 2] + icpt_ref[:2]
    diag_b = total[rows + 2 : rows + 4] + 1.0
    first_b = -grad_b / diag_b
    root_ref[...] = jnp.sqrt(diag)
    send_ref[:half, :] = pack(first)
    send_ref[half : half + BIAS, :] = jnp.concatenate(
        [first_b, jnp.sqrt(diag_b), jnp.zeros((BIAS - 4, LANES), jnp.float32)], 0
    )
    diag_ref[:half, :] = pack(diag)
    diag_ref[half:, :] = jnp.concatenate([diag_b, jnp.ones((BIAS - 2, LANES), jnp.float32)], 0)
    size = rows // (2 * group)
    at = block_of(core, 1 - core, line, plane, group) * size
    send_ref[half + BIAS :, :] = root_ref[pl.ds(pl.multiple_of(at, size), size), :]


def change_of(mine_ref, other_ref, left, right, half):
    low = low_lanes((half, LANES))
    mine = mine_ref[:half, :]
    other = other_ref[:half, :]
    lhs = jnp.concatenate(
        [
            jnp.where(low, mine, turn(left[:half])),
            jnp.where(low, turn(mine), turn(left[half:])),
        ],
        0,
    )
    rhs = jnp.concatenate(
        [
            jnp.where(low, right[:half], turn(other)),
            jnp.where(low, right[half:], other),
        ],
        0,
    )
    lanes = jnp.concatenate([other_ref[half : half + 1, :], other_ref[half + 1 : half + 2, :]], 1)
    return dot_nt(lhs, rhs) + lanes + column(mine_ref[half : half + 2, :])


def image_kernel(mine_ref, other_ref, left_ref, right_ref, weight_ref, sums_ref):
    core, _, _ = position()
    rows = left_ref.shape[0]
    half = rows // 2
    right = right_ref[...]
    scaled = weight_ref[...] * change_of(mine_ref, other_ref, left_ref[...], right, half)
    sums_ref[:half, :] = pack(dot_nn(scaled, right))
    ones = jnp.ones((8, rows), jnp.float32)
    sums_ref[half:, :] = jnp.concatenate(
        [bias_rows(dot_nt(ones, scaled), core == 1), jnp.zeros((BIAS - 2, LANES), jnp.float32)], 0
    )


def second_kernel(group, parts, *refs):
    sum_refs, (send_ref, diag_ref, second_ref, dots_ref) = refs[:parts], refs[parts:]
    total = sum_refs[0][...]
    for ref in sum_refs[1:]:
        total = total + ref[...]
    half = total.shape[0] - BIAS
    row = lax.broadcasted_iota(jnp.int32, total.shape, 0)
    used = row < half + 2
    first = jnp.where(used, send_ref[: half + BIAS, :], 0.0)
    diag = diag_ref[...]
    lift = jnp.where(used, total + first - diag * first, 0.0)
    second = lift / diag
    second_ref[...] = second
    scale = 1.0 / group
    lane = lax.broadcasted_iota(jnp.int32, (8, LANES), 1)
    dots = jnp.zeros((8, LANES), jnp.float32)
    for at, value in enumerate((first * first * diag, first * lift, second * lift, second * second)):
        dots = jnp.where(lane == at, jnp.sum(value) * scale, dots)
    dots_ref[...] = dots


def form_kernel(mine_ref, other_ref, left_ref, right_ref, weight_ref, dots_ref, out_ref):
    half = left_ref.shape[0] // 2
    change = change_of(mine_ref, other_ref, left_ref[...], right_ref[...], half)
    form = 0.5 * jnp.sum(weight_ref[...] * change * change)
    lane = lax.broadcasted_iota(jnp.int32, (1, LANES), 1)
    value = dots_ref[0:1, :] + jnp.where(lane == 3, form, 0.0)
    out_ref[...] = jnp.broadcast_to(value[None], out_ref.shape)


def finish_kernel(
    group, dots_ref, send_ref, peer_ref, second_ref, peer_second_ref, root_ref, theta_ref, disc_ref, icpt_ref
):
    core, line, plane = position()
    dots = jnp.sum(dots_ref[...], axis=0)
    lane = lax.broadcasted_iota(jnp.int32, (1, LANES), 1)
    a, f, h, d = [jnp.sum(jnp.where(lane == at, dots, 0.0), axis=1, keepdims=True) for at in range(4)]
    b = a + f
    e = f + h
    det = b * d - e * e
    s = (a * d - e * f) / det
    t = (f * f - a * h) / det
    rows = root_ref.shape[0]
    half = rows // 2
    size = rows // (2 * group)

    def direction(first_ref, next_ref, at):
        upper = at // group
        rows_at = pl.ds(pl.multiple_of(lax.rem(at, group) * size, size), size)
        value = s * first_ref[rows_at, :] + t * next_ref[rows_at, :]
        return jnp.where(upper == 1, turn(value), value)

    mine_at = block_of(core, core, line, plane, group)
    other_at = block_of(1 - core, core, line, plane, group)
    mine = direction(send_ref, second_ref, mine_at)
    mine = mine * root_ref[pl.ds(pl.multiple_of(mine_at * size, size), size), :]
    other = direction(peer_ref, peer_second_ref, other_at) * peer_ref[half + BIAS :, :]
    theta_ref[...] = jnp.where(core == 0, mine, other)[:, : LANES // 2]
    disc_ref[...] = jnp.where(core == 0, other, mine)[:, : LANES // 2]
    ask = jnp.where(core == 0, peer_ref[half : half + BIAS, :], send_ref[half : half + BIAS, :])
    ask_next = jnp.where(core == 0, peer_second_ref[half : half + 2, :], second_ref[half : half + 2, :])
    bias = (s * ask[0:2] + t * ask_next) * ask[2:4]
    disc_at = jnp.where(core == 0, other_at, mine_at)
    row = jnp.where(disc_at // group == 1, bias[1:2], bias[0:1])
    back = lax.rem(LANES - lax.rem(disc_at, group) * size, LANES)
    icpt_ref[...] = jnp.broadcast_to(pltpu.roll(row, back, 1), icpt_ref.shape)


def call(kernel, shapes, *args):
    out = [jax.ShapeDtypeStruct(shape, jnp.float32) for shape in shapes]
    return pl.pallas_call(
        kernel,
        out_shape=out,
        in_specs=[pl.BlockSpec(memory_space=pltpu.VMEM)] * len(args),
        out_specs=[pl.BlockSpec(memory_space=pltpu.VMEM)] * len(out),
        compiler_params=pltpu.CompilerParams(vmem_limit_bytes=32 * 2**20),
    )(*args)


def swap_cores(value, n_stu, n_que):
    return lax.ppermute(value, AXES, [(i, i ^ 1) for i in range(n_stu * n_que)])


def send_over(value, step, n_stu, n_que):
    pairs = []
    for stu in range(n_stu):
        for que in range(n_que):
            there = (stu, que ^ (2 * step)) if que % 2 == 0 else (stu ^ step, que)
            pairs.append((stu * n_que + que, there[0] * n_que + there[1]))
    return lax.ppermute(value, AXES, pairs)


def stages(group):
    base = 1
    while base < group:
        width = min(4, group // base)
        yield [base * k for k in range(1, width)]
        base *= width


def shards(n_stu, n_que, codes, theta, disc, intercept):
    group = n_stu
    assert n_que == 2 * group
    send = functools.partial(send_over, n_stu=n_stu, n_que=n_que)
    swap = functools.partial(swap_cores, n_stu=n_stu, n_que=n_que)
    size, width = theta.shape
    rows = 2 * group * size
    half = rows // 2
    assert width == LANES // 2 and rows == 2 * LANES
    assert disc.shape == theta.shape and codes.shape == (rows, half)
    core = lax.rem(lax.axis_index("que"), 2)
    pad = jnp.zeros((size, LANES - width - 1), jnp.float32)
    students = jnp.concatenate([theta, jnp.ones((size, 1), jnp.float32), pad], 1)
    questions = jnp.concatenate([disc, intercept[:, None], pad], 1)
    (code,) = call(arrange_kernel, [(rows, rows)], codes, swap(codes))
    kept = jnp.where(core == 0, students, questions)
    given = jnp.where(core == 0, questions, students)
    mine = jnp.concatenate([kept, swap(given)], 0)
    for steps in stages(group):
        for step in steps:
            if step & (step - 1) == 0:
                mine = jnp.concatenate([mine, send(mine, step)], 0)
    other = swap(mine)

    def totals(value):
        parts = [value]
        for number, steps in enumerate(stages(group)):
            if number:
                parts = [functools.reduce(jnp.add, parts)]
            parts = parts + [send(parts[0], step) for step in steps]
        return parts

    sums, left, right, weight, icpt = call(
        functools.partial(gradient_kernel, group),
        [(rows + BIAS, LANES), (rows, LANES), (rows, LANES), (rows, rows), (BIAS, LANES)],
        mine,
        other,
        code,
    )
    parts = totals(sums)
    first, diag, root = call(
        functools.partial(start_kernel, group, len(parts)),
        [(half + BIAS + size, LANES), (half + BIAS, LANES), (rows, LANES)],
        *parts,
        left,
        icpt,
    )
    peer = swap(first)
    (sums,) = call(image_kernel, [(half + BIAS, LANES)], first, peer, left, right, weight)
    parts = totals(sums)
    second, dots = call(
        functools.partial(second_kernel, group, len(parts)),
        [(half + BIAS, LANES), (8, LANES)],
        *parts,
        first,
        diag,
    )
    peer_second = swap(second)
    devices = n_stu * n_que
    (dots,) = call(form_kernel, [(devices, 1, LANES)], second, peer_second, left, right, weight, dots)
    dots = lax.all_to_all(dots, AXES, 0, 0, tiled=True)
    abilities, discs, icpts = call(
        functools.partial(finish_kernel, group),
        [(size, width), (size, width), (8, LANES)],
        dots,
        first,
        peer,
        second,
        peer_second,
        root,
    )
    return abilities, discs, icpts[0, :size]


def solution(mesh):
    placed = (P("stu", "que"), P(("stu", "que"), None), P(("que", "stu"), None), P(("que", "stu")))
    return jax.shard_map(
        functools.partial(shards, mesh.shape["stu"], mesh.shape["que"]),
        mesh=mesh,
        in_specs=placed,
        out_specs=(P(("stu", "que"), None), P(("que", "stu"), None), P(("que", "stu"))),
        check_vma=False,
    )
```

```python
import functools

import jax
import jax.numpy as jnp
from jax import lax
from jax.experimental import pallas as pl
from jax.experimental.pallas import tpu as pltpu
from jax.sharding import PartitionSpec as P

HIGH = lax.Precision.HIGHEST
AXES = ("stu", "que")
LANES = 128
BIAS = 8


def dot_nt(left, right):
    return lax.dot_general(
        left, right, (((1,), (1,)), ((), ())), precision=HIGH, preferred_element_type=jnp.float32
    )


def dot_nn(left, right):
    return jnp.dot(left, right, precision=HIGH, preferred_element_type=jnp.float32)


def position():
    que = lax.axis_index("que")
    return lax.rem(que, 2), que // 2, lax.axis_index("stu")


def block_of(side, core, line, plane, group):
    return jnp.where(side == 0, line * 2 + core, core * group + plane)


def low_lanes(shape):
    return lax.broadcasted_iota(jnp.int32, shape, 1) < LANES // 2


def turn(value):
    return pltpu.roll(value, LANES // 2, 1)


def pack(value):
    half = value.shape[0] // 2
    low = low_lanes((half, LANES))
    return jnp.where(low, value[:half], turn(value[half:]))


def bias_rows(lanes, mine):
    return jnp.where(mine, jnp.concatenate([lanes[0:1, :LANES], lanes[0:1, LANES:]], 0), 0.0)


def column(rows):
    wide = jnp.concatenate([rows, jnp.zeros((LANES - 2, LANES), jnp.float32)], 0)
    tall = wide.T
    return jnp.concatenate([tall[:, 0:1], tall[:, 1:2]], 0)


def arrange_kernel(own_ref, peer_ref, out_ref):
    core, _, _ = position()
    cols = own_ref.shape[1]

    @pl.when(core == 0)
    def _():
        out_ref[:, :cols] = own_ref[...].astype(jnp.float32)
        out_ref[:, cols:] = peer_ref[...].astype(jnp.float32)

    @pl.when(core == 1)
    def _():
        out_ref[:cols, :] = peer_ref[...].astype(jnp.float32).T
        out_ref[cols:, :] = own_ref[...].astype(jnp.float32).T


def place(src_ref, dst_ref, side, core, line, plane, group):
    rows = src_ref.shape[0] // (2 * group)
    for k in range(group):
        for j in range(2):
            at = block_of(side, core ^ j, line ^ k, plane ^ k, group) * rows
            first = (k * 2 + j) * rows
            dst_ref[pl.ds(pl.multiple_of(at, rows), rows), :] = src_ref[first : first + rows, :]


def gradient_kernel(group, mine_ref, other_ref, code_ref, sums_ref, left_ref, right_ref, weight_ref, icpt_ref):
    core, line, plane = position()
    place(mine_ref, left_ref, core, core, line, plane, group)
    place(other_ref, right_ref, 1 - core, 1 - core, line, plane, group)
    left = left_ref[...]
    right = right_ref[...]
    prob = 1.0 / (1.0 + jnp.exp(-dot_nt(left, right)))
    code = code_ref[...]
    seen = code > 0.0
    resid = jnp.where(seen, prob - jnp.where(code == 2.0, 1.0, 0.0), 0.0)
    weight = jnp.where(seen, prob * (1.0 - prob), 0.0)
    weight_ref[...] = weight
    rows = left.shape[0]
    grad = dot_nn(resid, right)
    diag = dot_nn(weight, right * right)
    sums_ref[:rows, :] = jnp.where(low_lanes((rows, LANES)), grad, turn(diag))
    ones = jnp.ones((8, rows), jnp.float32)
    mine = core == 1
    sums_ref[rows:, :] = jnp.concatenate(
        [
            bias_rows(dot_nt(ones, resid), mine),
            bias_rows(dot_nt(ones, weight), mine),
            jnp.zeros((BIAS - 4, LANES), jnp.float32),
        ],
        0,
    )
    pick = (lax.broadcasted_iota(jnp.int32, (8, LANES), 1) == LANES // 2).astype(jnp.float32)
    icpt = bias_rows(dot_nt(pick, left), mine)
    icpt_ref[...] = jnp.concatenate([icpt, jnp.zeros((BIAS - 2, LANES), jnp.float32)], 0)


def start_kernel(group, parts, *refs):
    sum_refs, (left_ref, icpt_ref, send_ref, diag_ref, root_ref) = refs[:parts], refs[parts:]
    core, line, plane = position()
    total = sum_refs[0][...]
    for ref in sum_refs[1:]:
        total = total + ref[...]
    rows = left_ref.shape[0]
    half = rows // 2
    low = low_lanes((rows, LANES))
    main = total[:rows]
    diag = jnp.where(low, turn(main) + 1.0, 1.0)
    first = jnp.where(low, -(main + left_ref[...]) / diag, 0.0)
    grad_b = total[rows : rows + 2] + icpt_ref[:2]
    diag_b = total[rows + 2 : rows + 4] + 1.0
    first_b = -grad_b / diag_b
    root_ref[...] = jnp.sqrt(diag)
    send_ref[:half, :] = pack(first)
    send_ref[half : half + BIAS, :] = jnp.concatenate(
        [first_b, jnp.sqrt(diag_b), jnp.zeros((BIAS - 4, LANES), jnp.float32)], 0
    )
    diag_ref[:half, :] = pack(diag)
    diag_ref[half:, :] = jnp.concatenate([diag_b, jnp.ones((BIAS - 2, LANES), jnp.float32)], 0)
    size = rows // (2 * group)
    at = block_of(core, 1 - core, line, plane, group) * size
    send_ref[half + BIAS :, :] = root_ref[pl.ds(pl.multiple_of(at, size), size), :]


def change_of(mine_ref, other_ref, left, right, half):
    low = low_lanes((half, LANES))
    mine = mine_ref[:half, :]
    other = other_ref[:half, :]
    lhs = jnp.concatenate(
        [
            jnp.where(low, mine, turn(left[:half])),
            jnp.where(low, turn(mine), turn(left[half:])),
        ],
        0,
    )
    rhs = jnp.concatenate(
        [
            jnp.where(low, right[:half], turn(other)),
            jnp.where(low, right[half:], other),
        ],
        0,
    )
    lanes = jnp.concatenate([other_ref[half : half + 1, :], other_ref[half + 1 : half + 2, :]], 1)
    return dot_nt(lhs, rhs) + lanes + column(mine_ref[half : half + 2, :])


def image_kernel(mine_ref, other_ref, left_ref, right_ref, weight_ref, sums_ref):
    core, _, _ = position()
    rows = left_ref.shape[0]
    half = rows // 2
    right = right_ref[...]
    scaled = weight_ref[...] * change_of(mine_ref, other_ref, left_ref[...], right, half)
    sums_ref[:half, :] = pack(dot_nn(scaled, right))
    ones = jnp.ones((8, rows), jnp.float32)
    sums_ref[half:, :] = jnp.concatenate(
        [bias_rows(dot_nt(ones, scaled), core == 1), jnp.zeros((BIAS - 2, LANES), jnp.float32)], 0
    )


def second_kernel(group, parts, *refs):
    sum_refs, (send_ref, diag_ref, second_ref, dots_ref) = refs[:parts], refs[parts:]
    total = sum_refs[0][...]
    for ref in sum_refs[1:]:
        total = total + ref[...]
    half = total.shape[0] - BIAS
    row = lax.broadcasted_iota(jnp.int32, total.shape, 0)
    used = row < half + 2
    first = jnp.where(used, send_ref[: half + BIAS, :], 0.0)
    diag = diag_ref[...]
    lift = jnp.where(used, total + first - diag * first, 0.0)
    second = lift / diag
    second_ref[...] = second
    scale = 1.0 / group
    lane = lax.broadcasted_iota(jnp.int32, (8, LANES), 1)
    dots = jnp.zeros((8, LANES), jnp.float32)
    for at, value in enumerate((first * first * diag, first * lift, second * lift, second * second)):
        dots = jnp.where(lane == at, jnp.sum(value) * scale, dots)
    dots_ref[...] = dots


def form_kernel(mine_ref, other_ref, left_ref, right_ref, weight_ref, dots_ref, out_ref):
    half = left_ref.shape[0] // 2
    change = change_of(mine_ref, other_ref, left_ref[...], right_ref[...], half)
    form = 0.5 * jnp.sum(weight_ref[...] * change * change)
    lane = lax.broadcasted_iota(jnp.int32, (1, LANES), 1)
    value = dots_ref[0:1, :] + jnp.where(lane == 3, form, 0.0)
    out_ref[...] = jnp.broadcast_to(value[None], out_ref.shape)


def finish_kernel(
    group, dots_ref, send_ref, peer_ref, second_ref, peer_second_ref, root_ref, theta_ref, disc_ref, icpt_ref
):
    core, line, plane = position()
    dots = jnp.sum(dots_ref[...], axis=0)
    lane = lax.broadcasted_iota(jnp.int32, (1, LANES), 1)
    a, f, h, d = [jnp.sum(jnp.where(lane == at, dots, 0.0), axis=1, keepdims=True) for at in range(4)]
    b = a + f
    e = f + h
    det = b * d - e * e
    s = (a * d - e * f) / det
    t = (f * f - a * h) / det
    rows = root_ref.shape[0]
    half = rows // 2
    size = rows // (2 * group)

    def direction(first_ref, next_ref, at):
        upper = at // group
        rows_at = pl.ds(pl.multiple_of(lax.rem(at, group) * size, size), size)
        value = s * first_ref[rows_at, :] + t * next_ref[rows_at, :]
        return jnp.where(upper == 1, turn(value), value)

    mine_at = block_of(core, core, line, plane, group)
    other_at = block_of(1 - core, core, line, plane, group)
    mine = direction(send_ref, second_ref, mine_at)
    mine = mine * root_ref[pl.ds(pl.multiple_of(mine_at * size, size), size), :]
    other = direction(peer_ref, peer_second_ref, other_at) * peer_ref[half + BIAS :, :]
    theta_ref[...] = jnp.where(core == 0, mine, other)[:, : LANES // 2]
    disc_ref[...] = jnp.where(core == 0, other, mine)[:, : LANES // 2]
    ask = jnp.where(core == 0, peer_ref[half : half + BIAS, :], send_ref[half : half + BIAS, :])
    ask_next = jnp.where(core == 0, peer_second_ref[half : half + 2, :], second_ref[half : half + 2, :])
    bias = (s * ask[0:2] + t * ask_next) * ask[2:4]
    disc_at = jnp.where(core == 0, other_at, mine_at)
    row = jnp.where(disc_at // group == 1, bias[1:2], bias[0:1])
    back = lax.rem(LANES - lax.rem(disc_at, group) * size, LANES)
    icpt_ref[...] = jnp.broadcast_to(pltpu.roll(row, back, 1), icpt_ref.shape)


def call(kernel, shapes, *args):
    out = [jax.ShapeDtypeStruct(shape, jnp.float32) for shape in shapes]
    return pl.pallas_call(
        kernel,
        out_shape=out,
        in_specs=[pl.BlockSpec(memory_space=pltpu.VMEM)] * len(args),
        out_specs=[pl.BlockSpec(memory_space=pltpu.VMEM)] * len(out),
        compiler_params=pltpu.CompilerParams(vmem_limit_bytes=32 * 2**20),
    )(*args)


def swap_cores(value, n_stu, n_que):
    return lax.ppermute(value, AXES, [(i, i ^ 1) for i in range(n_stu * n_que)])


def send_over(value, step, n_stu, n_que):
    pairs = []
    for stu in range(n_stu):
        for que in range(n_que):
            there = (stu, que ^ (2 * step)) if que % 2 == 0 else (stu ^ step, que)
            pairs.append((stu * n_que + que, there[0] * n_que + there[1]))
    return lax.ppermute(value, AXES, pairs)


def stages(group):
    base = 1
    while base < group:
        width = min(4, group // base)
        yield [base * k for k in range(1, width)]
        base *= width


def shards(n_stu, n_que, codes, theta, disc, intercept):
    group = n_stu
    assert n_que == 2 * group
    send = functools.partial(send_over, n_stu=n_stu, n_que=n_que)
    swap = functools.partial(swap_cores, n_stu=n_stu, n_que=n_que)
    size, width = theta.shape
    rows = 2 * group * size
    half = rows // 2
    assert width == LANES // 2 and rows == 2 * LANES
    assert disc.shape == theta.shape and codes.shape == (rows, half)
    core = lax.rem(lax.axis_index("que"), 2)
    pad = jnp.zeros((size, LANES - width - 1), jnp.float32)
    students = jnp.concatenate([theta, jnp.ones((size, 1), jnp.float32), pad], 1)
    questions = jnp.concatenate([disc, intercept[:, None], pad], 1)
    (code,) = call(arrange_kernel, [(rows, rows)], codes, swap(codes))
    kept = jnp.where(core == 0, students, questions)
    given = jnp.where(core == 0, questions, students)
    mine = jnp.concatenate([kept, swap(given)], 0)
    for steps in stages(group):
        mine = jnp.concatenate([mine] + [send(mine, step) for step in steps], 0)
    other = swap(mine)

    def totals(value):
        parts = [value]
        for number, steps in enumerate(stages(group)):
            if number:
                parts = [functools.reduce(jnp.add, parts)]
            parts = parts + [send(parts[0], step) for step in steps]
        return parts

    sums, left, right, weight, icpt = call(
        functools.partial(gradient_kernel, group),
        [(rows + BIAS, LANES), (rows, LANES), (rows, LANES), (rows, rows), (BIAS, LANES)],
        mine,
        other,
        code,
    )
    parts = totals(sums)
    first, diag, root = call(
        functools.partial(start_kernel, group, len(parts)),
        [(half + BIAS + size, LANES), (half + BIAS, LANES), (rows, LANES)],
        *parts,
        left,
        icpt,
    )
    peer = swap(first)
    (sums,) = call(image_kernel, [(half + BIAS, LANES)], first, peer, left, right, weight)
    parts = totals(sums)
    second, dots = call(
        functools.partial(second_kernel, group, len(parts)),
        [(half + BIAS, LANES), (8, LANES)],
        *parts,
        first,
        diag,
    )
    peer_second = swap(second)
    devices = n_stu * n_que
    (dots,) = call(form_kernel, [(devices, 1, LANES)], second, peer_second, left, right, weight, dots)
    dots = lax.all_to_all(dots, AXES, 0, 0, tiled=True)
    abilities, discs, icpts = call(
        functools.partial(finish_kernel, group),
        [(size, width), (size, width), (8, LANES)],
        dots,
        first,
        peer,
        second,
        peer_second,
        root,
    )
    return abilities, discs, icpts[0, :size]


def solution(mesh):
    placed = (P("stu", "que"), P(("stu", "que"), None), P(("que", "stu"), None), P(("que", "stu")))
    return jax.shard_map(
        functools.partial(shards, mesh.shape["stu"], mesh.shape["que"]),
        mesh=mesh,
        in_specs=placed,
        out_specs=(P(("stu", "que"), None), P(("que", "stu"), None), P(("que", "stu"))),
        check_vma=False,
    )
```

```python
import functools

import jax
import jax.numpy as jnp
from jax import lax
from jax.experimental import pallas as pl
from jax.experimental.pallas import tpu as pltpu
from jax.sharding import PartitionSpec as P

AXES = ("stu", "que")
LANES = 128
BIAS = 8


def halves(value):
    high = value.astype(jnp.bfloat16)
    return high, (value - high.astype(jnp.float32)).astype(jnp.bfloat16)


def product(left, right, dims):
    return lax.dot_general(left, right, (dims, ((), ())), preferred_element_type=jnp.float32)


def dot_nt(left, right):
    left_high, left_low = halves(left)
    right_high, right_low = halves(right)
    dims = ((1,), (1,))
    both = product(
        jnp.concatenate([left_high, left_low], 1), jnp.concatenate([right_high, right_high], 1), dims
    )
    return both + product(left_high, right_low, dims)


def dot_nn(left, right):
    left_high, left_low = halves(left)
    right_high, right_low = halves(right)
    dims = ((1,), (0,))
    both = product(left_high, jnp.concatenate([right_high, right_low], 1), dims)
    width = right.shape[1]
    return both[:, :width] + both[:, width:] + product(left_low, right_high, dims)


def position():
    que = lax.axis_index("que")
    return lax.rem(que, 2), que // 2, lax.axis_index("stu")


def block_of(side, core, line, plane, group):
    return jnp.where(side == 0, line * 2 + core, core * group + plane)


def low_lanes(shape):
    return lax.broadcasted_iota(jnp.int32, shape, 1) < LANES // 2


def turn(value):
    return pltpu.roll(value, LANES // 2, 1)


def pack(value):
    half = value.shape[0] // 2
    low = low_lanes((half, LANES))
    return jnp.where(low, value[:half], turn(value[half:]))


def bias_rows(lanes, mine):
    return jnp.where(mine, jnp.concatenate([lanes[:, :LANES], lanes[:, LANES:]], 0), 0.0)


def column(rows):
    wide = jnp.concatenate([rows, jnp.zeros((LANES - 2, LANES), jnp.float32)], 0)
    tall = wide.T
    return jnp.concatenate([tall[:, 0:1], tall[:, 1:2]], 0)


def block_kernel(theta_ref, disc_ref, icpt_ref, peer_theta_ref, peer_disc_ref, peer_icpt_ref, out_ref):
    core, _, _ = position()
    size, width = theta_ref.shape

    def fill(students_ref, questions_ref, intercept_ref, first):
        rows = slice(first, first + size)

        @pl.when(core == 0)
        def _():
            out_ref[rows, :width] = students_ref[...]
            lane = lax.broadcasted_iota(jnp.int32, (size, LANES - width), 1)
            out_ref[rows, width:] = jnp.where(lane == 0, 1.0, 0.0)

        @pl.when(core == 1)
        def _():
            out_ref[rows, :width] = questions_ref[...]
            row = jnp.concatenate([intercept_ref[...], jnp.zeros((1, LANES - size), jnp.float32)], 1)
            tall = jnp.concatenate([row, jnp.zeros((LANES - 1, LANES), jnp.float32)], 0).T
            out_ref[rows, width:] = tall[:size, : LANES - width]

    fill(theta_ref, disc_ref, icpt_ref, 0)
    fill(peer_theta_ref, peer_disc_ref, peer_icpt_ref, size)


def arrange_kernel(own_ref, peer_ref, out_ref):
    core, _, _ = position()
    cols = own_ref.shape[1]

    @pl.when(core == 0)
    def _():
        out_ref[:, :cols] = own_ref[...].astype(jnp.float32)
        out_ref[:, cols:] = peer_ref[...].astype(jnp.float32)

    @pl.when(core == 1)
    def _():
        out_ref[:cols, :] = peer_ref[...].astype(jnp.float32).T
        out_ref[cols:, :] = own_ref[...].astype(jnp.float32).T


def place(refs, dst_ref, side, core, line, plane, group):
    size = dst_ref.shape[0] // (2 * group)
    k = 0
    for ref in refs:
        for first in range(0, ref.shape[0], 2 * size):
            for j in range(2):
                at = block_of(side, core ^ j, line ^ k, plane ^ k, group) * size
                rows = slice(first + j * size, first + (j + 1) * size)
                dst_ref[pl.ds(pl.multiple_of(at, size), size), :] = ref[rows, :]
            k += 1


def gradient_kernel(group, parts, *refs):
    mine_refs, other_refs = refs[:parts], refs[parts : 2 * parts]
    code_ref, sums_ref, left_ref, right_ref, weight_ref, icpt_ref = refs[2 * parts :]
    core, line, plane = position()
    place(mine_refs, left_ref, core, core, line, plane, group)
    place(other_refs, right_ref, 1 - core, 1 - core, line, plane, group)
    left = left_ref[...]
    right = right_ref[...]
    prob = 1.0 / (1.0 + jnp.exp(-dot_nt(left, right)))
    code = code_ref[...]
    seen = code > 0.0
    resid = jnp.where(seen, prob - jnp.where(code == 2.0, 1.0, 0.0), 0.0)
    weight = jnp.where(seen, prob * (1.0 - prob), 0.0)
    weight_ref[...] = weight
    rows = left.shape[0]
    grad = dot_nn(resid, right)
    diag = dot_nn(weight, right * right)
    sums_ref[:rows, :] = jnp.where(low_lanes((rows, LANES)), grad, turn(diag))
    lane = lax.broadcasted_iota(jnp.int32, (rows, LANES), 1)
    at = LANES // 2
    extra = jnp.where(lane == at, grad, jnp.where(lane == at + 1, pltpu.roll(diag, 1, 1), pltpu.roll(left, 2, 1)))
    lanes = extra.T
    mine = core == 1
    sums_ref[rows:, :] = jnp.concatenate(
        [
            bias_rows(lanes[at : at + 1], mine),
            bias_rows(lanes[at + 1 : at + 2], mine),
            jnp.zeros((BIAS - 4, LANES), jnp.float32),
        ],
        0,
    )
    icpt = bias_rows(lanes[at + 2 : at + 3], mine)
    icpt_ref[...] = jnp.concatenate([icpt, jnp.zeros((BIAS - 2, LANES), jnp.float32)], 0)


def start_kernel(group, parts, *refs):
    sum_refs, (left_ref, icpt_ref, send_ref, diag_ref, root_ref) = refs[:parts], refs[parts:]
    core, line, plane = position()
    total = sum_refs[0][...]
    for ref in sum_refs[1:]:
        total = total + ref[...]
    rows = left_ref.shape[0]
    half = rows // 2
    low = low_lanes((rows, LANES))
    main = total[:rows]
    diag = jnp.where(low, turn(main) + 1.0, 1.0)
    first = jnp.where(low, -(main + left_ref[...]) / diag, 0.0)
    grad_b = total[rows : rows + 2] + icpt_ref[:2]
    diag_b = total[rows + 2 : rows + 4] + 1.0
    first_b = -grad_b / diag_b
    root_ref[...] = jnp.sqrt(diag)
    send_ref[:half, :] = pack(first)
    send_ref[half : half + BIAS, :] = jnp.concatenate(
        [first_b, jnp.sqrt(diag_b), jnp.zeros((BIAS - 4, LANES), jnp.float32)], 0
    )
    diag_ref[:half, :] = pack(diag)
    diag_ref[half:, :] = jnp.concatenate([diag_b, jnp.ones((BIAS - 2, LANES), jnp.float32)], 0)
    size = rows // (2 * group)
    at = block_of(core, 1 - core, line, plane, group) * size
    send_ref[half + BIAS :, :] = root_ref[pl.ds(pl.multiple_of(at, size), size), :]


def change_of(mine_ref, other_ref, left, right, half):
    low = low_lanes((half, LANES))
    mine = mine_ref[:half, :]
    other = other_ref[:half, :]
    lhs = jnp.concatenate(
        [
            jnp.where(low, mine, turn(left[:half])),
            jnp.where(low, turn(mine), turn(left[half:])),
        ],
        0,
    )
    rhs = jnp.concatenate(
        [
            jnp.where(low, right[:half], turn(other)),
            jnp.where(low, right[half:], other),
        ],
        0,
    )
    lanes = jnp.concatenate([other_ref[half : half + 1, :], other_ref[half + 1 : half + 2, :]], 1)
    return dot_nt(lhs, rhs) + lanes + column(mine_ref[half : half + 2, :])


def image_kernel(mine_ref, other_ref, left_ref, right_ref, weight_ref, sums_ref):
    core, _, _ = position()
    rows = left_ref.shape[0]
    half = rows // 2
    right = right_ref[...]
    scaled = weight_ref[...] * change_of(mine_ref, other_ref, left_ref[...], right, half)
    sums = dot_nn(scaled, right)
    sums_ref[:half, :] = pack(sums)
    at = LANES // 2
    bias = bias_rows(sums.T[at : at + 1], core == 1)
    sums_ref[half:, :] = jnp.concatenate([bias, jnp.zeros((BIAS - 2, LANES), jnp.float32)], 0)


def second_kernel(group, parts, *refs):
    sum_refs, (send_ref, diag_ref, second_ref, dots_ref) = refs[:parts], refs[parts:]
    total = sum_refs[0][...]
    for ref in sum_refs[1:]:
        total = total + ref[...]
    half = total.shape[0] - BIAS
    row = lax.broadcasted_iota(jnp.int32, total.shape, 0)
    used = row < half + 2
    first = jnp.where(used, send_ref[: half + BIAS, :], 0.0)
    diag = diag_ref[...]
    lift = jnp.where(used, total + first - diag * first, 0.0)
    second = lift / diag
    second_ref[...] = second
    scale = 1.0 / group
    lane = lax.broadcasted_iota(jnp.int32, (8, LANES), 1)
    dots = jnp.zeros((8, LANES), jnp.float32)
    for at, value in enumerate((first * first * diag, first * lift, second * lift, second * second)):
        dots = jnp.where(lane == at, jnp.sum(value) * scale, dots)
    dots_ref[...] = dots


def form_kernel(mine_ref, other_ref, left_ref, right_ref, weight_ref, dots_ref, out_ref):
    half = left_ref.shape[0] // 2
    change = change_of(mine_ref, other_ref, left_ref[...], right_ref[...], half)
    form = 0.5 * jnp.sum(weight_ref[...] * change * change)
    lane = lax.broadcasted_iota(jnp.int32, (1, LANES), 1)
    value = dots_ref[0:1, :] + jnp.where(lane == 3, form, 0.0)
    out_ref[...] = jnp.broadcast_to(value[None], out_ref.shape)


def finish_kernel(
    group, dots_ref, send_ref, peer_ref, second_ref, peer_second_ref, root_ref, theta_ref, disc_ref, icpt_ref
):
    core, line, plane = position()
    dots = jnp.sum(dots_ref[...], axis=0)
    lane = lax.broadcasted_iota(jnp.int32, (1, LANES), 1)
    a, f, h, d = [jnp.sum(jnp.where(lane == at, dots, 0.0), axis=1, keepdims=True) for at in range(4)]
    b = a + f
    e = f + h
    det = b * d - e * e
    s = (a * d - e * f) / det
    t = (f * f - a * h) / det
    rows = root_ref.shape[0]
    half = rows // 2
    size = rows // (2 * group)

    def direction(first_ref, next_ref, at):
        upper = at // group
        rows_at = pl.ds(pl.multiple_of(lax.rem(at, group) * size, size), size)
        value = s * first_ref[rows_at, :] + t * next_ref[rows_at, :]
        return jnp.where(upper == 1, turn(value), value)

    mine_at = block_of(core, core, line, plane, group)
    other_at = block_of(1 - core, core, line, plane, group)
    mine = direction(send_ref, second_ref, mine_at)
    mine = mine * root_ref[pl.ds(pl.multiple_of(mine_at * size, size), size), :]
    other = direction(peer_ref, peer_second_ref, other_at) * peer_ref[half + BIAS :, :]
    theta_ref[...] = jnp.where(core == 0, mine, other)[:, : LANES // 2]
    disc_ref[...] = jnp.where(core == 0, other, mine)[:, : LANES // 2]
    ask = jnp.where(core == 0, peer_ref[half : half + BIAS, :], send_ref[half : half + BIAS, :])
    ask_next = jnp.where(core == 0, peer_second_ref[half : half + 2, :], second_ref[half : half + 2, :])
    bias = (s * ask[0:2] + t * ask_next) * ask[2:4]
    disc_at = jnp.where(core == 0, other_at, mine_at)
    row = jnp.where(disc_at // group == 1, bias[1:2], bias[0:1])
    back = lax.rem(LANES - lax.rem(disc_at, group) * size, LANES)
    icpt_ref[...] = pltpu.roll(row, back, 1)[:, :size]


def call(kernel, shapes, *args):
    out = [jax.ShapeDtypeStruct(shape, jnp.float32) for shape in shapes]
    return pl.pallas_call(
        kernel,
        out_shape=out,
        in_specs=[pl.BlockSpec(memory_space=pltpu.VMEM)] * len(args),
        out_specs=[pl.BlockSpec(memory_space=pltpu.VMEM)] * len(out),
        compiler_params=pltpu.CompilerParams(vmem_limit_bytes=32 * 2**20),
    )(*args)


def swap_cores(value, n_stu, n_que):
    return lax.ppermute(value, AXES, [(i, i ^ 1) for i in range(n_stu * n_que)])


def send_over(value, step, n_stu, n_que):
    pairs = []
    for stu in range(n_stu):
        for que in range(n_que):
            there = (stu, que ^ (2 * step)) if que % 2 == 0 else (stu ^ step, que)
            pairs.append((stu * n_que + que, there[0] * n_que + there[1]))
    return lax.ppermute(value, AXES, pairs)


def stages(group):
    base = 1
    while base < group:
        width = min(4, group // base)
        yield [base * k for k in range(1, width)]
        base *= width


def shards(n_stu, n_que, codes, theta, disc, intercept):
    group = n_stu
    assert n_que == 2 * group
    send = functools.partial(send_over, n_stu=n_stu, n_que=n_que)
    swap = functools.partial(swap_cores, n_stu=n_stu, n_que=n_que)
    size, width = theta.shape
    rows = 2 * group * size
    half = rows // 2
    assert width == LANES // 2 and rows == 2 * LANES
    assert disc.shape == theta.shape and codes.shape == (rows, half)
    icpt = intercept[None, :]
    (mine,) = call(
        block_kernel, [(2 * size, LANES)], theta, disc, icpt, swap(theta), swap(disc), swap(icpt)
    )
    (code,) = call(arrange_kernel, [(rows, rows)], codes, swap(codes))
    mine = [mine]
    for steps in stages(group):
        joined = jnp.concatenate(mine, 0)
        mine = mine + [send(joined, step) for step in steps]
    other = [swap(piece) for piece in mine]

    def totals(value):
        parts = [value]
        for number, steps in enumerate(stages(group)):
            if number:
                parts = [functools.reduce(jnp.add, parts)]
            parts = parts + [send(parts[0], step) for step in steps]
        return parts

    sums, left, right, weight, icpt = call(
        functools.partial(gradient_kernel, group, len(mine)),
        [(rows + BIAS, LANES), (rows, LANES), (rows, LANES), (rows, rows), (BIAS, LANES)],
        *mine,
        *other,
        code,
    )
    parts = totals(sums)
    first, diag, root = call(
        functools.partial(start_kernel, group, len(parts)),
        [(half + BIAS + size, LANES), (half + BIAS, LANES), (rows, LANES)],
        *parts,
        left,
        icpt,
    )
    peer = swap(first)
    (sums,) = call(image_kernel, [(half + BIAS, LANES)], first, peer, left, right, weight)
    parts = totals(sums)
    second, dots = call(
        functools.partial(second_kernel, group, len(parts)),
        [(half + BIAS, LANES), (8, LANES)],
        *parts,
        first,
        diag,
    )
    peer_second = swap(second)
    devices = n_stu * n_que
    (dots,) = call(form_kernel, [(devices, 1, LANES)], second, peer_second, left, right, weight, dots)
    dots = lax.all_to_all(dots, AXES, 0, 0, tiled=True)
    abilities, discs, icpts = call(
        functools.partial(finish_kernel, group),
        [(size, width), (size, width), (1, size)],
        dots,
        first,
        peer,
        second,
        peer_second,
        root,
    )
    return abilities, discs, icpts[0]


def solution(mesh):
    placed = (P("stu", "que"), P(("stu", "que"), None), P(("que", "stu"), None), P(("que", "stu")))
    return jax.shard_map(
        functools.partial(shards, mesh.shape["stu"], mesh.shape["que"]),
        mesh=mesh,
        in_specs=placed,
        out_specs=(P(("stu", "que"), None), P(("que", "stu"), None), P(("que", "stu"))),
        check_vma=False,
    )
```

```python
import functools

import jax
import jax.numpy as jnp
from jax import lax
from jax.experimental import pallas as pl
from jax.experimental.pallas import tpu as pltpu
from jax.sharding import PartitionSpec as P

AXES = ("stu", "que")
LANES = 128
BIAS = 8


def halves(value):
    high = value.astype(jnp.bfloat16)
    return high, (value - high.astype(jnp.float32)).astype(jnp.bfloat16)


def product(left, right, dims):
    return lax.dot_general(left, right, (dims, ((), ())), preferred_element_type=jnp.float32)


def dot_nt(left, right):
    left_high, left_low = halves(left)
    right_high, right_low = halves(right)
    dims = ((1,), (1,))
    both = product(
        jnp.concatenate([left_high, left_low], 1), jnp.concatenate([right_high, right_high], 1), dims
    )
    return both + product(left_high, right_low, dims)


def dot_nn(left, right):
    left_high, left_low = halves(left)
    right_high, right_low = halves(right)
    dims = ((1,), (0,))
    both = product(left_high, jnp.concatenate([right_high, right_low], 1), dims)
    width = right.shape[1]
    return both[:, :width] + both[:, width:] + product(left_low, right_high, dims)


def position():
    que = lax.axis_index("que")
    return lax.rem(que, 2), que // 2, lax.axis_index("stu")


def block_of(side, core, line, plane, group):
    return jnp.where(side == 0, line * 2 + core, core * group + plane)


def low_lanes(shape):
    return lax.broadcasted_iota(jnp.int32, shape, 1) < LANES // 2


def turn(value):
    return pltpu.roll(value, LANES // 2, 1)


def pack(value):
    half = value.shape[0] // 2
    low = low_lanes((half, LANES))
    return jnp.where(low, value[:half], turn(value[half:]))


def bias_rows(lanes, mine):
    return jnp.where(mine, jnp.concatenate([lanes[:, :LANES], lanes[:, LANES:]], 0), 0.0)


def column(rows):
    wide = jnp.concatenate([rows, jnp.zeros((LANES - 2, LANES), jnp.float32)], 0)
    tall = wide.T
    return jnp.concatenate([tall[:, 0:1], tall[:, 1:2]], 0)


def arrange_kernel(own_ref, peer_ref, out_ref):
    core, _, _ = position()
    cols = own_ref.shape[1]

    @pl.when(core == 0)
    def _():
        out_ref[:, :cols] = own_ref[...].astype(jnp.float32)
        out_ref[:, cols:] = peer_ref[...].astype(jnp.float32)

    @pl.when(core == 1)
    def _():
        out_ref[:cols, :] = peer_ref[...].astype(jnp.float32).T
        out_ref[cols:, :] = own_ref[...].astype(jnp.float32).T


def pieces(refs, size):
    step = size + BIAS
    return [ref[first : first + step, :] for ref in refs for first in range(0, ref.shape[0], step)]


def place(blocks, dst_ref, side, columns, core, line, plane, group):
    size = dst_ref.shape[0] // (2 * group)
    lane = lax.broadcasted_iota(jnp.int32, (size, LANES), 1)
    half = LANES // 2
    for k, block in enumerate(blocks):
        for j in range(2):
            value = turn(block[:size]) if j else block[:size]
            last = jnp.where(side == 0, 1.0, columns[j * half : j * half + size, k : k + 1])
            at = block_of(side, core ^ j, line ^ k, plane ^ k, group) * size
            dst_ref[pl.ds(pl.multiple_of(at, size), size), :] = jnp.where(
                lane < half, value, jnp.where(lane == half, last, 0.0)
            )


def gradient_kernel(group, parts, *refs):
    code_ref, sums_ref, left_ref, right_ref, weight_ref, icpt_ref = refs[2 * parts :]
    core, line, plane = position()
    size = left_ref.shape[0] // (2 * group)
    mine = pieces(refs[:parts], size)
    other = pieces(refs[parts : 2 * parts], size)
    rows = [jnp.where(core == 0, there[size : size + 1], here[size : size + 1]) for here, there in zip(mine, other)]
    columns = jnp.concatenate(rows + [jnp.zeros((LANES - group, LANES), jnp.float32)], 0).T
    place(mine, left_ref, core, columns, core, line, plane, group)
    place(other, right_ref, 1 - core, columns, 1 - core, line, plane, group)
    left = left_ref[...]
    right = right_ref[...]
    prob = 1.0 / (1.0 + jnp.exp(-dot_nt(left, right)))
    code = code_ref[...]
    seen = code > 0.0
    resid = jnp.where(seen, prob - jnp.where(code == 2.0, 1.0, 0.0), 0.0)
    weight = jnp.where(seen, prob * (1.0 - prob), 0.0)
    weight_ref[...] = weight
    rows = left.shape[0]
    grad = dot_nn(resid, right)
    diag = dot_nn(weight, right * right)
    sums_ref[:rows, :] = jnp.where(low_lanes((rows, LANES)), grad, turn(diag))
    lane = lax.broadcasted_iota(jnp.int32, (rows, LANES), 1)
    at = LANES // 2
    extra = jnp.where(lane == at, grad, jnp.where(lane == at + 1, pltpu.roll(diag, 1, 1), pltpu.roll(left, 2, 1)))
    lanes = extra.T
    mine = core == 1
    sums_ref[rows:, :] = jnp.concatenate(
        [
            bias_rows(lanes[at : at + 1], mine),
            bias_rows(lanes[at + 1 : at + 2], mine),
            jnp.zeros((BIAS - 4, LANES), jnp.float32),
        ],
        0,
    )
    icpt = bias_rows(lanes[at + 2 : at + 3], mine)
    icpt_ref[...] = jnp.concatenate([icpt, jnp.zeros((BIAS - 2, LANES), jnp.float32)], 0)


def start_kernel(group, parts, *refs):
    sum_refs, (left_ref, icpt_ref, send_ref, diag_ref, root_ref) = refs[:parts], refs[parts:]
    core, line, plane = position()
    total = sum_refs[0][...]
    for ref in sum_refs[1:]:
        total = total + ref[...]
    rows = left_ref.shape[0]
    half = rows // 2
    low = low_lanes((rows, LANES))
    main = total[:rows]
    diag = jnp.where(low, turn(main) + 1.0, 1.0)
    first = jnp.where(low, -(main + left_ref[...]) / diag, 0.0)
    grad_b = total[rows : rows + 2] + icpt_ref[:2]
    diag_b = total[rows + 2 : rows + 4] + 1.0
    first_b = -grad_b / diag_b
    root_ref[...] = jnp.sqrt(diag)
    send_ref[:half, :] = pack(first)
    send_ref[half : half + BIAS, :] = jnp.concatenate(
        [first_b, jnp.sqrt(diag_b), jnp.zeros((BIAS - 4, LANES), jnp.float32)], 0
    )
    diag_ref[:half, :] = pack(diag)
    diag_ref[half:, :] = jnp.concatenate([diag_b, jnp.ones((BIAS - 2, LANES), jnp.float32)], 0)
    size = rows // (2 * group)
    at = block_of(core, 1 - core, line, plane, group) * size
    send_ref[half + BIAS :, :] = root_ref[pl.ds(pl.multiple_of(at, size), size), :]


def change_of(mine_ref, other_ref, left, right, half):
    low = low_lanes((half, LANES))
    mine = mine_ref[:half, :]
    other = other_ref[:half, :]
    lhs = jnp.concatenate(
        [
            jnp.where(low, mine, turn(left[:half])),
            jnp.where(low, turn(mine), turn(left[half:])),
        ],
        0,
    )
    rhs = jnp.concatenate(
        [
            jnp.where(low, right[:half], turn(other)),
            jnp.where(low, right[half:], other),
        ],
        0,
    )
    lanes = jnp.concatenate([other_ref[half : half + 1, :], other_ref[half + 1 : half + 2, :]], 1)
    return dot_nt(lhs, rhs) + lanes + column(mine_ref[half : half + 2, :])


def image_kernel(mine_ref, other_ref, left_ref, right_ref, weight_ref, sums_ref):
    core, _, _ = position()
    rows = left_ref.shape[0]
    half = rows // 2
    right = right_ref[...]
    scaled = weight_ref[...] * change_of(mine_ref, other_ref, left_ref[...], right, half)
    sums = dot_nn(scaled, right)
    sums_ref[:half, :] = pack(sums)
    at = LANES // 2
    bias = bias_rows(sums.T[at : at + 1], core == 1)
    sums_ref[half:, :] = jnp.concatenate([bias, jnp.zeros((BIAS - 2, LANES), jnp.float32)], 0)


def second_kernel(group, parts, *refs):
    sum_refs, (send_ref, diag_ref, second_ref, dots_ref) = refs[:parts], refs[parts:]
    total = sum_refs[0][...]
    for ref in sum_refs[1:]:
        total = total + ref[...]
    half = total.shape[0] - BIAS
    row = lax.broadcasted_iota(jnp.int32, total.shape, 0)
    used = row < half + 2
    first = jnp.where(used, send_ref[: half + BIAS, :], 0.0)
    diag = diag_ref[...]
    lift = jnp.where(used, total + first - diag * first, 0.0)
    second = lift / diag
    second_ref[...] = second
    scale = 1.0 / group
    lane = lax.broadcasted_iota(jnp.int32, (8, LANES), 1)
    dots = jnp.zeros((8, LANES), jnp.float32)
    for at, value in enumerate((first * first * diag, first * lift, second * lift, second * second)):
        dots = jnp.where(lane == at, jnp.sum(value) * scale, dots)
    dots_ref[...] = dots


def form_kernel(mine_ref, other_ref, left_ref, right_ref, weight_ref, dots_ref, out_ref):
    half = left_ref.shape[0] // 2
    change = change_of(mine_ref, other_ref, left_ref[...], right_ref[...], half)
    form = 0.5 * jnp.sum(weight_ref[...] * change * change)
    lane = lax.broadcasted_iota(jnp.int32, (1, LANES), 1)
    value = dots_ref[0:1, :] + jnp.where(lane == 3, form, 0.0)
    out_ref[...] = jnp.broadcast_to(value[None], out_ref.shape)


def finish_kernel(
    group, dots_ref, send_ref, peer_ref, second_ref, peer_second_ref, root_ref, theta_ref, disc_ref, icpt_ref
):
    core, line, plane = position()
    dots = jnp.sum(dots_ref[...], axis=0)
    lane = lax.broadcasted_iota(jnp.int32, (1, LANES), 1)
    a, f, h, d = [jnp.sum(jnp.where(lane == at, dots, 0.0), axis=1, keepdims=True) for at in range(4)]
    b = a + f
    e = f + h
    det = b * d - e * e
    s = (a * d - e * f) / det
    t = (f * f - a * h) / det
    rows = root_ref.shape[0]
    half = rows // 2
    size = rows // (2 * group)

    def direction(first_ref, next_ref, at):
        upper = at // group
        rows_at = pl.ds(pl.multiple_of(lax.rem(at, group) * size, size), size)
        value = s * first_ref[rows_at, :] + t * next_ref[rows_at, :]
        return jnp.where(upper == 1, turn(value), value)

    mine_at = block_of(core, core, line, plane, group)
    other_at = block_of(1 - core, core, line, plane, group)
    mine = direction(send_ref, second_ref, mine_at)
    mine = mine * root_ref[pl.ds(pl.multiple_of(mine_at * size, size), size), :]
    other = direction(peer_ref, peer_second_ref, other_at) * peer_ref[half + BIAS :, :]
    theta_ref[...] = jnp.where(core == 0, mine, other)[:, : LANES // 2]
    disc_ref[...] = jnp.where(core == 0, other, mine)[:, : LANES // 2]
    ask = jnp.where(core == 0, peer_ref[half : half + BIAS, :], send_ref[half : half + BIAS, :])
    ask_next = jnp.where(core == 0, peer_second_ref[half : half + 2, :], second_ref[half : half + 2, :])
    bias = (s * ask[0:2] + t * ask_next) * ask[2:4]
    disc_at = jnp.where(core == 0, other_at, mine_at)
    row = jnp.where(disc_at // group == 1, bias[1:2], bias[0:1])
    back = lax.rem(LANES - lax.rem(disc_at, group) * size, LANES)
    icpt_ref[...] = pltpu.roll(row, back, 1)[:, :size]


def call(kernel, shapes, *args):
    out = [jax.ShapeDtypeStruct(shape, jnp.float32) for shape in shapes]
    return pl.pallas_call(
        kernel,
        out_shape=out,
        in_specs=[pl.BlockSpec(memory_space=pltpu.VMEM)] * len(args),
        out_specs=[pl.BlockSpec(memory_space=pltpu.VMEM)] * len(out),
        compiler_params=pltpu.CompilerParams(vmem_limit_bytes=32 * 2**20),
    )(*args)


def swap_cores(value, n_stu, n_que):
    return lax.ppermute(value, AXES, [(i, i ^ 1) for i in range(n_stu * n_que)])


def send_over(value, step, n_stu, n_que):
    pairs = []
    for stu in range(n_stu):
        for que in range(n_que):
            there = (stu, que ^ (2 * step)) if que % 2 == 0 else (stu ^ step, que)
            pairs.append((stu * n_que + que, there[0] * n_que + there[1]))
    return lax.ppermute(value, AXES, pairs)


def stages(group):
    base = 1
    while base < group:
        width = min(4, group // base)
        yield [base * k for k in range(1, width)]
        base *= width


def shards(n_stu, n_que, codes, theta, disc, intercept):
    group = n_stu
    assert n_que == 2 * group
    send = functools.partial(send_over, n_stu=n_stu, n_que=n_que)
    swap = functools.partial(swap_cores, n_stu=n_stu, n_que=n_que)
    size, width = theta.shape
    rows = 2 * group * size
    half = rows // 2
    assert width == LANES // 2 and rows == 2 * LANES
    assert disc.shape == theta.shape and codes.shape == (rows, half)
    core = lax.rem(lax.axis_index("que"), 2)
    peer_theta, peer_disc, peer_icpt = swap(theta), swap(disc), swap(intercept)
    here = jnp.where(core == 0, theta, disc)
    there = jnp.where(core == 0, peer_theta, peer_disc)
    icpt = jnp.pad(jnp.stack([intercept, peer_icpt]), ((0, 0), (0, width - size))).reshape(1, LANES)
    mine = jnp.concatenate(
        [jnp.concatenate([here, there], 1), icpt, jnp.zeros((BIAS - 1, LANES), jnp.float32)], 0
    )
    (code,) = call(arrange_kernel, [(rows, rows)], codes, swap(codes))
    mine = [mine]
    for steps in stages(group):
        joined = jnp.concatenate(mine, 0)
        mine = mine + [send(joined, step) for step in steps]
    other = [swap(piece) for piece in mine]

    def totals(value):
        parts = [value]
        for number, steps in enumerate(stages(group)):
            if number:
                parts = [functools.reduce(jnp.add, parts)]
            parts = parts + [send(parts[0], step) for step in steps]
        return parts

    sums, left, right, weight, icpt = call(
        functools.partial(gradient_kernel, group, len(mine)),
        [(rows + BIAS, LANES), (rows, LANES), (rows, LANES), (rows, rows), (BIAS, LANES)],
        *mine,
        *other,
        code,
    )
    parts = totals(sums)
    first, diag, root = call(
        functools.partial(start_kernel, group, len(parts)),
        [(half + BIAS + size, LANES), (half + BIAS, LANES), (rows, LANES)],
        *parts,
        left,
        icpt,
    )
    peer = swap(first)
    (sums,) = call(image_kernel, [(half + BIAS, LANES)], first, peer, left, right, weight)
    parts = totals(sums)
    second, dots = call(
        functools.partial(second_kernel, group, len(parts)),
        [(half + BIAS, LANES), (8, LANES)],
        *parts,
        first,
        diag,
    )
    peer_second = swap(second)
    devices = n_stu * n_que
    (dots,) = call(form_kernel, [(devices, 1, LANES)], second, peer_second, left, right, weight, dots)
    dots = lax.all_to_all(dots, AXES, 0, 0, tiled=True)
    abilities, discs, icpts = call(
        functools.partial(finish_kernel, group),
        [(size, width), (size, width), (1, size)],
        dots,
        first,
        peer,
        second,
        peer_second,
        root,
    )
    return abilities, discs, icpts[0]


def solution(mesh):
    placed = (P("stu", "que"), P(("stu", "que"), None), P(("que", "stu"), None), P(("que", "stu")))
    return jax.shard_map(
        functools.partial(shards, mesh.shape["stu"], mesh.shape["que"]),
        mesh=mesh,
        in_specs=placed,
        out_specs=(P(("stu", "que"), None), P(("que", "stu"), None), P(("que", "stu"))),
        check_vma=False,
    )
```

```python
import functools

import jax
import jax.numpy as jnp
from jax import lax
from jax.experimental import pallas as pl
from jax.experimental.pallas import tpu as pltpu
from jax.sharding import PartitionSpec as P

AXES = ("stu", "que")
LANES = 128
GATHER_ORDER = (1, 3, 2)
FIRST_ORDER = (1, 3, 2)
SECOND_ORDER = (2, 1, 3)
BIAS = 8


def halves(value):
    high = value.astype(jnp.bfloat16)
    return high, (value - high.astype(jnp.float32)).astype(jnp.bfloat16)


def product(left, right, dims):
    return lax.dot_general(left, right, (dims, ((), ())), preferred_element_type=jnp.float32)


def dot_nt(left, right):
    left_high, left_low = halves(left)
    right_high, right_low = halves(right)
    dims = ((1,), (1,))
    both = product(
        jnp.concatenate([left_high, left_low], 1), jnp.concatenate([right_high, right_high], 1), dims
    )
    return both + product(left_high, right_low, dims)


def dot_nn(left, right):
    left_high, left_low = halves(left)
    right_high, right_low = halves(right)
    dims = ((1,), (0,))
    both = product(left_high, jnp.concatenate([right_high, right_low], 1), dims)
    width = right.shape[1]
    return both[:, :width] + both[:, width:] + product(left_low, right_high, dims)


def position():
    que = lax.axis_index("que")
    return lax.rem(que, 2), que // 2, lax.axis_index("stu")


def block_of(side, core, line, plane, group):
    return jnp.where(side == 0, line * 2 + core, core * group + plane)


def low_lanes(shape):
    return lax.broadcasted_iota(jnp.int32, shape, 1) < LANES // 2


def turn(value):
    return pltpu.roll(value, LANES // 2, 1)


def pack(value):
    half = value.shape[0] // 2
    low = low_lanes((half, LANES))
    return jnp.where(low, value[:half], turn(value[half:]))


def bias_rows(lanes):
    return jnp.concatenate([lanes[:, :LANES], lanes[:, LANES:]], 0)


def bias_lanes(rows):
    return jnp.concatenate([rows[0:1], rows[1:2]], 1)


def column(rows):
    wide = jnp.concatenate([rows, jnp.zeros((LANES - 2, LANES), jnp.float32)], 0)
    tall = wide.T
    return jnp.concatenate([tall[:, 0:1], tall[:, 1:2]], 0)


def arrange_kernel(own_ref, peer_ref, out_ref):
    core, _, _ = position()
    cols = own_ref.shape[1]

    @pl.when(core == 0)
    def _():
        out_ref[:, :cols] = own_ref[...].astype(jnp.float32)
        out_ref[:, cols:] = peer_ref[...].astype(jnp.float32)

    @pl.when(core == 1)
    def _():
        out_ref[:cols, :] = peer_ref[...].astype(jnp.float32).T
        out_ref[cols:, :] = own_ref[...].astype(jnp.float32).T


def pieces(refs, size):
    step = size + BIAS
    return [ref[first : first + step, :] for ref in refs for first in range(0, ref.shape[0], step)]


def place(blocks, dst_ref, side, columns, core, line, plane, group):
    size = dst_ref.shape[0] // (2 * group)
    lane = lax.broadcasted_iota(jnp.int32, (size, LANES), 1)
    half = LANES // 2
    for at, (k, block) in enumerate(blocks):
        for j in range(2):
            value = turn(block[:size]) if j else block[:size]
            last = jnp.where(side == 0, 1.0, columns[j * half : j * half + size, at : at + 1])
            row = block_of(side, core ^ j, line ^ k, plane ^ k, group) * size
            dst_ref[pl.ds(pl.multiple_of(row, size), size), :] = jnp.where(
                lane < half, value, jnp.where(lane == half, last, 0.0)
            )


def gradient_kernel(group, places, parts, *refs):
    code_ref, sums_ref, left_ref, right_ref, weight_ref, icpt_ref = refs[2 * parts :]
    core, line, plane = position()
    size = left_ref.shape[0] // (2 * group)
    mine = pieces(refs[:parts], size)
    other = pieces(refs[parts : 2 * parts], size)
    rows = [jnp.where(core == 0, there[size : size + 1], here[size : size + 1]) for here, there in zip(mine, other)]
    columns = jnp.concatenate(rows + [jnp.zeros((LANES - group, LANES), jnp.float32)], 0).T
    place(list(zip(places, mine)), left_ref, core, columns, core, line, plane, group)
    place(list(zip(places, other)), right_ref, 1 - core, columns, 1 - core, line, plane, group)
    left = left_ref[...]
    right = right_ref[...]
    prob = 1.0 / (1.0 + jnp.exp(-dot_nt(left, right)))
    code = code_ref[...]
    seen = code > 0.0
    resid = jnp.where(seen, prob - jnp.where(code == 2.0, 1.0, 0.0), 0.0)
    weight = jnp.where(seen, prob * (1.0 - prob), 0.0)
    weight_ref[...] = weight
    rows = left.shape[0]
    grad = dot_nn(resid, right)
    diag = dot_nn(weight, right * right)
    sums_ref[:rows, :] = jnp.where(low_lanes((rows, LANES)), grad, turn(diag))
    at = LANES // 2

    @pl.when(core == 0)
    def _():
        sums_ref[rows:, :] = jnp.zeros((BIAS, LANES), jnp.float32)
        icpt_ref[...] = jnp.zeros((BIAS, LANES), jnp.float32)

    @pl.when(core == 1)
    def _():
        lane = lax.broadcasted_iota(jnp.int32, (rows, LANES), 1)
        moved = jnp.where(lane == at + 1, pltpu.roll(diag, 1, 1), pltpu.roll(left, 2, 1))
        lanes = jnp.where(lane == at, grad, moved).T
        spare = jnp.zeros((BIAS - 4, LANES), jnp.float32)
        sums_ref[rows:, :] = jnp.concatenate([bias_rows(lanes[at : at + 1]), bias_rows(lanes[at + 1 : at + 2]), spare], 0)
        spare = jnp.zeros((BIAS - 2, LANES), jnp.float32)
        icpt_ref[...] = jnp.concatenate([bias_rows(lanes[at + 2 : at + 3]), spare], 0)


def start_kernel(group, parts, *refs):
    sum_refs, (left_ref, icpt_ref, send_ref, diag_ref, root_ref) = refs[:parts], refs[parts:]
    core, line, plane = position()
    total = sum_refs[0][...]
    for ref in sum_refs[1:]:
        total = total + ref[...]
    rows = left_ref.shape[0]
    half = rows // 2
    low = low_lanes((rows, LANES))
    main = total[:rows]
    diag = jnp.where(low, turn(main) + 1.0, 1.0)
    first = jnp.where(low, -(main + left_ref[...]) / diag, 0.0)
    grad_b = total[rows : rows + 2] + icpt_ref[:2]
    diag_b = total[rows + 2 : rows + 4] + 1.0
    first_b = -grad_b / diag_b
    root_ref[...] = jnp.sqrt(diag)
    send_ref[:half, :] = pack(first)
    send_ref[half : half + BIAS, :] = jnp.concatenate(
        [first_b, jnp.sqrt(diag_b), jnp.zeros((BIAS - 4, LANES), jnp.float32)], 0
    )
    diag_ref[:half, :] = pack(diag)
    diag_ref[half:, :] = jnp.concatenate([diag_b, jnp.ones((BIAS - 2, LANES), jnp.float32)], 0)
    size = rows // (2 * group)
    at = block_of(core, 1 - core, line, plane, group) * size
    send_ref[half + BIAS :, :] = root_ref[pl.ds(pl.multiple_of(at, size), size), :]


def change_of(mine_ref, other_ref, left, right, half):
    low = low_lanes((half, LANES))
    mine = mine_ref[:half, :]
    other = other_ref[:half, :]
    lhs = jnp.concatenate(
        [
            jnp.where(low, mine, turn(left[:half])),
            jnp.where(low, turn(mine), turn(left[half:])),
        ],
        0,
    )
    rhs = jnp.concatenate(
        [
            jnp.where(low, right[:half], turn(other)),
            jnp.where(low, right[half:], other),
        ],
        0,
    )
    return dot_nt(lhs, rhs)


def with_bias(change, mine_ref, other_ref, half, use):
    core, _, _ = position()

    @pl.when(core == 0)
    def _():
        use(change + bias_lanes(other_ref[half : half + 2, :]))

    @pl.when(core == 1)
    def _():
        use(change + column(mine_ref[half : half + 2, :]))


def image_kernel(mine_ref, other_ref, left_ref, right_ref, weight_ref, sums_ref):
    core, _, _ = position()
    half = left_ref.shape[0] // 2
    right = right_ref[...]
    change = change_of(mine_ref, other_ref, left_ref[...], right, half)
    at = LANES // 2

    def use(value):
        sums = dot_nn(weight_ref[...] * value, right)
        sums_ref[:half, :] = pack(sums)
        sums_ref[half:, :] = jnp.zeros((BIAS, LANES), jnp.float32)

        @pl.when(core == 1)
        def _():
            sums_ref[half : half + 2, :] = bias_rows(sums.T[at : at + 1])

    with_bias(change, mine_ref, other_ref, half, use)


def second_kernel(group, parts, *refs):
    sum_refs, (send_ref, diag_ref, second_ref, dots_ref) = refs[:parts], refs[parts:]
    total = sum_refs[0][...]
    for ref in sum_refs[1:]:
        total = total + ref[...]
    half = total.shape[0] - BIAS
    row = lax.broadcasted_iota(jnp.int32, total.shape, 0)
    used = row < half + 2
    first = jnp.where(used, send_ref[: half + BIAS, :], 0.0)
    diag = diag_ref[...]
    lift = jnp.where(used, total + first - diag * first, 0.0)
    second = lift / diag
    second_ref[...] = second
    scale = 1.0 / group
    lane = lax.broadcasted_iota(jnp.int32, (8, LANES), 1)
    dots = jnp.zeros((8, LANES), jnp.float32)
    for at, value in enumerate((first * first * diag, first * lift, second * lift, second * second)):
        dots = jnp.where(lane == at, jnp.sum(value) * scale, dots)
    dots_ref[...] = dots


def form_kernel(mine_ref, other_ref, left_ref, right_ref, weight_ref, dots_ref, out_ref):
    half = left_ref.shape[0] // 2
    change = change_of(mine_ref, other_ref, left_ref[...], right_ref[...], half)

    def use(value):
        form = 0.5 * jnp.sum(weight_ref[...] * value * value)
        lane = lax.broadcasted_iota(jnp.int32, (1, LANES), 1)
        dots = dots_ref[0:1, :] + jnp.where(lane == 3, form, 0.0)
        out_ref[...] = jnp.broadcast_to(dots[None], out_ref.shape)

    with_bias(change, mine_ref, other_ref, half, use)


def finish_kernel(
    group, dots_ref, send_ref, peer_ref, second_ref, peer_second_ref, root_ref, theta_ref, disc_ref, icpt_ref
):
    core, line, plane = position()
    dots = jnp.sum(dots_ref[...], axis=0)
    lane = lax.broadcasted_iota(jnp.int32, (1, LANES), 1)
    a, f, h, d = [jnp.sum(jnp.where(lane == at, dots, 0.0), axis=1, keepdims=True) for at in range(4)]
    b = a + f
    e = f + h
    det = b * d - e * e
    s = (a * d - e * f) / det
    t = (f * f - a * h) / det
    rows = root_ref.shape[0]
    half = rows // 2
    size = rows // (2 * group)

    def direction(first_ref, next_ref, at):
        upper = at // group
        rows_at = pl.ds(pl.multiple_of(lax.rem(at, group) * size, size), size)
        value = s * first_ref[rows_at, :] + t * next_ref[rows_at, :]
        return jnp.where(upper == 1, turn(value), value)

    mine_at = block_of(core, core, line, plane, group)
    other_at = block_of(1 - core, core, line, plane, group)
    mine = direction(send_ref, second_ref, mine_at)
    mine = mine * root_ref[pl.ds(pl.multiple_of(mine_at * size, size), size), :]
    other = direction(peer_ref, peer_second_ref, other_at) * peer_ref[half + BIAS :, :]
    theta_ref[...] = jnp.where(core == 0, mine, other)[:, : LANES // 2]
    disc_ref[...] = jnp.where(core == 0, other, mine)[:, : LANES // 2]
    ask = jnp.where(core == 0, peer_ref[half : half + BIAS, :], send_ref[half : half + BIAS, :])
    ask_next = jnp.where(core == 0, peer_second_ref[half : half + 2, :], second_ref[half : half + 2, :])
    bias = (s * ask[0:2] + t * ask_next) * ask[2:4]
    disc_at = jnp.where(core == 0, other_at, mine_at)
    row = jnp.where(disc_at // group == 1, bias[1:2], bias[0:1])
    back = lax.rem(LANES - lax.rem(disc_at, group) * size, LANES)
    icpt_ref[...] = pltpu.roll(row, back, 1)[:, :size]


def call(kernel, shapes, *args):
    out = [jax.ShapeDtypeStruct(shape, jnp.float32) for shape in shapes]
    return pl.pallas_call(
        kernel,
        out_shape=out,
        in_specs=[pl.BlockSpec(memory_space=pltpu.VMEM)] * len(args),
        out_specs=[pl.BlockSpec(memory_space=pltpu.VMEM)] * len(out),
        compiler_params=pltpu.CompilerParams(vmem_limit_bytes=32 * 2**20),
    )(*args)


def swap_cores(value, n_stu, n_que):
    return lax.ppermute(value, AXES, [(i, i ^ 1) for i in range(n_stu * n_que)])


def send_over(value, step, n_stu, n_que):
    pairs = []
    for stu in range(n_stu):
        for que in range(n_que):
            there = (stu, que ^ (2 * step)) if que % 2 == 0 else (stu ^ step, que)
            pairs.append((stu * n_que + que, there[0] * n_que + there[1]))
    return lax.ppermute(value, AXES, pairs)


def stages(group, order):
    base = 1
    while base < group:
        width = min(4, group // base)
        yield [base * k for k in order if k < width]
        base *= width


def shards(n_stu, n_que, codes, theta, disc, intercept):
    group = n_stu
    assert n_que == 2 * group
    send = functools.partial(send_over, n_stu=n_stu, n_que=n_que)
    swap = functools.partial(swap_cores, n_stu=n_stu, n_que=n_que)
    size, width = theta.shape
    rows = 2 * group * size
    half = rows // 2
    assert width == LANES // 2 and rows == 2 * LANES
    assert disc.shape == theta.shape and codes.shape == (rows, half)
    core = lax.rem(lax.axis_index("que"), 2)
    peer_theta, peer_disc, peer_icpt = swap(theta), swap(disc), swap(intercept)
    here = jnp.where(core == 0, theta, disc)
    there = jnp.where(core == 0, peer_theta, peer_disc)
    icpt = jnp.pad(jnp.stack([intercept, peer_icpt]), ((0, 0), (0, width - size))).reshape(1, LANES)
    mine = jnp.concatenate(
        [jnp.concatenate([here, there], 1), icpt, jnp.zeros((BIAS - 1, LANES), jnp.float32)], 0
    )
    (code,) = call(arrange_kernel, [(rows, rows)], codes, swap(codes))
    mine = [mine]
    places = [0]
    for steps in stages(group, GATHER_ORDER):
        joined = jnp.concatenate(mine, 0)
        mine = mine + [send(joined, step) for step in steps]
        places = places + [step + place for step in steps for place in places]
    other = [swap(piece) for piece in mine]

    def totals(value, order):
        parts = [value]
        for number, steps in enumerate(stages(group, order)):
            if number:
                parts = [functools.reduce(jnp.add, parts)]
            parts = parts + [send(parts[0], step) for step in steps]
        return parts

    sums, left, right, weight, icpt = call(
        functools.partial(gradient_kernel, group, tuple(places), len(mine)),
        [(rows + BIAS, LANES), (rows, LANES), (rows, LANES), (rows, rows), (BIAS, LANES)],
        *mine,
        *other,
        code,
    )
    parts = totals(sums, FIRST_ORDER)
    first, diag, root = call(
        functools.partial(start_kernel, group, len(parts)),
        [(half + BIAS + size, LANES), (half + BIAS, LANES), (rows, LANES)],
        *parts,
        left,
        icpt,
    )
    peer = swap(first)
    (sums,) = call(image_kernel, [(half + BIAS, LANES)], first, peer, left, right, weight)
    parts = totals(sums, SECOND_ORDER)
    second, dots = call(
        functools.partial(second_kernel, group, len(parts)),
        [(half + BIAS, LANES), (8, LANES)],
        *parts,
        first,
        diag,
    )
    peer_second = swap(second)
    devices = n_stu * n_que
    (dots,) = call(form_kernel, [(devices, 1, LANES)], second, peer_second, left, right, weight, dots)
    dots = lax.all_to_all(dots, AXES, 0, 0, tiled=True)
    abilities, discs, icpts = call(
        functools.partial(finish_kernel, group),
        [(size, width), (size, width), (1, size)],
        dots,
        first,
        peer,
        second,
        peer_second,
        root,
    )
    return abilities, discs, icpts[0]


def solution(mesh):
    placed = (P("stu", "que"), P(("stu", "que"), None), P(("que", "stu"), None), P(("que", "stu")))
    return jax.shard_map(
        functools.partial(shards, mesh.shape["stu"], mesh.shape["que"]),
        mesh=mesh,
        in_specs=placed,
        out_specs=(P(("stu", "que"), None), P(("que", "stu"), None), P(("que", "stu"))),
        check_vma=False,
    )
```

```python
import functools

import jax
import jax.numpy as jnp
from jax import lax
from jax.experimental import pallas as pl
from jax.experimental.pallas import tpu as pltpu
from jax.sharding import PartitionSpec as P

AXES = ("stu", "que")
LANES = 128
GATHER_ORDER = (1, 3, 2)
FIRST_ORDER = (1, 3, 2)
SECOND_ORDER = (2, 1, 3)
BIAS = 8


def halves(value):
    high = value.astype(jnp.bfloat16)
    return high, (value - high.astype(jnp.float32)).astype(jnp.bfloat16)


def product(left, right, dims):
    return lax.dot_general(left, right, (dims, ((), ())), preferred_element_type=jnp.float32)


def dot_nt(left, right):
    left_high, left_low = halves(left)
    right_high, right_low = halves(right)
    dims = ((1,), (1,))
    both = product(
        jnp.concatenate([left_high, left_low], 1), jnp.concatenate([right_high, right_high], 1), dims
    )
    return both + product(left_high, right_low, dims)


def dot_nn(left, right):
    left_high, left_low = halves(left)
    right_high, right_low = halves(right)
    dims = ((1,), (0,))
    both = product(left_high, jnp.concatenate([right_high, right_low], 1), dims)
    width = right.shape[1]
    return both[:, :width] + both[:, width:] + product(left_low, right_high, dims)


def position():
    que = lax.axis_index("que")
    return lax.rem(que, 2), que // 2, lax.axis_index("stu")


def block_of(side, core, line, plane, group):
    return jnp.where(side == 0, line * 2 + core, core * group + plane)


def low_lanes(shape):
    return lax.broadcasted_iota(jnp.int32, shape, 1) < LANES // 2


def turn(value):
    return pltpu.roll(value, LANES // 2, 1)


def pack(value):
    half = value.shape[0] // 2
    low = low_lanes((half, LANES))
    return jnp.where(low, value[:half], turn(value[half:]))


def bias_rows(lanes):
    return jnp.concatenate([lanes[:, :LANES], lanes[:, LANES:]], 0)


def bias_lanes(rows):
    return jnp.concatenate([rows[0:1], rows[1:2]], 1)


def column(rows):
    wide = jnp.concatenate([rows, jnp.zeros((LANES - 2, LANES), jnp.float32)], 0)
    tall = wide.T
    return jnp.concatenate([tall[:, 0:1], tall[:, 1:2]], 0)


def arrange_kernel(own_ref, peer_ref, out_ref):
    core, _, _ = position()
    cols = own_ref.shape[1]

    @pl.when(core == 0)
    def _():
        out_ref[:, :cols] = own_ref[...].astype(jnp.float32)
        out_ref[:, cols:] = peer_ref[...].astype(jnp.float32)

    @pl.when(core == 1)
    def _():
        out_ref[:cols, :] = peer_ref[...].astype(jnp.float32).T
        out_ref[cols:, :] = own_ref[...].astype(jnp.float32).T


def pieces(refs, size):
    step = size + BIAS
    return [ref[first : first + step, :] for ref in refs for first in range(0, ref.shape[0], step)]


def place(blocks, dst_ref, side, columns, core, line, plane, group):
    size = dst_ref.shape[0] // (2 * group)
    lane = lax.broadcasted_iota(jnp.int32, (size, LANES), 1)
    half = LANES // 2
    for at, (k, block) in enumerate(blocks):
        for j in range(2):
            value = turn(block[:size]) if j else block[:size]
            last = jnp.where(side == 0, 1.0, columns[j * half : j * half + size, at : at + 1])
            row = block_of(side, core ^ j, line ^ k, plane ^ k, group) * size
            dst_ref[pl.ds(pl.multiple_of(row, size), size), :] = jnp.where(
                lane < half, value, jnp.where(lane == half, last, 0.0)
            )


def gradient_kernel(group, places, parts, *refs):
    code_ref, sums_ref, left_ref, right_ref, weight_ref, icpt_ref = refs[2 * parts :]
    core, line, plane = position()
    size = left_ref.shape[0] // (2 * group)
    mine = pieces(refs[:parts], size)
    other = pieces(refs[parts : 2 * parts], size)
    rows = [jnp.where(core == 0, there[size : size + 1], here[size : size + 1]) for here, there in zip(mine, other)]
    columns = jnp.concatenate(rows + [jnp.zeros((LANES - group, LANES), jnp.float32)], 0).T
    place(list(zip(places, mine)), left_ref, core, columns, core, line, plane, group)
    place(list(zip(places, other)), right_ref, 1 - core, columns, 1 - core, line, plane, group)
    left = left_ref[...]
    right = right_ref[...]
    prob = 1.0 / (1.0 + jnp.exp(-dot_nt(left, right)))
    code = code_ref[...]
    seen = code > 0.0
    resid = jnp.where(seen, prob - jnp.where(code == 2.0, 1.0, 0.0), 0.0)
    weight = jnp.where(seen, prob * (1.0 - prob), 0.0)
    weight_ref[...] = weight
    rows = left.shape[0]
    grad = dot_nn(resid, right)
    diag = dot_nn(weight, right * right)
    sums_ref[:rows, :] = jnp.where(low_lanes((rows, LANES)), grad, turn(diag))
    at = LANES // 2

    @pl.when(core == 0)
    def _():
        sums_ref[rows:, :] = jnp.zeros((BIAS, LANES), jnp.float32)
        icpt_ref[...] = jnp.zeros((BIAS, LANES), jnp.float32)

    @pl.when(core == 1)
    def _():
        lane = lax.broadcasted_iota(jnp.int32, (rows, LANES), 1)
        moved = jnp.where(lane == at + 1, pltpu.roll(diag, 1, 1), pltpu.roll(left, 2, 1))
        lanes = jnp.where(lane == at, grad, moved).T
        spare = jnp.zeros((BIAS - 4, LANES), jnp.float32)
        sums_ref[rows:, :] = jnp.concatenate([bias_rows(lanes[at : at + 1]), bias_rows(lanes[at + 1 : at + 2]), spare], 0)
        spare = jnp.zeros((BIAS - 2, LANES), jnp.float32)
        icpt_ref[...] = jnp.concatenate([bias_rows(lanes[at + 2 : at + 3]), spare], 0)


def start_kernel(group, parts, *refs):
    sum_refs, (left_ref, icpt_ref, send_ref, diag_ref, root_ref) = refs[:parts], refs[parts:]
    core, line, plane = position()
    total = sum_refs[0][...]
    for ref in sum_refs[1:]:
        total = total + ref[...]
    rows = left_ref.shape[0]
    half = rows // 2
    low = low_lanes((rows, LANES))
    main = total[:rows]
    diag = jnp.where(low, turn(main) + 1.0, 1.0)
    first = jnp.where(low, -(main + left_ref[...]) / diag, 0.0)
    grad_b = total[rows : rows + 2] + icpt_ref[:2]
    diag_b = total[rows + 2 : rows + 4] + 1.0
    first_b = -grad_b / diag_b
    root_ref[...] = jnp.sqrt(diag)
    send_ref[:half, :] = pack(first)
    send_ref[half : half + BIAS, :] = jnp.concatenate(
        [first_b, jnp.sqrt(diag_b), jnp.zeros((BIAS - 4, LANES), jnp.float32)], 0
    )
    diag_ref[:half, :] = pack(diag)
    diag_ref[half:, :] = jnp.concatenate([diag_b, jnp.ones((BIAS - 2, LANES), jnp.float32)], 0)
    size = rows // (2 * group)
    at = block_of(core, 1 - core, line, plane, group) * size
    send_ref[half + BIAS :, :] = root_ref[pl.ds(pl.multiple_of(at, size), size), :]


def change_of(mine_ref, other_ref, left, right, half):
    low = low_lanes((half, LANES))
    mine = mine_ref[:half, :]
    other = other_ref[:half, :]
    lhs = jnp.concatenate(
        [
            jnp.where(low, mine, turn(left[:half])),
            jnp.where(low, turn(mine), turn(left[half:])),
        ],
        0,
    )
    rhs = jnp.concatenate(
        [
            jnp.where(low, right[:half], turn(other)),
            jnp.where(low, right[half:], other),
        ],
        0,
    )
    return dot_nt(lhs, rhs)


def with_bias(change, mine_ref, other_ref, half, use):
    core, _, _ = position()

    @pl.when(core == 0)
    def _():
        use(change + bias_lanes(other_ref[half : half + 2, :]))

    @pl.when(core == 1)
    def _():
        use(change + column(mine_ref[half : half + 2, :]))


def image_kernel(mine_ref, other_ref, left_ref, right_ref, weight_ref, sums_ref):
    core, _, _ = position()
    half = left_ref.shape[0] // 2
    right = right_ref[...]
    change = change_of(mine_ref, other_ref, left_ref[...], right, half)
    at = LANES // 2

    def use(value):
        sums = dot_nn(weight_ref[...] * value, right)
        sums_ref[:half, :] = pack(sums)
        sums_ref[half:, :] = jnp.zeros((BIAS, LANES), jnp.float32)

        @pl.when(core == 1)
        def _():
            sums_ref[half : half + 2, :] = bias_rows(sums.T[at : at + 1])

    with_bias(change, mine_ref, other_ref, half, use)


def second_kernel(group, parts, *refs):
    sum_refs, (send_ref, diag_ref, second_ref, dots_ref) = refs[:parts], refs[parts:]
    total = sum_refs[0][...]
    for ref in sum_refs[1:]:
        total = total + ref[...]
    half = total.shape[0] - BIAS
    row = lax.broadcasted_iota(jnp.int32, total.shape, 0)
    used = row < half + 2
    first = jnp.where(used, send_ref[: half + BIAS, :], 0.0)
    diag = diag_ref[...]
    lift = jnp.where(used, total + first - diag * first, 0.0)
    second = lift / diag
    second_ref[...] = second
    scale = 1.0 / group
    lane = lax.broadcasted_iota(jnp.int32, (8, LANES), 1)
    dots = jnp.zeros((8, LANES), jnp.float32)
    for at, value in enumerate((first * first * diag, first * lift, second * lift, second * second)):
        dots = jnp.where(lane == at, jnp.sum(value) * scale, dots)
    dots_ref[...] = dots


def form_kernel(mine_ref, other_ref, left_ref, right_ref, weight_ref, dots_ref, out_ref):
    half = left_ref.shape[0] // 2
    change = change_of(mine_ref, other_ref, left_ref[...], right_ref[...], half)

    def use(value):
        form = 0.5 * jnp.sum(weight_ref[...] * value * value)
        lane = lax.broadcasted_iota(jnp.int32, (1, LANES), 1)
        dots = dots_ref[0:1, :] + jnp.where(lane == 3, form, 0.0)
        out_ref[...] = jnp.broadcast_to(dots[None], out_ref.shape)

    with_bias(change, mine_ref, other_ref, half, use)


def finish_kernel(
    group, dots_ref, send_ref, peer_ref, second_ref, peer_second_ref, root_ref, theta_ref, disc_ref, icpt_ref
):
    core, line, plane = position()
    dots = jnp.sum(dots_ref[...], axis=0)
    lane = lax.broadcasted_iota(jnp.int32, (1, LANES), 1)
    a, f, h, d = [jnp.sum(jnp.where(lane == at, dots, 0.0), axis=1, keepdims=True) for at in range(4)]
    b = a + f
    e = f + h
    det = b * d - e * e
    s = (a * d - e * f) / det
    t = (f * f - a * h) / det
    rows = root_ref.shape[0]
    half = rows // 2
    size = rows // (2 * group)

    def direction(first_ref, next_ref, at):
        upper = at // group
        rows_at = pl.ds(pl.multiple_of(lax.rem(at, group) * size, size), size)
        value = s * first_ref[rows_at, :] + t * next_ref[rows_at, :]
        return jnp.where(upper == 1, turn(value), value)

    mine_at = block_of(core, core, line, plane, group)
    other_at = block_of(1 - core, core, line, plane, group)
    mine = direction(send_ref, second_ref, mine_at)
    mine = mine * root_ref[pl.ds(pl.multiple_of(mine_at * size, size), size), :]
    other = direction(peer_ref, peer_second_ref, other_at) * peer_ref[half + BIAS :, :]
    theta_ref[...] = jnp.where(core == 0, mine, other)[:, : LANES // 2]
    disc_ref[...] = jnp.where(core == 0, other, mine)[:, : LANES // 2]
    ask = jnp.where(core == 0, peer_ref[half : half + BIAS, :], send_ref[half : half + BIAS, :])
    ask_next = jnp.where(core == 0, peer_second_ref[half : half + 2, :], second_ref[half : half + 2, :])
    bias = (s * ask[0:2] + t * ask_next) * ask[2:4]
    disc_at = jnp.where(core == 0, other_at, mine_at)
    row = jnp.where(disc_at // group == 1, bias[1:2], bias[0:1])
    back = lax.rem(LANES - lax.rem(disc_at, group) * size, LANES)
    icpt_ref[...] = pltpu.roll(row, back, 1)[:, :size]


def call(kernel, shapes, *args):
    out = [jax.ShapeDtypeStruct(shape, jnp.float32) for shape in shapes]
    return pl.pallas_call(
        kernel,
        out_shape=out,
        in_specs=[pl.BlockSpec(memory_space=pltpu.VMEM)] * len(args),
        out_specs=[pl.BlockSpec(memory_space=pltpu.VMEM)] * len(out),
        compiler_params=pltpu.CompilerParams(vmem_limit_bytes=32 * 2**20),
    )(*args)


def swap_cores(value, n_stu, n_que):
    return lax.ppermute(value, AXES, [(i, i ^ 1) for i in range(n_stu * n_que)])


def send_over(value, step, n_stu, n_que, crossed=False):
    pairs = []
    for stu in range(n_stu):
        for que in range(n_que):
            there = (stu, que ^ (2 * step)) if (que % 2 == 0) != crossed else (stu ^ step, que)
            pairs.append((stu * n_que + que, there[0] * n_que + there[1]))
    return lax.ppermute(value, AXES, pairs)


def stages(group, order):
    base = 1
    while base < group:
        width = min(4, group // base)
        yield [base * k for k in order if k < width]
        base *= width


def shards(n_stu, n_que, codes, theta, disc, intercept):
    group = n_stu
    assert n_que == 2 * group
    send = functools.partial(send_over, n_stu=n_stu, n_que=n_que)
    swap = functools.partial(swap_cores, n_stu=n_stu, n_que=n_que)
    size, width = theta.shape
    rows = 2 * group * size
    half = rows // 2
    assert width == LANES // 2 and rows == 2 * LANES
    assert disc.shape == theta.shape and codes.shape == (rows, half)
    core = lax.rem(lax.axis_index("que"), 2)
    peer_theta, peer_disc, peer_icpt = swap(theta), swap(disc), swap(intercept)

    def block(own, own_icpt, peers, peers_icpt):
        icpt = jnp.pad(jnp.stack([own_icpt, peers_icpt]), ((0, 0), (0, width - size))).reshape(1, LANES)
        spare = jnp.zeros((BIAS - 1, LANES), jnp.float32)
        return jnp.concatenate([jnp.concatenate([own, peers], 1), icpt, spare], 0)

    def side(students, questions):
        return jnp.where(core == 0, students, questions)

    mine = [block(side(theta, disc), intercept, side(peer_theta, peer_disc), peer_icpt)]
    other = [block(side(peer_disc, peer_theta), peer_icpt, side(disc, theta), intercept)]
    (code,) = call(arrange_kernel, [(rows, rows)], codes, swap(codes))
    places = [0]
    for steps in stages(group, GATHER_ORDER):
        ours, theirs = jnp.concatenate(mine, 0), jnp.concatenate(other, 0)
        for step in steps:
            crossed = step == max(steps)
            piece = send(theirs if crossed else ours, step, crossed=crossed)
            back = swap(piece)
            mine.append(back if crossed else piece)
            other.append(piece if crossed else back)
        places = places + [step + place for step in steps for place in places]

    def totals(value, order):
        parts = [value]
        for number, steps in enumerate(stages(group, order)):
            if number:
                parts = [functools.reduce(jnp.add, parts)]
            parts = parts + [send(parts[0], step) for step in steps]
        return parts

    sums, left, right, weight, icpt = call(
        functools.partial(gradient_kernel, group, tuple(places), len(mine)),
        [(rows + BIAS, LANES), (rows, LANES), (rows, LANES), (rows, rows), (BIAS, LANES)],
        *mine,
        *other,
        code,
    )
    parts = totals(sums, FIRST_ORDER)
    first, diag, root = call(
        functools.partial(start_kernel, group, len(parts)),
        [(half + BIAS + size, LANES), (half + BIAS, LANES), (rows, LANES)],
        *parts,
        left,
        icpt,
    )
    peer = swap(first)
    (sums,) = call(image_kernel, [(half + BIAS, LANES)], first, peer, left, right, weight)
    parts = totals(sums, SECOND_ORDER)
    second, dots = call(
        functools.partial(second_kernel, group, len(parts)),
        [(half + BIAS, LANES), (8, LANES)],
        *parts,
        first,
        diag,
    )
    peer_second = swap(second)
    devices = n_stu * n_que
    (dots,) = call(form_kernel, [(devices, 1, LANES)], second, peer_second, left, right, weight, dots)
    dots = lax.all_to_all(dots, AXES, 0, 0, tiled=True)
    abilities, discs, icpts = call(
        functools.partial(finish_kernel, group),
        [(size, width), (size, width), (1, size)],
        dots,
        first,
        peer,
        second,
        peer_second,
        root,
    )
    return abilities, discs, icpts[0]


def solution(mesh):
    placed = (P("stu", "que"), P(("stu", "que"), None), P(("que", "stu"), None), P(("que", "stu")))
    return jax.shard_map(
        functools.partial(shards, mesh.shape["stu"], mesh.shape["que"]),
        mesh=mesh,
        in_specs=placed,
        out_specs=(P(("stu", "que"), None), P(("que", "stu"), None), P(("que", "stu"))),
        check_vma=False,
    )
```

```python
import functools

import jax
import jax.numpy as jnp
from jax import lax
from jax.experimental import pallas as pl
from jax.experimental.pallas import tpu as pltpu
from jax.sharding import PartitionSpec as P

AXES = ("stu", "que")
LANES = 128
GATHER_ORDER = (1, 3, 2)
FIRST_ORDER = (3, 1, 2)
SECOND_ORDER = (2, 1, 3)
BIAS = 8


def halves(value):
    high = value.astype(jnp.bfloat16)
    return high, (value - high.astype(jnp.float32)).astype(jnp.bfloat16)


def product(left, right, dims):
    return lax.dot_general(left, right, (dims, ((), ())), preferred_element_type=jnp.float32)


def dot_nt(left, right):
    left_high, left_low = halves(left)
    right_high, right_low = halves(right)
    dims = ((1,), (1,))
    both = product(
        jnp.concatenate([left_high, left_low], 1), jnp.concatenate([right_high, right_high], 1), dims
    )
    return both + product(left_high, right_low, dims)


def dot_nn(left, right):
    left_high, left_low = halves(left)
    right_high, right_low = halves(right)
    dims = ((1,), (0,))
    both = product(left_high, jnp.concatenate([right_high, right_low], 1), dims)
    width = right.shape[1]
    return both[:, :width] + both[:, width:] + product(left_low, right_high, dims)


def position():
    que = lax.axis_index("que")
    return lax.rem(que, 2), que // 2, lax.axis_index("stu")


def block_of(side, core, line, plane, group):
    return jnp.where(side == 0, line * 2 + core, core * group + plane)


def low_lanes(shape):
    return lax.broadcasted_iota(jnp.int32, shape, 1) < LANES // 2


def turn(value):
    return pltpu.roll(value, LANES // 2, 1)


def pack(value):
    half = value.shape[0] // 2
    low = low_lanes((half, LANES))
    return jnp.where(low, value[:half], turn(value[half:]))


def bias_rows(lanes):
    return jnp.concatenate([lanes[:, :LANES], lanes[:, LANES:]], 0)


def bias_lanes(rows):
    return jnp.concatenate([rows[0:1], rows[1:2]], 1)


def column(rows):
    wide = jnp.concatenate([rows, jnp.zeros((LANES - 2, LANES), jnp.float32)], 0)
    tall = wide.T
    return jnp.concatenate([tall[:, 0:1], tall[:, 1:2]], 0)


def arrange_kernel(own_ref, peer_ref, out_ref):
    core, _, _ = position()
    cols = own_ref.shape[1]

    @pl.when(core == 0)
    def _():
        out_ref[:, :cols] = own_ref[...].astype(jnp.float32)
        out_ref[:, cols:] = peer_ref[...].astype(jnp.float32)

    @pl.when(core == 1)
    def _():
        out_ref[:cols, :] = peer_ref[...].astype(jnp.float32).T
        out_ref[cols:, :] = own_ref[...].astype(jnp.float32).T


def pieces(refs, size):
    step = size + BIAS
    return [ref[first : first + step, :] for ref in refs for first in range(0, ref.shape[0], step)]


def place(blocks, dst_ref, side, columns, core, line, plane, group):
    size = dst_ref.shape[0] // (2 * group)
    lane = lax.broadcasted_iota(jnp.int32, (size, LANES), 1)
    half = LANES // 2
    for at, (k, block) in enumerate(blocks):
        for j in range(2):
            value = turn(block[:size]) if j else block[:size]
            last = jnp.where(side == 0, 1.0, columns[j * half : j * half + size, at : at + 1])
            row = block_of(side, core ^ j, line ^ k, plane ^ k, group) * size
            dst_ref[pl.ds(pl.multiple_of(row, size), size), :] = jnp.where(
                lane < half, value, jnp.where(lane == half, last, 0.0)
            )


def gradient_kernel(group, places, parts, *refs):
    code_ref, sums_ref, left_ref, right_ref, weight_ref, icpt_ref = refs[2 * parts :]
    core, line, plane = position()
    size = left_ref.shape[0] // (2 * group)
    mine = pieces(refs[:parts], size)
    other = pieces(refs[parts : 2 * parts], size)
    rows = [jnp.where(core == 0, there[size : size + 1], here[size : size + 1]) for here, there in zip(mine, other)]
    columns = jnp.concatenate(rows + [jnp.zeros((LANES - group, LANES), jnp.float32)], 0).T
    place(list(zip(places, mine)), left_ref, core, columns, core, line, plane, group)
    place(list(zip(places, other)), right_ref, 1 - core, columns, 1 - core, line, plane, group)
    left = left_ref[...]
    right = right_ref[...]
    prob = 1.0 / (1.0 + jnp.exp(-dot_nt(left, right)))
    code = code_ref[...]
    seen = code > 0.0
    resid = jnp.where(seen, prob - jnp.where(code == 2.0, 1.0, 0.0), 0.0)
    weight = jnp.where(seen, prob * (1.0 - prob), 0.0)
    weight_ref[...] = weight
    rows = left.shape[0]
    grad = dot_nn(resid, right)
    diag = dot_nn(weight, right * right)
    sums_ref[:rows, :] = jnp.where(low_lanes((rows, LANES)), grad, turn(diag))
    at = LANES // 2

    @pl.when(core == 0)
    def _():
        sums_ref[rows:, :] = jnp.zeros((BIAS, LANES), jnp.float32)
        icpt_ref[...] = jnp.zeros((BIAS, LANES), jnp.float32)

    @pl.when(core == 1)
    def _():
        lane = lax.broadcasted_iota(jnp.int32, (rows, LANES), 1)
        moved = jnp.where(lane == at + 1, pltpu.roll(diag, 1, 1), pltpu.roll(left, 2, 1))
        lanes = jnp.where(lane == at, grad, moved).T
        spare = jnp.zeros((BIAS - 4, LANES), jnp.float32)
        sums_ref[rows:, :] = jnp.concatenate([bias_rows(lanes[at : at + 1]), bias_rows(lanes[at + 1 : at + 2]), spare], 0)
        spare = jnp.zeros((BIAS - 2, LANES), jnp.float32)
        icpt_ref[...] = jnp.concatenate([bias_rows(lanes[at + 2 : at + 3]), spare], 0)


def start_kernel(group, parts, *refs):
    sum_refs, (left_ref, icpt_ref, send_ref, diag_ref, root_ref) = refs[:parts], refs[parts:]
    core, line, plane = position()
    total = sum_refs[0][...]
    for ref in sum_refs[1:]:
        total = total + ref[...]
    rows = left_ref.shape[0]
    half = rows // 2
    low = low_lanes((rows, LANES))
    main = total[:rows]
    diag = jnp.where(low, turn(main) + 1.0, 1.0)
    first = jnp.where(low, -(main + left_ref[...]) / diag, 0.0)
    grad_b = total[rows : rows + 2] + icpt_ref[:2]
    diag_b = total[rows + 2 : rows + 4] + 1.0
    first_b = -grad_b / diag_b
    root_ref[...] = jnp.sqrt(diag)
    send_ref[:half, :] = pack(first)
    send_ref[half : half + BIAS, :] = jnp.concatenate(
        [first_b, jnp.sqrt(diag_b), jnp.zeros((BIAS - 4, LANES), jnp.float32)], 0
    )
    diag_ref[:half, :] = pack(diag)
    diag_ref[half:, :] = jnp.concatenate([diag_b, jnp.ones((BIAS - 2, LANES), jnp.float32)], 0)
    size = rows // (2 * group)
    at = block_of(core, 1 - core, line, plane, group) * size
    send_ref[half + BIAS :, :] = root_ref[pl.ds(pl.multiple_of(at, size), size), :]


def change_of(mine_ref, other_ref, left, right, half):
    low = low_lanes((half, LANES))
    mine = mine_ref[:half, :]
    other = other_ref[:half, :]
    lhs = jnp.concatenate(
        [
            jnp.where(low, mine, turn(left[:half])),
            jnp.where(low, turn(mine), turn(left[half:])),
        ],
        0,
    )
    rhs = jnp.concatenate(
        [
            jnp.where(low, right[:half], turn(other)),
            jnp.where(low, right[half:], other),
        ],
        0,
    )
    return dot_nt(lhs, rhs)


def with_bias(change, mine_ref, other_ref, half, use):
    core, _, _ = position()

    @pl.when(core == 0)
    def _():
        use(change + bias_lanes(other_ref[half : half + 2, :]))

    @pl.when(core == 1)
    def _():
        use(change + column(mine_ref[half : half + 2, :]))


def image_kernel(mine_ref, other_ref, left_ref, right_ref, weight_ref, sums_ref):
    core, _, _ = position()
    half = left_ref.shape[0] // 2
    right = right_ref[...]
    change = change_of(mine_ref, other_ref, left_ref[...], right, half)
    at = LANES // 2

    def use(value):
        sums = dot_nn(weight_ref[...] * value, right)
        sums_ref[:half, :] = pack(sums)
        sums_ref[half:, :] = jnp.zeros((BIAS, LANES), jnp.float32)

        @pl.when(core == 1)
        def _():
            sums_ref[half : half + 2, :] = bias_rows(sums.T[at : at + 1])

    with_bias(change, mine_ref, other_ref, half, use)


def second_kernel(group, parts, *refs):
    sum_refs, (send_ref, diag_ref, second_ref, dots_ref) = refs[:parts], refs[parts:]
    total = sum_refs[0][...]
    for ref in sum_refs[1:]:
        total = total + ref[...]
    half = total.shape[0] - BIAS
    row = lax.broadcasted_iota(jnp.int32, total.shape, 0)
    used = row < half + 2
    first = jnp.where(used, send_ref[: half + BIAS, :], 0.0)
    diag = diag_ref[...]
    lift = jnp.where(used, total + first - diag * first, 0.0)
    second = lift / diag
    second_ref[...] = second
    terms = (first * first * diag, first * lift, second * lift, second * second)
    dots_ref[...] = jnp.concatenate(
        [jnp.sum(term, axis=0, keepdims=True) for term in terms] + [jnp.zeros((8 - len(terms), LANES), jnp.float32)], 0
    ) * (1.0 / group)


def form_kernel(mine_ref, other_ref, left_ref, right_ref, weight_ref, dots_ref, out_ref):
    half = left_ref.shape[0] // 2
    change = change_of(mine_ref, other_ref, left_ref[...], right_ref[...], half)

    def use(value):
        form = 0.5 * jnp.sum(weight_ref[...] * value * value, axis=0, keepdims=True)
        row = lax.broadcasted_iota(jnp.int32, (8, LANES), 0)
        terms = dots_ref[...] + jnp.where(row == 3, form[:, :LANES] + form[:, LANES:], 0.0)
        sums = jnp.sum(terms, axis=1, keepdims=True)
        lane = lax.broadcasted_iota(jnp.int32, (8, LANES), 1)
        dots = jnp.sum(jnp.where(lane == row, sums, 0.0), axis=0, keepdims=True)
        out_ref[...] = jnp.broadcast_to(dots[None], out_ref.shape)

    with_bias(change, mine_ref, other_ref, half, use)


def finish_kernel(
    group, dots_ref, send_ref, peer_ref, second_ref, peer_second_ref, root_ref, theta_ref, disc_ref, icpt_ref
):
    core, line, plane = position()
    dots = jnp.sum(dots_ref[...], axis=0)
    lane = lax.broadcasted_iota(jnp.int32, (8, LANES), 1)
    row = lax.broadcasted_iota(jnp.int32, (8, LANES), 0)
    sums = jnp.sum(jnp.where(lane == row, dots, 0.0), axis=1, keepdims=True)
    a, f, h, d = [sums[at : at + 1] for at in range(4)]
    b = a + f
    e = f + h
    det = b * d - e * e
    s = (a * d - e * f) / det
    t = (f * f - a * h) / det
    rows = root_ref.shape[0]
    half = rows // 2
    size = rows // (2 * group)

    def direction(first_ref, next_ref, at):
        upper = at // group
        rows_at = pl.ds(pl.multiple_of(lax.rem(at, group) * size, size), size)
        value = s * first_ref[rows_at, :] + t * next_ref[rows_at, :]
        return jnp.where(upper == 1, turn(value), value)

    mine_at = block_of(core, core, line, plane, group)
    other_at = block_of(1 - core, core, line, plane, group)
    mine = direction(send_ref, second_ref, mine_at)
    mine = mine * root_ref[pl.ds(pl.multiple_of(mine_at * size, size), size), :]
    other = direction(peer_ref, peer_second_ref, other_at) * peer_ref[half + BIAS :, :]
    theta_ref[...] = jnp.where(core == 0, mine, other)[:, : LANES // 2]
    disc_ref[...] = jnp.where(core == 0, other, mine)[:, : LANES // 2]
    ask = jnp.where(core == 0, peer_ref[half : half + BIAS, :], send_ref[half : half + BIAS, :])
    ask_next = jnp.where(core == 0, peer_second_ref[half : half + 2, :], second_ref[half : half + 2, :])
    bias = (s * ask[0:2] + t * ask_next) * ask[2:4]
    disc_at = jnp.where(core == 0, other_at, mine_at)
    row = jnp.where(disc_at // group == 1, bias[1:2], bias[0:1])
    back = lax.rem(LANES - lax.rem(disc_at, group) * size, LANES)
    icpt_ref[...] = pltpu.roll(row, back, 1)[:, :size]


def call(kernel, shapes, *args):
    out = [jax.ShapeDtypeStruct(shape, jnp.float32) for shape in shapes]
    return pl.pallas_call(
        kernel,
        out_shape=out,
        in_specs=[pl.BlockSpec(memory_space=pltpu.VMEM)] * len(args),
        out_specs=[pl.BlockSpec(memory_space=pltpu.VMEM)] * len(out),
        compiler_params=pltpu.CompilerParams(vmem_limit_bytes=32 * 2**20),
    )(*args)


def swap_cores(value, n_stu, n_que):
    return lax.ppermute(value, AXES, [(i, i ^ 1) for i in range(n_stu * n_que)])


def send_over(value, step, n_stu, n_que, crossed=False):
    pairs = []
    for stu in range(n_stu):
        for que in range(n_que):
            there = (stu, que ^ (2 * step)) if (que % 2 == 0) != crossed else (stu ^ step, que)
            pairs.append((stu * n_que + que, there[0] * n_que + there[1]))
    return lax.ppermute(value, AXES, pairs)


def stages(group, order):
    base = 1
    while base < group:
        width = min(4, group // base)
        yield [base * k for k in order if k < width]
        base *= width


def shards(n_stu, n_que, codes, theta, disc, intercept):
    group = n_stu
    assert n_que == 2 * group
    send = functools.partial(send_over, n_stu=n_stu, n_que=n_que)
    swap = functools.partial(swap_cores, n_stu=n_stu, n_que=n_que)
    size, width = theta.shape
    rows = 2 * group * size
    half = rows // 2
    assert width == LANES // 2 and rows == 2 * LANES
    assert disc.shape == theta.shape and codes.shape == (rows, half)
    core = lax.rem(lax.axis_index("que"), 2)
    peer_theta, peer_disc, peer_icpt = swap(theta), swap(disc), swap(intercept)

    def block(own, own_icpt, peers, peers_icpt):
        icpt = jnp.pad(jnp.stack([own_icpt, peers_icpt]), ((0, 0), (0, width - size))).reshape(1, LANES)
        spare = jnp.zeros((BIAS - 1, LANES), jnp.float32)
        return jnp.concatenate([jnp.concatenate([own, peers], 1), icpt, spare], 0)

    def side(students, questions):
        return jnp.where(core == 0, students, questions)

    mine = [block(side(theta, disc), intercept, side(peer_theta, peer_disc), peer_icpt)]
    other = [block(side(peer_disc, peer_theta), peer_icpt, side(disc, theta), intercept)]
    (code,) = call(arrange_kernel, [(rows, rows)], codes, swap(codes))
    places = [0]
    for steps in stages(group, GATHER_ORDER):
        ours, theirs = jnp.concatenate(mine, 0), jnp.concatenate(other, 0)
        for step in steps:
            crossed = step == max(steps)
            piece = send(theirs if crossed else ours, step, crossed=crossed)
            back = swap(piece)
            mine.append(back if crossed else piece)
            other.append(piece if crossed else back)
        places = places + [step + place for step in steps for place in places]

    def totals(value, order):
        parts = [value]
        for number, steps in enumerate(stages(group, order)):
            if number:
                parts = [functools.reduce(jnp.add, parts)]
            parts = parts + [send(parts[0], step) for step in steps]
        return parts

    sums, left, right, weight, icpt = call(
        functools.partial(gradient_kernel, group, tuple(places), len(mine)),
        [(rows + BIAS, LANES), (rows, LANES), (rows, LANES), (rows, rows), (BIAS, LANES)],
        *mine,
        *other,
        code,
    )
    parts = totals(sums, FIRST_ORDER)
    first, diag, root = call(
        functools.partial(start_kernel, group, len(parts)),
        [(half + BIAS + size, LANES), (half + BIAS, LANES), (rows, LANES)],
        *parts,
        left,
        icpt,
    )
    peer = swap(first)
    (sums,) = call(image_kernel, [(half + BIAS, LANES)], first, peer, left, right, weight)
    parts = totals(sums, SECOND_ORDER)
    second, dots = call(
        functools.partial(second_kernel, group, len(parts)),
        [(half + BIAS, LANES), (8, LANES)],
        *parts,
        first,
        diag,
    )
    peer_second = swap(second)
    devices = n_stu * n_que
    (dots,) = call(form_kernel, [(devices, 1, LANES)], second, peer_second, left, right, weight, dots)
    dots = lax.all_to_all(dots, AXES, 0, 0, tiled=True)
    abilities, discs, icpts = call(
        functools.partial(finish_kernel, group),
        [(size, width), (size, width), (1, size)],
        dots,
        first,
        peer,
        second,
        peer_second,
        root,
    )
    return abilities, discs, icpts[0]


def solution(mesh):
    placed = (P("stu", "que"), P(("stu", "que"), None), P(("que", "stu"), None), P(("que", "stu")))
    return jax.shard_map(
        functools.partial(shards, mesh.shape["stu"], mesh.shape["que"]),
        mesh=mesh,
        in_specs=placed,
        out_specs=(P(("stu", "que"), None), P(("que", "stu"), None), P(("que", "stu"))),
        check_vma=False,
    )
```

```python
import functools

import jax
import jax.numpy as jnp
from jax import lax
from jax.experimental import pallas as pl
from jax.experimental.pallas import tpu as pltpu
from jax.sharding import PartitionSpec as P

AXES = ("stu", "que")
LANES = 128
GATHER_ORDER = (1, 3, 2)
FIRST_ORDER = (3, 1, 2)
SECOND_ORDER = (1, 2, 3)
BIAS = 8


def halves(value):
    high = value.astype(jnp.bfloat16)
    return high, (value - high.astype(jnp.float32)).astype(jnp.bfloat16)


def product(left, right, dims):
    return lax.dot_general(left, right, (dims, ((), ())), preferred_element_type=jnp.float32)


def dot_nt(left, right):
    left_high, left_low = halves(left)
    right_high, right_low = halves(right)
    dims = ((1,), (1,))
    both = product(
        jnp.concatenate([left_high, left_low], 1), jnp.concatenate([right_high, right_high], 1), dims
    )
    return both + product(left_high, right_low, dims)


def dot_nn(left, right):
    left_high, left_low = halves(left)
    right_high, right_low = halves(right)
    dims = ((1,), (0,))
    both = product(left_high, jnp.concatenate([right_high, right_low], 1), dims)
    width = right.shape[1]
    return both[:, :width] + both[:, width:] + product(left_low, right_high, dims)


def position():
    que = lax.axis_index("que")
    return lax.rem(que, 2), que // 2, lax.axis_index("stu")


def block_of(side, core, line, plane, group):
    return jnp.where(side == 0, line * 2 + core, core * group + plane)


def low_lanes(shape):
    return lax.broadcasted_iota(jnp.int32, shape, 1) < LANES // 2


def turn(value):
    return pltpu.roll(value, LANES // 2, 1)


def pack(value):
    half = value.shape[0] // 2
    low = low_lanes((half, LANES))
    return jnp.where(low, value[:half], turn(value[half:]))


def bias_rows(lanes):
    return jnp.concatenate([lanes[:, :LANES], lanes[:, LANES:]], 0)


def bias_lanes(rows):
    return jnp.concatenate([rows[0:1], rows[1:2]], 1)


def column(rows):
    wide = jnp.concatenate([rows, jnp.zeros((LANES - 2, LANES), jnp.float32)], 0)
    tall = wide.T
    return jnp.concatenate([tall[:, 0:1], tall[:, 1:2]], 0)


def arrange_kernel(own_ref, peer_ref, out_ref):
    core, _, _ = position()
    cols = own_ref.shape[1]

    @pl.when(core == 0)
    def _():
        out_ref[:, :cols] = own_ref[...].astype(jnp.float32)
        out_ref[:, cols:] = peer_ref[...].astype(jnp.float32)

    @pl.when(core == 1)
    def _():
        out_ref[:cols, :] = peer_ref[...].astype(jnp.float32).T
        out_ref[cols:, :] = own_ref[...].astype(jnp.float32).T


def pieces(refs, size):
    step = size + BIAS
    return [ref[first : first + step, :] for ref in refs for first in range(0, ref.shape[0], step)]


def place(blocks, dst_ref, side, columns, core, line, plane, group):
    size = dst_ref.shape[0] // (2 * group)
    lane = lax.broadcasted_iota(jnp.int32, (size, LANES), 1)
    half = LANES // 2
    for at, (k, block) in enumerate(blocks):
        for j in range(2):
            value = turn(block[:size]) if j else block[:size]
            last = jnp.where(side == 0, 1.0, columns[j * half : j * half + size, at : at + 1])
            row = block_of(side, core ^ j, line ^ k, plane ^ k, group) * size
            dst_ref[pl.ds(pl.multiple_of(row, size), size), :] = jnp.where(
                lane < half, value, jnp.where(lane == half, last, 0.0)
            )


def gradient_kernel(group, places, parts, *refs):
    code_ref, sums_ref, left_ref, right_ref, weight_ref, icpt_ref = refs[2 * parts :]
    core, line, plane = position()
    size = left_ref.shape[0] // (2 * group)
    mine = pieces(refs[:parts], size)
    other = pieces(refs[parts : 2 * parts], size)
    rows = [jnp.where(core == 0, there[size : size + 1], here[size : size + 1]) for here, there in zip(mine, other)]
    columns = jnp.concatenate(rows + [jnp.zeros((LANES - group, LANES), jnp.float32)], 0).T
    place(list(zip(places, mine)), left_ref, core, columns, core, line, plane, group)
    place(list(zip(places, other)), right_ref, 1 - core, columns, 1 - core, line, plane, group)
    left = left_ref[...]
    right = right_ref[...]
    prob = 1.0 / (1.0 + jnp.exp(-dot_nt(left, right)))
    code = code_ref[...]
    seen = code > 0.0
    resid = jnp.where(seen, prob - jnp.where(code == 2.0, 1.0, 0.0), 0.0)
    weight = jnp.where(seen, prob * (1.0 - prob), 0.0)
    weight_ref[...] = weight
    rows = left.shape[0]
    grad = dot_nn(resid, right)
    diag = dot_nn(weight, right * right)
    sums_ref[:rows, :] = jnp.where(low_lanes((rows, LANES)), grad, turn(diag))
    at = LANES // 2

    @pl.when(core == 0)
    def _():
        sums_ref[rows:, :] = jnp.zeros((BIAS, LANES), jnp.float32)
        icpt_ref[...] = jnp.zeros((BIAS, LANES), jnp.float32)

    @pl.when(core == 1)
    def _():
        lane = lax.broadcasted_iota(jnp.int32, (rows, LANES), 1)
        moved = jnp.where(lane == at + 1, pltpu.roll(diag, 1, 1), pltpu.roll(left, 2, 1))
        lanes = jnp.where(lane == at, grad, moved).T
        spare = jnp.zeros((BIAS - 4, LANES), jnp.float32)
        sums_ref[rows:, :] = jnp.concatenate([bias_rows(lanes[at : at + 1]), bias_rows(lanes[at + 1 : at + 2]), spare], 0)
        spare = jnp.zeros((BIAS - 2, LANES), jnp.float32)
        icpt_ref[...] = jnp.concatenate([bias_rows(lanes[at + 2 : at + 3]), spare], 0)


def start_kernel(group, parts, *refs):
    sum_refs, (left_ref, icpt_ref, send_ref, diag_ref, root_ref) = refs[:parts], refs[parts:]
    core, line, plane = position()
    total = sum_refs[0][...]
    for ref in sum_refs[1:]:
        total = total + ref[...]
    rows = left_ref.shape[0]
    half = rows // 2
    low = low_lanes((rows, LANES))
    main = total[:rows]
    diag = jnp.where(low, turn(main) + 1.0, 1.0)
    first = jnp.where(low, -(main + left_ref[...]) / diag, 0.0)
    grad_b = total[rows : rows + 2] + icpt_ref[:2]
    diag_b = total[rows + 2 : rows + 4] + 1.0
    first_b = -grad_b / diag_b
    root_ref[...] = jnp.sqrt(diag)
    send_ref[:half, :] = pack(first)
    send_ref[half : half + BIAS, :] = jnp.concatenate(
        [first_b, jnp.sqrt(diag_b), jnp.zeros((BIAS - 4, LANES), jnp.float32)], 0
    )
    diag_ref[:half, :] = pack(diag)
    diag_ref[half:, :] = jnp.concatenate([diag_b, jnp.ones((BIAS - 2, LANES), jnp.float32)], 0)
    size = rows // (2 * group)
    at = block_of(core, 1 - core, line, plane, group) * size
    send_ref[half + BIAS :, :] = root_ref[pl.ds(pl.multiple_of(at, size), size), :]


def change_of(mine_ref, other_ref, left, right, half):
    low = low_lanes((half, LANES))
    mine = mine_ref[:half, :]
    other = other_ref[:half, :]
    lhs = jnp.concatenate(
        [
            jnp.where(low, mine, turn(left[:half])),
            jnp.where(low, turn(mine), turn(left[half:])),
        ],
        0,
    )
    rhs = jnp.concatenate(
        [
            jnp.where(low, right[:half], turn(other)),
            jnp.where(low, right[half:], other),
        ],
        0,
    )
    return dot_nt(lhs, rhs)


def with_bias(change, mine_ref, other_ref, half, use):
    core, _, _ = position()

    @pl.when(core == 0)
    def _():
        use(change + bias_lanes(other_ref[half : half + 2, :]))

    @pl.when(core == 1)
    def _():
        use(change + column(mine_ref[half : half + 2, :]))


def image_kernel(mine_ref, other_ref, left_ref, right_ref, weight_ref, sums_ref):
    core, _, _ = position()
    half = left_ref.shape[0] // 2
    right = right_ref[...]
    change = change_of(mine_ref, other_ref, left_ref[...], right, half)
    at = LANES // 2

    def use(value):
        sums = dot_nn(weight_ref[...] * value, right)
        sums_ref[:half, :] = pack(sums)
        sums_ref[half:, :] = jnp.zeros((BIAS, LANES), jnp.float32)

        @pl.when(core == 1)
        def _():
            sums_ref[half : half + 2, :] = bias_rows(sums.T[at : at + 1])

    with_bias(change, mine_ref, other_ref, half, use)


def second_kernel(group, parts, *refs):
    sum_refs, (send_ref, diag_ref, second_ref, dots_ref) = refs[:parts], refs[parts:]
    total = sum_refs[0][...]
    for ref in sum_refs[1:]:
        total = total + ref[...]
    half = total.shape[0] - BIAS
    row = lax.broadcasted_iota(jnp.int32, total.shape, 0)
    used = row < half + 2
    first = jnp.where(used, send_ref[: half + BIAS, :], 0.0)
    diag = diag_ref[...]
    lift = jnp.where(used, total + first - diag * first, 0.0)
    second = lift / diag
    second_ref[...] = second
    terms = (first * first * diag, first * lift, second * lift, second * second)
    dots_ref[...] = jnp.concatenate(
        [jnp.sum(term, axis=0, keepdims=True) for term in terms] + [jnp.zeros((8 - len(terms), LANES), jnp.float32)], 0
    ) * (1.0 / group)


def form_kernel(mine_ref, other_ref, left_ref, right_ref, weight_ref, dots_ref, out_ref):
    half = left_ref.shape[0] // 2
    change = change_of(mine_ref, other_ref, left_ref[...], right_ref[...], half)

    def use(value):
        form = 0.5 * jnp.sum(weight_ref[...] * value * value, axis=0, keepdims=True)
        row = lax.broadcasted_iota(jnp.int32, (8, LANES), 0)
        terms = dots_ref[...] + jnp.where(row == 3, form[:, :LANES] + form[:, LANES:], 0.0)
        sums = jnp.sum(terms, axis=1, keepdims=True)
        lane = lax.broadcasted_iota(jnp.int32, (8, LANES), 1)
        dots = jnp.sum(jnp.where(lane == row, sums, 0.0), axis=0, keepdims=True)
        out_ref[...] = jnp.broadcast_to(dots[None], out_ref.shape)

    with_bias(change, mine_ref, other_ref, half, use)


def finish_kernel(
    group, dots_ref, send_ref, peer_ref, second_ref, peer_second_ref, root_ref, theta_ref, disc_ref, icpt_ref
):
    core, line, plane = position()
    dots = jnp.sum(dots_ref[...], axis=0)
    lane = lax.broadcasted_iota(jnp.int32, (8, LANES), 1)
    row = lax.broadcasted_iota(jnp.int32, (8, LANES), 0)
    sums = jnp.sum(jnp.where(lane == row, dots, 0.0), axis=1, keepdims=True)
    a, f, h, d = [sums[at : at + 1] for at in range(4)]
    b = a + f
    e = f + h
    det = b * d - e * e
    s = (a * d - e * f) / det
    t = (f * f - a * h) / det
    rows = root_ref.shape[0]
    half = rows // 2
    size = rows // (2 * group)

    def direction(first_ref, next_ref, at):
        upper = at // group
        rows_at = pl.ds(pl.multiple_of(lax.rem(at, group) * size, size), size)
        value = s * first_ref[rows_at, :] + t * next_ref[rows_at, :]
        return jnp.where(upper == 1, turn(value), value)

    mine_at = block_of(core, core, line, plane, group)
    other_at = block_of(1 - core, core, line, plane, group)
    mine = direction(send_ref, second_ref, mine_at)
    mine = mine * root_ref[pl.ds(pl.multiple_of(mine_at * size, size), size), :]
    other = direction(peer_ref, peer_second_ref, other_at) * peer_ref[half + BIAS :, :]
    theta_ref[...] = jnp.where(core == 0, mine, other)[:, : LANES // 2]
    disc_ref[...] = jnp.where(core == 0, other, mine)[:, : LANES // 2]
    ask = jnp.where(core == 0, peer_ref[half : half + BIAS, :], send_ref[half : half + BIAS, :])
    ask_next = jnp.where(core == 0, peer_second_ref[half : half + 2, :], second_ref[half : half + 2, :])
    bias = (s * ask[0:2] + t * ask_next) * ask[2:4]
    disc_at = jnp.where(core == 0, other_at, mine_at)
    row = jnp.where(disc_at // group == 1, bias[1:2], bias[0:1])
    back = lax.rem(LANES - lax.rem(disc_at, group) * size, LANES)
    icpt_ref[...] = pltpu.roll(row, back, 1)[:, :size]


def call(kernel, shapes, *args):
    out = [jax.ShapeDtypeStruct(shape, jnp.float32) for shape in shapes]
    return pl.pallas_call(
        kernel,
        out_shape=out,
        in_specs=[pl.BlockSpec(memory_space=pltpu.VMEM)] * len(args),
        out_specs=[pl.BlockSpec(memory_space=pltpu.VMEM)] * len(out),
        compiler_params=pltpu.CompilerParams(vmem_limit_bytes=32 * 2**20),
    )(*args)


def swap_cores(value, n_stu, n_que):
    return lax.ppermute(value, AXES, [(i, i ^ 1) for i in range(n_stu * n_que)])


def send_over(value, step, n_stu, n_que, crossed=False):
    pairs = []
    for stu in range(n_stu):
        for que in range(n_que):
            there = (stu, que ^ (2 * step)) if (que % 2 == 0) != crossed else (stu ^ step, que)
            pairs.append((stu * n_que + que, there[0] * n_que + there[1]))
    return lax.ppermute(value, AXES, pairs)


def stages(group, order):
    base = 1
    while base < group:
        width = min(4, group // base)
        yield [base * k for k in order if k < width]
        base *= width


def shards(n_stu, n_que, codes, theta, disc, intercept):
    group = n_stu
    assert n_que == 2 * group
    send = functools.partial(send_over, n_stu=n_stu, n_que=n_que)
    swap = functools.partial(swap_cores, n_stu=n_stu, n_que=n_que)
    size, width = theta.shape
    rows = 2 * group * size
    half = rows // 2
    assert width == LANES // 2 and rows == 2 * LANES
    assert disc.shape == theta.shape and codes.shape == (rows, half)
    core = lax.rem(lax.axis_index("que"), 2)
    peer_theta, peer_disc, peer_icpt = swap(theta), swap(disc), swap(intercept)

    def block(own, own_icpt, peers, peers_icpt):
        icpt = jnp.pad(jnp.stack([own_icpt, peers_icpt]), ((0, 0), (0, width - size))).reshape(1, LANES)
        spare = jnp.zeros((BIAS - 1, LANES), jnp.float32)
        return jnp.concatenate([jnp.concatenate([own, peers], 1), icpt, spare], 0)

    def side(students, questions):
        return jnp.where(core == 0, students, questions)

    mine = [block(side(theta, disc), intercept, side(peer_theta, peer_disc), peer_icpt)]
    other = [block(side(peer_disc, peer_theta), peer_icpt, side(disc, theta), intercept)]
    (code,) = call(arrange_kernel, [(rows, rows)], codes, swap(codes))
    places = [0]
    for steps in stages(group, GATHER_ORDER):
        ours, theirs = jnp.concatenate(mine, 0), jnp.concatenate(other, 0)
        for step in steps:
            crossed = step == max(steps)
            piece = send(theirs if crossed else ours, step, crossed=crossed)
            back = swap(piece)
            mine.append(back if crossed else piece)
            other.append(piece if crossed else back)
        places = places + [step + place for step in steps for place in places]

    def totals(value, order):
        parts = [value]
        for number, steps in enumerate(stages(group, order)):
            if number:
                parts = [functools.reduce(jnp.add, parts)]
            parts = parts + [send(parts[0], step) for step in steps]
        return parts

    sums, left, right, weight, icpt = call(
        functools.partial(gradient_kernel, group, tuple(places), len(mine)),
        [(rows + BIAS, LANES), (rows, LANES), (rows, LANES), (rows, rows), (BIAS, LANES)],
        *mine,
        *other,
        code,
    )
    parts = totals(sums, FIRST_ORDER)
    first, diag, root = call(
        functools.partial(start_kernel, group, len(parts)),
        [(half + BIAS + size, LANES), (half + BIAS, LANES), (rows, LANES)],
        *parts,
        left,
        icpt,
    )
    peer = swap(first)
    (sums,) = call(image_kernel, [(half + BIAS, LANES)], first, peer, left, right, weight)
    parts = totals(sums, SECOND_ORDER)
    second, dots = call(
        functools.partial(second_kernel, group, len(parts)),
        [(half + BIAS, LANES), (8, LANES)],
        *parts,
        first,
        diag,
    )
    peer_second = swap(second)
    devices = n_stu * n_que
    (dots,) = call(form_kernel, [(devices, 1, LANES)], second, peer_second, left, right, weight, dots)
    dots = lax.all_to_all(dots, AXES, 0, 0, tiled=True)
    abilities, discs, icpts = call(
        functools.partial(finish_kernel, group),
        [(size, width), (size, width), (1, size)],
        dots,
        first,
        peer,
        second,
        peer_second,
        root,
    )
    return abilities, discs, icpts[0]


def solution(mesh):
    placed = (P("stu", "que"), P(("stu", "que"), None), P(("que", "stu"), None), P(("que", "stu")))
    return jax.shard_map(
        functools.partial(shards, mesh.shape["stu"], mesh.shape["que"]),
        mesh=mesh,
        in_specs=placed,
        out_specs=(P(("stu", "que"), None), P(("que", "stu"), None), P(("que", "stu"))),
        check_vma=False,
    )
```

```python
import functools

import jax
import jax.numpy as jnp
from jax import lax
from jax.experimental import pallas as pl
from jax.experimental.pallas import tpu as pltpu
from jax.sharding import PartitionSpec as P

AXES = ("stu", "que")
LANES = 128
GATHER_ORDER = (1, 3, 2)
FIRST_ORDER = (3, 1, 2)
SECOND_ORDER = (1, 2, 3)
BIAS = 8


def halves(value):
    high = value.astype(jnp.bfloat16)
    return high, (value - high.astype(jnp.float32)).astype(jnp.bfloat16)


def product(left, right, dims):
    return lax.dot_general(left, right, (dims, ((), ())), preferred_element_type=jnp.float32)


def dot_nt(left, right):
    left_high, left_low = halves(left)
    right_high, right_low = halves(right)
    dims = ((1,), (1,))
    both = product(
        jnp.concatenate([left_high, left_low], 1), jnp.concatenate([right_high, right_high], 1), dims
    )
    return both + product(left_high, right_low, dims)


def dot_nn(left, right):
    left_high, left_low = halves(left)
    right_high, right_low = halves(right)
    dims = ((1,), (0,))
    both = product(left_high, jnp.concatenate([right_high, right_low], 1), dims)
    width = right.shape[1]
    return both[:, :width] + both[:, width:] + product(left_low, right_high, dims)


def position():
    que = lax.axis_index("que")
    return lax.rem(que, 2), que // 2, lax.axis_index("stu")


def block_of(side, core, line, plane, group):
    return jnp.where(side == 0, line * 2 + core, core * group + plane)


def low_lanes(shape):
    return lax.broadcasted_iota(jnp.int32, shape, 1) < LANES // 2


def turn(value):
    return pltpu.roll(value, LANES // 2, 1)


def pack(value):
    half = value.shape[0] // 2
    low = low_lanes((half, LANES))
    return jnp.where(low, value[:half], turn(value[half:]))


def bias_rows(lanes):
    return jnp.concatenate([lanes[:, :LANES], lanes[:, LANES:]], 0)


def bias_lanes(rows):
    return jnp.concatenate([rows[0:1], rows[1:2]], 1)


def column(rows):
    tall = jnp.concatenate([rows, jnp.zeros((BIAS - 2, LANES), jnp.float32)], 0).T
    return jnp.concatenate([tall[:, 0:1], tall[:, 1:2]], 0)


def arrange_kernel(own_ref, peer_ref, out_ref):
    core, _, _ = position()
    cols = own_ref.shape[1]

    @pl.when(core == 0)
    def _():
        out_ref[:, :cols] = own_ref[...].astype(jnp.float32)
        out_ref[:, cols:] = peer_ref[...].astype(jnp.float32)

    @pl.when(core == 1)
    def _():
        out_ref[:cols, :] = peer_ref[...].astype(jnp.float32).T
        out_ref[cols:, :] = own_ref[...].astype(jnp.float32).T


def pieces(refs, size):
    step = size + BIAS
    return [ref[first : first + step, :] for ref in refs for first in range(0, ref.shape[0], step)]


def place(blocks, dst_ref, side, columns, core, line, plane, group):
    size = dst_ref.shape[0] // (2 * group)
    lane = lax.broadcasted_iota(jnp.int32, (size, LANES), 1)
    half = LANES // 2
    for at, (k, block) in enumerate(blocks):
        for j in range(2):
            value = turn(block[:size]) if j else block[:size]
            last = jnp.where(side == 0, 1.0, columns[j * half : j * half + size, at : at + 1])
            row = block_of(side, core ^ j, line ^ k, plane ^ k, group) * size
            dst_ref[pl.ds(pl.multiple_of(row, size), size), :] = jnp.where(
                lane < half, value, jnp.where(lane == half, last, 0.0)
            )


def gradient_kernel(group, places, parts, *refs):
    code_ref, sums_ref, left_ref, right_ref, weight_ref, icpt_ref = refs[2 * parts :]
    core, line, plane = position()
    size = left_ref.shape[0] // (2 * group)
    mine = pieces(refs[:parts], size)
    other = pieces(refs[parts : 2 * parts], size)
    rows = [jnp.where(core == 0, there[size : size + 1], here[size : size + 1]) for here, there in zip(mine, other)]
    columns = jnp.concatenate(rows + [jnp.zeros((-group % BIAS, LANES), jnp.float32)] * (group % BIAS > 0), 0).T
    place(list(zip(places, mine)), left_ref, core, columns, core, line, plane, group)
    place(list(zip(places, other)), right_ref, 1 - core, columns, 1 - core, line, plane, group)
    left = left_ref[...]
    right = right_ref[...]
    prob = 1.0 / (1.0 + jnp.exp(-dot_nt(left, right)))
    code = code_ref[...]
    seen = code > 0.0
    resid = jnp.where(seen, prob - jnp.where(code == 2.0, 1.0, 0.0), 0.0)
    weight = jnp.where(seen, prob * (1.0 - prob), 0.0)
    weight_ref[...] = weight
    rows = left.shape[0]
    grad = dot_nn(resid, right)
    diag = dot_nn(weight, right * right)
    sums_ref[:rows, :] = jnp.where(low_lanes((rows, LANES)), grad, turn(diag))
    at = LANES // 2

    @pl.when(core == 0)
    def _():
        sums_ref[rows:, :] = jnp.zeros((BIAS, LANES), jnp.float32)
        icpt_ref[...] = jnp.zeros((BIAS, LANES), jnp.float32)

    @pl.when(core == 1)
    def _():
        lane = lax.broadcasted_iota(jnp.int32, (rows, LANES), 1)
        moved = jnp.where(lane == at + 1, pltpu.roll(diag, 1, 1), pltpu.roll(left, 2, 1))
        lanes = jnp.where(lane == at, grad, moved).T
        spare = jnp.zeros((BIAS - 4, LANES), jnp.float32)
        sums_ref[rows:, :] = jnp.concatenate([bias_rows(lanes[at : at + 1]), bias_rows(lanes[at + 1 : at + 2]), spare], 0)
        spare = jnp.zeros((BIAS - 2, LANES), jnp.float32)
        icpt_ref[...] = jnp.concatenate([bias_rows(lanes[at + 2 : at + 3]), spare], 0)


def start_kernel(group, parts, *refs):
    sum_refs, (left_ref, icpt_ref, send_ref, diag_ref, whole_ref) = refs[:parts], refs[parts:]
    core, line, plane = position()
    total = sum_refs[0][...]
    for ref in sum_refs[1:]:
        total = total + ref[...]
    rows = left_ref.shape[0]
    half = rows // 2
    low = low_lanes((rows, LANES))
    main = total[:rows]
    diag = jnp.where(low, turn(main) + 1.0, 1.0)
    first = jnp.where(low, -(main + left_ref[...]) / diag, 0.0)
    grad_b = total[rows : rows + 2] + icpt_ref[:2]
    diag_b = total[rows + 2 : rows + 4] + 1.0
    first_b = -grad_b / diag_b
    whole_ref[...] = diag
    send_ref[:half, :] = pack(first)
    send_ref[half : half + BIAS, :] = jnp.concatenate(
        [first_b, diag_b, jnp.zeros((BIAS - 4, LANES), jnp.float32)], 0
    )
    diag_ref[:half, :] = pack(diag)
    diag_ref[half:, :] = jnp.concatenate([diag_b, jnp.ones((BIAS - 2, LANES), jnp.float32)], 0)
    size = rows // (2 * group)
    at = block_of(core, 1 - core, line, plane, group) * size
    send_ref[half + BIAS :, :] = whole_ref[pl.ds(pl.multiple_of(at, size), size), :]


def change_of(mine_ref, other_ref, left, right, half):
    low = low_lanes((half, LANES))
    mine = mine_ref[:half, :]
    other = other_ref[:half, :]
    lhs = jnp.concatenate(
        [
            jnp.where(low, mine, turn(left[:half])),
            jnp.where(low, turn(mine), turn(left[half:])),
        ],
        0,
    )
    rhs = jnp.concatenate(
        [
            jnp.where(low, right[:half], turn(other)),
            jnp.where(low, right[half:], other),
        ],
        0,
    )
    return dot_nt(lhs, rhs)


def with_bias(change, mine_ref, other_ref, half, use):
    core, _, _ = position()

    @pl.when(core == 0)
    def _():
        use(change + bias_lanes(other_ref[half : half + 2, :]))

    @pl.when(core == 1)
    def _():
        use(change + column(mine_ref[half : half + 2, :]))


def image_kernel(mine_ref, other_ref, left_ref, right_ref, weight_ref, sums_ref):
    core, _, _ = position()
    half = left_ref.shape[0] // 2
    right = right_ref[...]
    change = change_of(mine_ref, other_ref, left_ref[...], right, half)
    at = LANES // 2

    def use(value):
        sums = dot_nn(weight_ref[...] * value, right)
        sums_ref[:half, :] = pack(sums)
        sums_ref[half:, :] = jnp.zeros((BIAS, LANES), jnp.float32)

        @pl.when(core == 1)
        def _():
            sums_ref[half : half + 2, :] = bias_rows(sums.T[at : at + 1])

    with_bias(change, mine_ref, other_ref, half, use)


def second_kernel(group, parts, *refs):
    sum_refs, (send_ref, diag_ref, second_ref, dots_ref) = refs[:parts], refs[parts:]
    total = sum_refs[0][...]
    for ref in sum_refs[1:]:
        total = total + ref[...]
    half = total.shape[0] - BIAS
    row = lax.broadcasted_iota(jnp.int32, total.shape, 0)
    used = row < half + 2
    first = jnp.where(used, send_ref[: half + BIAS, :], 0.0)
    diag = diag_ref[...]
    lift = jnp.where(used, total + first - diag * first, 0.0)
    second = lift / diag
    second_ref[...] = second
    terms = (first * first * diag, first * lift, second * lift, second * second)
    dots_ref[...] = jnp.concatenate(
        [jnp.sum(term, axis=0, keepdims=True) for term in terms] + [jnp.zeros((8 - len(terms), LANES), jnp.float32)], 0
    ) * (1.0 / group)


def form_kernel(mine_ref, other_ref, left_ref, right_ref, weight_ref, dots_ref, out_ref):
    half = left_ref.shape[0] // 2
    change = change_of(mine_ref, other_ref, left_ref[...], right_ref[...], half)

    def use(value):
        form = 0.5 * jnp.sum(weight_ref[...] * value * value, axis=0, keepdims=True)
        row = lax.broadcasted_iota(jnp.int32, (8, LANES), 0)
        terms = dots_ref[...] + jnp.where(row == 3, form[:, :LANES] + form[:, LANES:], 0.0)
        sums = jnp.sum(terms, axis=1, keepdims=True)
        lane = lax.broadcasted_iota(jnp.int32, (8, LANES), 1)
        dots = jnp.sum(jnp.where(lane == row, sums, 0.0), axis=0, keepdims=True)
        out_ref[...] = jnp.broadcast_to(dots[None], out_ref.shape)

    with_bias(change, mine_ref, other_ref, half, use)


def finish_kernel(
    group, dots_ref, send_ref, peer_ref, second_ref, peer_second_ref, whole_ref, theta_ref, disc_ref, icpt_ref
):
    core, line, plane = position()
    dots = jnp.sum(dots_ref[...], axis=0)
    lane = lax.broadcasted_iota(jnp.int32, (8, LANES), 1)
    row = lax.broadcasted_iota(jnp.int32, (8, LANES), 0)
    sums = jnp.sum(jnp.where(lane == row, dots, 0.0), axis=1, keepdims=True)
    a, f, h, d = [sums[at : at + 1] for at in range(4)]
    b = a + f
    e = f + h
    det = b * d - e * e
    s = (a * d - e * f) / det
    t = (f * f - a * h) / det
    rows = whole_ref.shape[0]
    half = rows // 2
    size = rows // (2 * group)

    def direction(first_ref, next_ref, at):
        upper = at // group
        rows_at = pl.ds(pl.multiple_of(lax.rem(at, group) * size, size), size)
        value = s * first_ref[rows_at, :] + t * next_ref[rows_at, :]
        return jnp.where(upper == 1, turn(value), value)

    mine_at = block_of(core, core, line, plane, group)
    other_at = block_of(1 - core, core, line, plane, group)
    mine = direction(send_ref, second_ref, mine_at)
    mine = mine * jnp.sqrt(whole_ref[pl.ds(pl.multiple_of(mine_at * size, size), size), :])
    other = direction(peer_ref, peer_second_ref, other_at) * jnp.sqrt(peer_ref[half + BIAS :, :])
    theta_ref[...] = jnp.where(core == 0, mine, other)[:, : LANES // 2]
    disc_ref[...] = jnp.where(core == 0, other, mine)[:, : LANES // 2]
    ask = jnp.where(core == 0, peer_ref[half : half + BIAS, :], send_ref[half : half + BIAS, :])
    ask_next = jnp.where(core == 0, peer_second_ref[half : half + 2, :], second_ref[half : half + 2, :])
    bias = (s * ask[0:2] + t * ask_next) * jnp.sqrt(ask[2:4])
    disc_at = jnp.where(core == 0, other_at, mine_at)
    row = jnp.where(disc_at // group == 1, bias[1:2], bias[0:1])
    back = lax.rem(LANES - lax.rem(disc_at, group) * size, LANES)
    icpt_ref[...] = pltpu.roll(row, back, 1)[:, :size]


def call(kernel, shapes, *args):
    out = [jax.ShapeDtypeStruct(shape, jnp.float32) for shape in shapes]
    return pl.pallas_call(
        kernel,
        out_shape=out,
        in_specs=[pl.BlockSpec(memory_space=pltpu.VMEM)] * len(args),
        out_specs=[pl.BlockSpec(memory_space=pltpu.VMEM)] * len(out),
        compiler_params=pltpu.CompilerParams(vmem_limit_bytes=32 * 2**20),
    )(*args)


def swap_cores(value, n_stu, n_que):
    return lax.ppermute(value, AXES, [(i, i ^ 1) for i in range(n_stu * n_que)])


def send_over(value, step, n_stu, n_que, crossed=False):
    pairs = []
    for stu in range(n_stu):
        for que in range(n_que):
            there = (stu, que ^ (2 * step)) if (que % 2 == 0) != crossed else (stu ^ step, que)
            pairs.append((stu * n_que + que, there[0] * n_que + there[1]))
    return lax.ppermute(value, AXES, pairs)


def stages(group, order):
    base = 1
    while base < group:
        width = min(4, group // base)
        yield [base * k for k in order if k < width]
        base *= width


def shards(n_stu, n_que, codes, theta, disc, intercept):
    group = n_stu
    assert n_que == 2 * group
    send = functools.partial(send_over, n_stu=n_stu, n_que=n_que)
    swap = functools.partial(swap_cores, n_stu=n_stu, n_que=n_que)
    size, width = theta.shape
    rows = 2 * group * size
    half = rows // 2
    assert width == LANES // 2 and rows == 2 * LANES
    assert disc.shape == theta.shape and codes.shape == (rows, half)
    core = lax.rem(lax.axis_index("que"), 2)
    peer_theta, peer_disc, peer_icpt = swap(theta), swap(disc), swap(intercept)

    def block(own, own_icpt, peers, peers_icpt):
        icpt = jnp.pad(jnp.stack([own_icpt, peers_icpt]), ((0, 0), (0, width - size))).reshape(1, LANES)
        spare = jnp.zeros((BIAS - 1, LANES), jnp.float32)
        return jnp.concatenate([jnp.concatenate([own, peers], 1), icpt, spare], 0)

    def side(students, questions):
        return jnp.where(core == 0, students, questions)

    mine = [block(side(theta, disc), intercept, side(peer_theta, peer_disc), peer_icpt)]
    other = [block(side(peer_disc, peer_theta), peer_icpt, side(disc, theta), intercept)]
    (code,) = call(arrange_kernel, [(rows, rows)], codes, swap(codes))
    places = [0]
    for steps in stages(group, GATHER_ORDER):
        ours, theirs = jnp.concatenate(mine, 0), jnp.concatenate(other, 0)
        for step in steps:
            crossed = step == max(steps)
            piece = send(theirs if crossed else ours, step, crossed=crossed)
            back = swap(piece)
            mine.append(back if crossed else piece)
            other.append(piece if crossed else back)
        places = places + [step + place for step in steps for place in places]

    def totals(value, order):
        parts = [value]
        for number, steps in enumerate(stages(group, order)):
            if number:
                parts = [functools.reduce(jnp.add, parts)]
            parts = parts + [send(parts[0], step) for step in steps]
        return parts

    sums, left, right, weight, icpt = call(
        functools.partial(gradient_kernel, group, tuple(places), len(mine)),
        [(rows + BIAS, LANES), (rows, LANES), (rows, LANES), (rows, rows), (BIAS, LANES)],
        *mine,
        *other,
        code,
    )
    parts = totals(sums, FIRST_ORDER)
    first, diag, whole = call(
        functools.partial(start_kernel, group, len(parts)),
        [(half + BIAS + size, LANES), (half + BIAS, LANES), (rows, LANES)],
        *parts,
        left,
        icpt,
    )
    peer = swap(first)
    (sums,) = call(image_kernel, [(half + BIAS, LANES)], first, peer, left, right, weight)
    parts = totals(sums, SECOND_ORDER)
    second, dots = call(
        functools.partial(second_kernel, group, len(parts)),
        [(half + BIAS, LANES), (8, LANES)],
        *parts,
        first,
        diag,
    )
    peer_second = swap(second)
    devices = n_stu * n_que
    (dots,) = call(form_kernel, [(devices, 1, LANES)], second, peer_second, left, right, weight, dots)
    dots = lax.all_to_all(dots, AXES, 0, 0, tiled=True)
    abilities, discs, icpts = call(
        functools.partial(finish_kernel, group),
        [(size, width), (size, width), (1, size)],
        dots,
        first,
        peer,
        second,
        peer_second,
        whole,
    )
    return abilities, discs, icpts[0]


def solution(mesh):
    placed = (P("stu", "que"), P(("stu", "que"), None), P(("que", "stu"), None), P(("que", "stu")))
    return jax.shard_map(
        functools.partial(shards, mesh.shape["stu"], mesh.shape["que"]),
        mesh=mesh,
        in_specs=placed,
        out_specs=(P(("stu", "que"), None), P(("que", "stu"), None), P(("que", "stu"))),
        check_vma=False,
    )
```

```python
import functools

import jax
import jax.numpy as jnp
from jax import lax
from jax.experimental import pallas as pl
from jax.experimental.pallas import tpu as pltpu
from jax.sharding import PartitionSpec as P

AXES = ("stu", "que")
LANES = 128
GATHER_ORDER = (1, 3, 2)
FIRST_ORDER = (3, 1, 2)
SECOND_ORDER = (1, 2, 3)
BIAS = 8


def halves(value):
    high = value.astype(jnp.bfloat16)
    return high, (value - high.astype(jnp.float32)).astype(jnp.bfloat16)


def product(left, right, dims):
    return lax.dot_general(left, right, (dims, ((), ())), preferred_element_type=jnp.float32)


def dot_nt(left, right):
    left_high, left_low = halves(left)
    right_high, right_low = halves(right)
    dims = ((1,), (1,))
    both = product(
        jnp.concatenate([left_high, left_low], 1), jnp.concatenate([right_high, right_high], 1), dims
    )
    return both + product(left_high, right_low, dims)


def dot_nn(left, right):
    left_high, left_low = halves(left)
    right_high, right_low = halves(right)
    dims = ((1,), (0,))
    both = product(left_high, jnp.concatenate([right_high, right_low], 1), dims)
    width = right.shape[1]
    return both[:, :width] + both[:, width:] + product(left_low, right_high, dims)


def position():
    que = lax.axis_index("que")
    return lax.rem(que, 2), que // 2, lax.axis_index("stu")


def block_of(side, core, line, plane, group):
    return jnp.where(side == 0, line * 2 + core, core * group + plane)


def low_lanes(shape):
    return lax.broadcasted_iota(jnp.int32, shape, 1) < LANES // 2


def turn(value):
    return pltpu.roll(value, LANES // 2, 1)


def pack(value):
    half = value.shape[0] // 2
    low = low_lanes((half, LANES))
    return jnp.where(low, value[:half], turn(value[half:]))


def bias_rows(lanes):
    return jnp.concatenate([lanes[:, :LANES], lanes[:, LANES:]], 0)


def bias_lanes(rows):
    return jnp.concatenate([rows[0:1], rows[1:2]], 1)


def column(rows):
    tall = jnp.concatenate([rows, jnp.zeros((BIAS - 2, LANES), jnp.float32)], 0).T
    return jnp.concatenate([tall[:, 0:1], tall[:, 1:2]], 0)


def arrange_kernel(own_ref, peer_ref, out_ref):
    core, _, _ = position()
    cols = own_ref.shape[1]

    @pl.when(core == 0)
    def _():
        out_ref[:, :cols] = own_ref[...].astype(jnp.float32)
        out_ref[:, cols:] = peer_ref[...].astype(jnp.float32)

    @pl.when(core == 1)
    def _():
        out_ref[:cols, :] = peer_ref[...].astype(jnp.float32).T
        out_ref[cols:, :] = own_ref[...].astype(jnp.float32).T


def pieces(refs, size):
    step = size + BIAS
    return [ref[first : first + step, :] for ref in refs for first in range(0, ref.shape[0], step)]


def place(blocks, dst_ref, side, columns, core, line, plane, group):
    size = dst_ref.shape[0] // (2 * group)
    lane = lax.broadcasted_iota(jnp.int32, (size, LANES), 1)
    half = LANES // 2
    for at, (k, block) in enumerate(blocks):
        for j in range(2):
            value = turn(block[:size]) if j else block[:size]
            last = jnp.where(side == 0, 1.0, columns[j * half : j * half + size, at : at + 1])
            row = block_of(side, core ^ j, line ^ k, plane ^ k, group) * size
            dst_ref[pl.ds(pl.multiple_of(row, size), size), :] = jnp.where(
                lane < half, value, jnp.where(lane == half, last, 0.0)
            )


def gradient_kernel(group, places, parts, *refs):
    code_ref, sums_ref, left_ref, right_ref, weight_ref, icpt_ref = refs[2 * parts :]
    core, line, plane = position()
    size = left_ref.shape[0] // (2 * group)
    mine = pieces(refs[:parts], size)
    other = pieces(refs[parts : 2 * parts], size)
    rows = [jnp.where(core == 0, there[size : size + 1], here[size : size + 1]) for here, there in zip(mine, other)]
    columns = jnp.concatenate(rows + [jnp.zeros((-group % BIAS, LANES), jnp.float32)] * (group % BIAS > 0), 0).T
    place(list(zip(places, mine)), left_ref, core, columns, core, line, plane, group)
    place(list(zip(places, other)), right_ref, 1 - core, columns, 1 - core, line, plane, group)
    left = left_ref[...]
    right = right_ref[...]
    prob = 1.0 / (1.0 + jnp.exp(-dot_nt(left, right)))
    code = code_ref[...]
    seen = code > 0.0
    resid = jnp.where(seen, prob - jnp.where(code == 2.0, 1.0, 0.0), 0.0)
    weight = jnp.where(seen, prob * (1.0 - prob), 0.0)
    weight_ref[...] = weight
    rows = left.shape[0]
    grad = dot_nn(resid, right)
    diag = dot_nn(weight, right * right)
    sums_ref[:rows, :] = jnp.where(low_lanes((rows, LANES)), grad, turn(diag))
    at = LANES // 2

    @pl.when(core == 0)
    def _():
        sums_ref[rows:, :] = jnp.zeros((BIAS, LANES), jnp.float32)
        icpt_ref[...] = jnp.zeros((BIAS, LANES), jnp.float32)

    @pl.when(core == 1)
    def _():
        lane = lax.broadcasted_iota(jnp.int32, (rows, LANES), 1)
        moved = jnp.where(lane == at + 1, pltpu.roll(diag, 1, 1), pltpu.roll(left, 2, 1))
        lanes = jnp.where(lane == at, grad, moved).T
        spare = jnp.zeros((BIAS - 4, LANES), jnp.float32)
        sums_ref[rows:, :] = jnp.concatenate([bias_rows(lanes[at : at + 1]), bias_rows(lanes[at + 1 : at + 2]), spare], 0)
        spare = jnp.zeros((BIAS - 2, LANES), jnp.float32)
        icpt_ref[...] = jnp.concatenate([bias_rows(lanes[at + 2 : at + 3]), spare], 0)


def start_kernel(group, parts, *refs):
    sum_refs, (left_ref, icpt_ref, send_ref, diag_ref, whole_ref) = refs[:parts], refs[parts:]
    core, line, plane = position()
    total = sum_refs[0][...]
    for ref in sum_refs[1:]:
        total = total + ref[...]
    rows = left_ref.shape[0]
    half = rows // 2
    low = low_lanes((rows, LANES))
    main = total[:rows]
    diag = jnp.where(low, turn(main) + 1.0, 1.0)
    first = jnp.where(low, -(main + left_ref[...]) / diag, 0.0)
    grad_b = total[rows : rows + 2] + icpt_ref[:2]
    diag_b = total[rows + 2 : rows + 4] + 1.0
    first_b = -grad_b / diag_b
    whole_ref[...] = diag
    send_ref[:half, :] = pack(first)
    send_ref[half : half + BIAS, :] = jnp.concatenate(
        [first_b, diag_b, jnp.zeros((BIAS - 4, LANES), jnp.float32)], 0
    )
    diag_ref[:half, :] = pack(diag)
    diag_ref[half:, :] = jnp.concatenate([diag_b, jnp.ones((BIAS - 2, LANES), jnp.float32)], 0)
    size = rows // (2 * group)
    at = block_of(core, 1 - core, line, plane, group) * size
    send_ref[half + BIAS :, :] = whole_ref[pl.ds(pl.multiple_of(at, size), size), :]


def change_of(mine_ref, other_ref, left, right, half):
    low = low_lanes((half, LANES))
    mine = mine_ref[:half, :]
    other = other_ref[:half, :]
    lhs = jnp.concatenate(
        [
            jnp.where(low, mine, turn(left[:half])),
            jnp.where(low, turn(mine), turn(left[half:])),
        ],
        0,
    )
    rhs = jnp.concatenate(
        [
            jnp.where(low, right[:half], turn(other)),
            jnp.where(low, right[half:], other),
        ],
        0,
    )
    return dot_nt(lhs, rhs)


def with_bias(change, mine_ref, other_ref, half, use):
    core, _, _ = position()

    @pl.when(core == 0)
    def _():
        use(change + bias_lanes(other_ref[half : half + 2, :]))

    @pl.when(core == 1)
    def _():
        use(change + column(mine_ref[half : half + 2, :]))


def image_kernel(mine_ref, other_ref, left_ref, right_ref, weight_ref, sums_ref):
    core, _, _ = position()
    half = left_ref.shape[0] // 2
    right = right_ref[...]
    change = change_of(mine_ref, other_ref, left_ref[...], right, half)
    at = LANES // 2

    def use(value):
        sums = dot_nn(weight_ref[...] * value, right)
        sums_ref[:half, :] = pack(sums)
        sums_ref[half:, :] = jnp.zeros((BIAS, LANES), jnp.float32)

        @pl.when(core == 1)
        def _():
            sums_ref[half : half + 2, :] = bias_rows(sums.T[at : at + 1])

    with_bias(change, mine_ref, other_ref, half, use)


def second_kernel(group, parts, *refs):
    sum_refs, (send_ref, diag_ref, second_ref, dots_ref) = refs[:parts], refs[parts:]
    total = sum_refs[0][...]
    for ref in sum_refs[1:]:
        total = total + ref[...]
    half = total.shape[0] - BIAS
    row = lax.broadcasted_iota(jnp.int32, total.shape, 0)
    used = row < half + 2
    first = jnp.where(used, send_ref[: half + BIAS, :], 0.0)
    diag = diag_ref[...]
    lift = jnp.where(used, total + first - diag * first, 0.0)
    second = lift / diag
    second_ref[...] = second
    terms = (first * first * diag, first * lift, second * lift, second * second)
    dots_ref[...] = jnp.concatenate(
        [jnp.sum(term, axis=0, keepdims=True) for term in terms] + [jnp.zeros((8 - len(terms), LANES), jnp.float32)], 0
    ) * (1.0 / group)


def form_kernel(mine_ref, other_ref, left_ref, right_ref, weight_ref, dots_ref, out_ref):
    core, _, _ = position()
    half = left_ref.shape[0] // 2

    def give(terms):
        row = lax.broadcasted_iota(jnp.int32, (8, LANES), 0)
        lane = lax.broadcasted_iota(jnp.int32, (8, LANES), 1)
        sums = jnp.sum(terms, axis=1, keepdims=True)
        dots = jnp.sum(jnp.where(lane == row, sums, 0.0), axis=0, keepdims=True)
        out_ref[...] = jnp.broadcast_to(dots[None], out_ref.shape)

    @pl.when(core == 0)
    def _():
        change = change_of(mine_ref, other_ref, left_ref[...], right_ref[...], half)
        change = change + bias_lanes(other_ref[half : half + 2, :])
        form = jnp.sum(weight_ref[...] * change * change, axis=0, keepdims=True)
        row = lax.broadcasted_iota(jnp.int32, (8, LANES), 0)
        give(dots_ref[...] + jnp.where(row == 3, form[:, :LANES] + form[:, LANES:], 0.0))

    @pl.when(core == 1)
    def _():
        give(dots_ref[...])


def finish_kernel(
    group, dots_ref, send_ref, peer_ref, second_ref, peer_second_ref, whole_ref, theta_ref, disc_ref, icpt_ref
):
    core, line, plane = position()
    dots = jnp.sum(dots_ref[...], axis=0)
    lane = lax.broadcasted_iota(jnp.int32, (8, LANES), 1)
    row = lax.broadcasted_iota(jnp.int32, (8, LANES), 0)
    sums = jnp.sum(jnp.where(lane == row, dots, 0.0), axis=1, keepdims=True)
    a, f, h, d = [sums[at : at + 1] for at in range(4)]
    b = a + f
    e = f + h
    det = b * d - e * e
    s = (a * d - e * f) / det
    t = (f * f - a * h) / det
    rows = whole_ref.shape[0]
    half = rows // 2
    size = rows // (2 * group)

    def direction(first_ref, next_ref, at):
        upper = at // group
        rows_at = pl.ds(pl.multiple_of(lax.rem(at, group) * size, size), size)
        value = s * first_ref[rows_at, :] + t * next_ref[rows_at, :]
        return jnp.where(upper == 1, turn(value), value)

    mine_at = block_of(core, core, line, plane, group)
    other_at = block_of(1 - core, core, line, plane, group)
    mine = direction(send_ref, second_ref, mine_at)
    mine = mine * jnp.sqrt(whole_ref[pl.ds(pl.multiple_of(mine_at * size, size), size), :])
    other = direction(peer_ref, peer_second_ref, other_at) * jnp.sqrt(peer_ref[half + BIAS :, :])
    theta_ref[...] = jnp.where(core == 0, mine, other)[:, : LANES // 2]
    disc_ref[...] = jnp.where(core == 0, other, mine)[:, : LANES // 2]
    ask = jnp.where(core == 0, peer_ref[half : half + BIAS, :], send_ref[half : half + BIAS, :])
    ask_next = jnp.where(core == 0, peer_second_ref[half : half + 2, :], second_ref[half : half + 2, :])
    bias = (s * ask[0:2] + t * ask_next) * jnp.sqrt(ask[2:4])
    disc_at = jnp.where(core == 0, other_at, mine_at)
    row = jnp.where(disc_at // group == 1, bias[1:2], bias[0:1])
    back = lax.rem(LANES - lax.rem(disc_at, group) * size, LANES)
    icpt_ref[...] = pltpu.roll(row, back, 1)[:, :size]


def call(kernel, shapes, *args):
    out = [jax.ShapeDtypeStruct(shape, jnp.float32) for shape in shapes]
    return pl.pallas_call(
        kernel,
        out_shape=out,
        in_specs=[pl.BlockSpec(memory_space=pltpu.VMEM)] * len(args),
        out_specs=[pl.BlockSpec(memory_space=pltpu.VMEM)] * len(out),
        compiler_params=pltpu.CompilerParams(vmem_limit_bytes=32 * 2**20),
    )(*args)


def swap_cores(value, n_stu, n_que):
    return lax.ppermute(value, AXES, [(i, i ^ 1) for i in range(n_stu * n_que)])


def send_over(value, step, n_stu, n_que, crossed=False):
    pairs = []
    for stu in range(n_stu):
        for que in range(n_que):
            there = (stu, que ^ (2 * step)) if (que % 2 == 0) != crossed else (stu ^ step, que)
            pairs.append((stu * n_que + que, there[0] * n_que + there[1]))
    return lax.ppermute(value, AXES, pairs)


def stages(group, order):
    base = 1
    while base < group:
        width = min(4, group // base)
        yield [base * k for k in order if k < width]
        base *= width


def shards(n_stu, n_que, codes, theta, disc, intercept):
    group = n_stu
    assert n_que == 2 * group
    send = functools.partial(send_over, n_stu=n_stu, n_que=n_que)
    swap = functools.partial(swap_cores, n_stu=n_stu, n_que=n_que)
    size, width = theta.shape
    rows = 2 * group * size
    half = rows // 2
    assert width == LANES // 2 and rows == 2 * LANES
    assert disc.shape == theta.shape and codes.shape == (rows, half)
    core = lax.rem(lax.axis_index("que"), 2)
    peer_theta, peer_disc, peer_icpt = swap(theta), swap(disc), swap(intercept)

    def block(own, own_icpt, peers, peers_icpt):
        icpt = jnp.pad(jnp.stack([own_icpt, peers_icpt]), ((0, 0), (0, width - size))).reshape(1, LANES)
        spare = jnp.zeros((BIAS - 1, LANES), jnp.float32)
        return jnp.concatenate([jnp.concatenate([own, peers], 1), icpt, spare], 0)

    def side(students, questions):
        return jnp.where(core == 0, students, questions)

    mine = [block(side(theta, disc), intercept, side(peer_theta, peer_disc), peer_icpt)]
    other = [block(side(peer_disc, peer_theta), peer_icpt, side(disc, theta), intercept)]
    (code,) = call(arrange_kernel, [(rows, rows)], codes, swap(codes))
    places = [0]
    for steps in stages(group, GATHER_ORDER):
        ours, theirs = jnp.concatenate(mine, 0), jnp.concatenate(other, 0)
        for step in steps:
            crossed = step == max(steps)
            piece = send(theirs if crossed else ours, step, crossed=crossed)
            back = swap(piece)
            mine.append(back if crossed else piece)
            other.append(piece if crossed else back)
        places = places + [step + place for step in steps for place in places]

    def totals(value, order):
        parts = [value]
        for number, steps in enumerate(stages(group, order)):
            if number:
                parts = [functools.reduce(jnp.add, parts)]
            parts = parts + [send(parts[0], step) for step in steps]
        return parts

    sums, left, right, weight, icpt = call(
        functools.partial(gradient_kernel, group, tuple(places), len(mine)),
        [(rows + BIAS, LANES), (rows, LANES), (rows, LANES), (rows, rows), (BIAS, LANES)],
        *mine,
        *other,
        code,
    )
    parts = totals(sums, FIRST_ORDER)
    first, diag, whole = call(
        functools.partial(start_kernel, group, len(parts)),
        [(half + BIAS + size, LANES), (half + BIAS, LANES), (rows, LANES)],
        *parts,
        left,
        icpt,
    )
    peer = swap(first)
    (sums,) = call(image_kernel, [(half + BIAS, LANES)], first, peer, left, right, weight)
    parts = totals(sums, SECOND_ORDER)
    second, dots = call(
        functools.partial(second_kernel, group, len(parts)),
        [(half + BIAS, LANES), (8, LANES)],
        *parts,
        first,
        diag,
    )
    peer_second = swap(second)
    devices = n_stu * n_que
    (dots,) = call(form_kernel, [(devices, 1, LANES)], second, peer_second, left, right, weight, dots)
    dots = lax.all_to_all(dots, AXES, 0, 0, tiled=True)
    abilities, discs, icpts = call(
        functools.partial(finish_kernel, group),
        [(size, width), (size, width), (1, size)],
        dots,
        first,
        peer,
        second,
        peer_second,
        whole,
    )
    return abilities, discs, icpts[0]


def solution(mesh):
    placed = (P("stu", "que"), P(("stu", "que"), None), P(("que", "stu"), None), P(("que", "stu")))
    return jax.shard_map(
        functools.partial(shards, mesh.shape["stu"], mesh.shape["que"]),
        mesh=mesh,
        in_specs=placed,
        out_specs=(P(("stu", "que"), None), P(("que", "stu"), None), P(("que", "stu"))),
        check_vma=False,
    )
```

```python
import functools

import jax
import jax.numpy as jnp
from jax import lax
from jax.experimental import pallas as pl
from jax.experimental.pallas import tpu as pltpu
from jax.sharding import PartitionSpec as P

AXES = ("stu", "que")
LANES = 128
GATHER_ORDER = (1, 3, 2)
FIRST_ORDER = (3, 1, 2)
SECOND_ORDER = (1, 2, 3)
BIAS = 8


def halves(value):
    high = value.astype(jnp.bfloat16)
    return high, (value - high.astype(jnp.float32)).astype(jnp.bfloat16)


def product(left, right, dims):
    return lax.dot_general(left, right, (dims, ((), ())), preferred_element_type=jnp.float32)


def dot_nt(left, right):
    left_high, left_low = halves(left)
    right_high, right_low = halves(right)
    dims = ((1,), (1,))
    both = product(
        jnp.concatenate([left_high, left_low], 1), jnp.concatenate([right_high, right_high], 1), dims
    )
    return both + product(left_high, right_low, dims)


def dot_nn(left, right):
    left_high, left_low = halves(left)
    right_high, right_low = halves(right)
    dims = ((1,), (0,))
    both = product(left_high, jnp.concatenate([right_high, right_low], 1), dims)
    width = right.shape[1]
    return both[:, :width] + both[:, width:] + product(left_low, right_high, dims)


def position():
    que = lax.axis_index("que")
    return lax.rem(que, 2), que // 2, lax.axis_index("stu")


def block_of(side, core, line, plane, group):
    return jnp.where(side == 0, line * 2 + core, core * group + plane)


def low_lanes(shape):
    return lax.broadcasted_iota(jnp.int32, shape, 1) < LANES // 2


def turn(value):
    return pltpu.roll(value, LANES // 2, 1)


def pack(value):
    half = value.shape[0] // 2
    low = low_lanes((half, LANES))
    return jnp.where(low, value[:half], turn(value[half:]))


def bias_rows(lanes):
    return jnp.concatenate([lanes[:, :LANES], lanes[:, LANES:]], 0)


def bias_lanes(rows):
    return jnp.concatenate([rows[0:1], rows[1:2]], 1)


def column(rows):
    tall = jnp.concatenate([rows, jnp.zeros((BIAS - 2, LANES), jnp.float32)], 0).T
    return jnp.concatenate([tall[:, 0:1], tall[:, 1:2]], 0)


def arrange_kernel(own_ref, peer_ref, out_ref):
    core, _, _ = position()
    cols = own_ref.shape[1]

    @pl.when(core == 0)
    def _():
        out_ref[:, :cols] = own_ref[...].astype(jnp.float32)
        out_ref[:, cols:] = peer_ref[...].astype(jnp.float32)

    @pl.when(core == 1)
    def _():
        out_ref[:cols, :] = peer_ref[...].astype(jnp.float32).T
        out_ref[cols:, :] = own_ref[...].astype(jnp.float32).T


def pieces(refs, size):
    step = size + BIAS
    return [ref[first : first + step, :] for ref in refs for first in range(0, ref.shape[0], step)]


def place(blocks, dst_ref, side, columns, core, line, plane, group):
    size = dst_ref.shape[0] // (2 * group)
    lane = lax.broadcasted_iota(jnp.int32, (size, LANES), 1)
    half = LANES // 2
    for at, (k, block) in enumerate(blocks):
        for j in range(2):
            value = turn(block[:size]) if j else block[:size]
            last = jnp.where(side == 0, 1.0, columns[j * half : j * half + size, at : at + 1])
            row = block_of(side, core ^ j, line ^ k, plane ^ k, group) * size
            dst_ref[pl.ds(pl.multiple_of(row, size), size), :] = jnp.where(
                lane < half, value, jnp.where(lane == half, last, 0.0)
            )


def gradient_kernel(group, places, parts, *refs):
    code_ref, sums_ref, left_ref, right_ref, weight_ref, icpt_ref = refs[2 * parts :]
    core, line, plane = position()
    size = left_ref.shape[0] // (2 * group)
    mine = pieces(refs[:parts], size)
    other = pieces(refs[parts : 2 * parts], size)
    rows = [jnp.where(core == 0, there[size : size + 1], here[size : size + 1]) for here, there in zip(mine, other)]
    columns = jnp.concatenate(rows + [jnp.zeros((-group % BIAS, LANES), jnp.float32)] * (group % BIAS > 0), 0).T
    place(list(zip(places, mine)), left_ref, core, columns, core, line, plane, group)
    place(list(zip(places, other)), right_ref, 1 - core, columns, 1 - core, line, plane, group)
    left = left_ref[...]
    right = right_ref[...]
    prob = 1.0 / (1.0 + jnp.exp(-dot_nt(left, right)))
    code = code_ref[...]
    seen = code > 0.0
    resid = jnp.where(seen, prob - jnp.where(code == 2.0, 1.0, 0.0), 0.0)
    weight = jnp.where(seen, prob * (1.0 - prob), 0.0)
    weight_ref[...] = weight
    rows = left.shape[0]
    grad = dot_nn(resid, right)
    diag = dot_nn(weight, right * right)
    sums_ref[:rows, :] = jnp.where(low_lanes((rows, LANES)), grad, turn(diag))
    at = LANES // 2

    @pl.when(core == 0)
    def _():
        sums_ref[rows:, :] = jnp.zeros((BIAS, LANES), jnp.float32)
        icpt_ref[...] = jnp.zeros((BIAS, LANES), jnp.float32)

    @pl.when(core == 1)
    def _():
        lane = lax.broadcasted_iota(jnp.int32, (rows, LANES), 1)
        moved = jnp.where(lane == at + 1, pltpu.roll(diag, 1, 1), pltpu.roll(left, 2, 1))
        lanes = jnp.where(lane == at, grad, moved).T
        spare = jnp.zeros((BIAS - 4, LANES), jnp.float32)
        sums_ref[rows:, :] = jnp.concatenate([bias_rows(lanes[at : at + 1]), bias_rows(lanes[at + 1 : at + 2]), spare], 0)
        spare = jnp.zeros((BIAS - 2, LANES), jnp.float32)
        icpt_ref[...] = jnp.concatenate([bias_rows(lanes[at + 2 : at + 3]), spare], 0)


def start_kernel(group, parts, *refs):
    sum_refs, (left_ref, icpt_ref, send_ref, diag_ref, whole_ref) = refs[:parts], refs[parts:]
    core, line, plane = position()
    total = sum_refs[0][...]
    for ref in sum_refs[1:]:
        total = total + ref[...]
    rows = left_ref.shape[0]
    half = rows // 2
    low = low_lanes((rows, LANES))
    main = total[:rows]
    diag = jnp.where(low, turn(main) + 1.0, 1.0)
    first = jnp.where(low, -(main + left_ref[...]) / diag, 0.0)
    grad_b = total[rows : rows + 2] + icpt_ref[:2]
    diag_b = total[rows + 2 : rows + 4] + 1.0
    first_b = -grad_b / diag_b
    whole_ref[...] = diag
    send_ref[:half, :] = pack(first)
    send_ref[half : half + BIAS, :] = jnp.concatenate(
        [first_b, diag_b, jnp.zeros((BIAS - 4, LANES), jnp.float32)], 0
    )
    diag_ref[:half, :] = pack(diag)
    diag_ref[half:, :] = jnp.concatenate([diag_b, jnp.ones((BIAS - 2, LANES), jnp.float32)], 0)
    size = rows // (2 * group)
    at = block_of(core, 1 - core, line, plane, group) * size
    send_ref[half + BIAS :, :] = whole_ref[pl.ds(pl.multiple_of(at, size), size), :]


def change_of(mine_ref, other_ref, left, right, half):
    low = low_lanes((half, LANES))
    mine = mine_ref[:half, :]
    other = other_ref[:half, :]
    lhs = jnp.concatenate(
        [
            jnp.where(low, mine, turn(left[:half])),
            jnp.where(low, turn(mine), turn(left[half:])),
        ],
        0,
    )
    rhs = jnp.concatenate(
        [
            jnp.where(low, right[:half], turn(other)),
            jnp.where(low, right[half:], other),
        ],
        0,
    )
    return dot_nt(lhs, rhs)


def with_bias(change, mine_ref, other_ref, half, use):
    core, _, _ = position()

    @pl.when(core == 0)
    def _():
        use(change + bias_lanes(other_ref[half : half + 2, :]))

    @pl.when(core == 1)
    def _():
        use(change + column(mine_ref[half : half + 2, :]))


def image_kernel(mine_ref, other_ref, left_ref, right_ref, weight_ref, sums_ref):
    core, _, _ = position()
    half = left_ref.shape[0] // 2
    right = right_ref[...]
    change = change_of(mine_ref, other_ref, left_ref[...], right, half)
    at = LANES // 2

    def use(value):
        sums = dot_nn(weight_ref[...] * value, right)
        sums_ref[:half, :] = pack(sums)
        sums_ref[half:, :] = jnp.zeros((BIAS, LANES), jnp.float32)

        @pl.when(core == 1)
        def _():
            sums_ref[half : half + 2, :] = bias_rows(sums.T[at : at + 1])

    with_bias(change, mine_ref, other_ref, half, use)


def second_kernel(group, parts, *refs):
    sum_refs, (send_ref, diag_ref, second_ref, dots_ref) = refs[:parts], refs[parts:]
    total = sum_refs[0][...]
    for ref in sum_refs[1:]:
        total = total + ref[...]
    half = total.shape[0] - BIAS
    row = lax.broadcasted_iota(jnp.int32, total.shape, 0)
    used = row < half + 2
    first = jnp.where(used, send_ref[: half + BIAS, :], 0.0)
    diag = diag_ref[...]
    lift = jnp.where(used, total + first - diag * first, 0.0)
    second = lift / diag
    second_ref[...] = second
    terms = (first * first * diag, first * lift, second * lift, second * second)
    dots_ref[...] = jnp.concatenate(
        [jnp.sum(term, axis=0, keepdims=True) for term in terms] + [jnp.zeros((8 - len(terms), LANES), jnp.float32)], 0
    ) * (1.0 / group)


def form_kernel(mine_ref, other_ref, left_ref, right_ref, weight_ref, dots_ref, out_ref):
    core, _, _ = position()
    half = left_ref.shape[0] // 2

    def give(terms):
        row = lax.broadcasted_iota(jnp.int32, (8, LANES), 0)
        lane = lax.broadcasted_iota(jnp.int32, (8, LANES), 1)
        sums = jnp.sum(terms, axis=1, keepdims=True)
        dots = jnp.sum(jnp.where(lane == row, sums, 0.0), axis=0, keepdims=True)
        out_ref[...] = jnp.broadcast_to(dots[None], out_ref.shape)

    @pl.when(core == 0)
    def _():
        change = change_of(mine_ref, other_ref, left_ref[...], right_ref[...], half)
        change = change + bias_lanes(other_ref[half : half + 2, :])
        form = jnp.sum(weight_ref[...] * change * change, axis=0, keepdims=True)
        row = lax.broadcasted_iota(jnp.int32, (8, LANES), 0)
        give(dots_ref[...] + jnp.where(row == 3, form[:, :LANES] + form[:, LANES:], 0.0))

    @pl.when(core == 1)
    def _():
        give(dots_ref[...])


def finish_kernel(
    group, dots_ref, send_ref, peer_ref, second_ref, peer_second_ref, whole_ref, theta_ref, disc_ref, icpt_ref
):
    core, line, plane = position()
    dots = jnp.sum(dots_ref[...], axis=0)
    lane = lax.broadcasted_iota(jnp.int32, (8, LANES), 1)
    row = lax.broadcasted_iota(jnp.int32, (8, LANES), 0)
    sums = jnp.sum(jnp.where(lane == row, dots, 0.0), axis=1, keepdims=True)
    a, f, h, d = [sums[at : at + 1] for at in range(4)]
    b = a + f
    e = f + h
    scale = 1.0 / (b * d - e * e)
    s = (a * d - e * f) * scale
    t = (f * f - a * h) * scale
    rows = whole_ref.shape[0]
    half = rows // 2
    size = rows // (2 * group)

    def direction(first_ref, next_ref, at):
        upper = at // group
        rows_at = pl.ds(pl.multiple_of(lax.rem(at, group) * size, size), size)
        value = s * first_ref[rows_at, :] + t * next_ref[rows_at, :]
        return jnp.where(upper == 1, turn(value), value)

    mine_at = block_of(core, core, line, plane, group)
    other_at = block_of(1 - core, core, line, plane, group)
    mine = direction(send_ref, second_ref, mine_at)
    mine = mine * jnp.sqrt(whole_ref[pl.ds(pl.multiple_of(mine_at * size, size), size), :])
    other = direction(peer_ref, peer_second_ref, other_at) * jnp.sqrt(peer_ref[half + BIAS :, :])
    theta_ref[...] = jnp.where(core == 0, mine, other)[:, : LANES // 2]
    disc_ref[...] = jnp.where(core == 0, other, mine)[:, : LANES // 2]
    ask = jnp.where(core == 0, peer_ref[half : half + BIAS, :], send_ref[half : half + BIAS, :])
    ask_next = jnp.where(core == 0, peer_second_ref[half : half + 2, :], second_ref[half : half + 2, :])
    bias = (s * ask[0:2] + t * ask_next) * jnp.sqrt(ask[2:4])
    disc_at = jnp.where(core == 0, other_at, mine_at)
    row = jnp.where(disc_at // group == 1, bias[1:2], bias[0:1])
    back = lax.rem(LANES - lax.rem(disc_at, group) * size, LANES)
    icpt_ref[...] = pltpu.roll(row, back, 1)[:, :size]


def call(kernel, shapes, *args):
    out = [jax.ShapeDtypeStruct(shape, jnp.float32) for shape in shapes]
    return pl.pallas_call(
        kernel,
        out_shape=out,
        in_specs=[pl.BlockSpec(memory_space=pltpu.VMEM)] * len(args),
        out_specs=[pl.BlockSpec(memory_space=pltpu.VMEM)] * len(out),
        compiler_params=pltpu.CompilerParams(vmem_limit_bytes=32 * 2**20),
    )(*args)


def swap_cores(value, n_stu, n_que):
    return lax.ppermute(value, AXES, [(i, i ^ 1) for i in range(n_stu * n_que)])


def send_over(value, step, n_stu, n_que, crossed=False):
    pairs = []
    for stu in range(n_stu):
        for que in range(n_que):
            there = (stu, que ^ (2 * step)) if (que % 2 == 0) != crossed else (stu ^ step, que)
            pairs.append((stu * n_que + que, there[0] * n_que + there[1]))
    return lax.ppermute(value, AXES, pairs)


def stages(group, order):
    base = 1
    while base < group:
        width = min(4, group // base)
        yield [base * k for k in order if k < width]
        base *= width


def shards(n_stu, n_que, codes, theta, disc, intercept):
    group = n_stu
    assert n_que == 2 * group
    send = functools.partial(send_over, n_stu=n_stu, n_que=n_que)
    swap = functools.partial(swap_cores, n_stu=n_stu, n_que=n_que)
    size, width = theta.shape
    rows = 2 * group * size
    half = rows // 2
    assert width == LANES // 2 and rows == 2 * LANES
    assert disc.shape == theta.shape and codes.shape == (rows, half)
    core = lax.rem(lax.axis_index("que"), 2)
    peer_theta, peer_disc, peer_icpt = swap(theta), swap(disc), swap(intercept)

    def block(own, own_icpt, peers, peers_icpt):
        icpt = jnp.pad(jnp.stack([own_icpt, peers_icpt]), ((0, 0), (0, width - size))).reshape(1, LANES)
        spare = jnp.zeros((BIAS - 1, LANES), jnp.float32)
        return jnp.concatenate([jnp.concatenate([own, peers], 1), icpt, spare], 0)

    def side(students, questions):
        return jnp.where(core == 0, students, questions)

    mine = [block(side(theta, disc), intercept, side(peer_theta, peer_disc), peer_icpt)]
    other = [block(side(peer_disc, peer_theta), peer_icpt, side(disc, theta), intercept)]
    (code,) = call(arrange_kernel, [(rows, rows)], codes, swap(codes))
    places = [0]
    for steps in stages(group, GATHER_ORDER):
        ours, theirs = jnp.concatenate(mine, 0), jnp.concatenate(other, 0)
        for step in steps:
            crossed = step == max(steps)
            piece = send(theirs if crossed else ours, step, crossed=crossed)
            back = swap(piece)
            mine.append(back if crossed else piece)
            other.append(piece if crossed else back)
        places = places + [step + place for step in steps for place in places]

    def totals(value, order):
        parts = [value]
        for number, steps in enumerate(stages(group, order)):
            if number:
                parts = [functools.reduce(jnp.add, parts)]
            parts = parts + [send(parts[0], step) for step in steps]
        return parts

    sums, left, right, weight, icpt = call(
        functools.partial(gradient_kernel, group, tuple(places), len(mine)),
        [(rows + BIAS, LANES), (rows, LANES), (rows, LANES), (rows, rows), (BIAS, LANES)],
        *mine,
        *other,
        code,
    )
    parts = totals(sums, FIRST_ORDER)
    first, diag, whole = call(
        functools.partial(start_kernel, group, len(parts)),
        [(half + BIAS + size, LANES), (half + BIAS, LANES), (rows, LANES)],
        *parts,
        left,
        icpt,
    )
    peer = swap(first)
    (sums,) = call(image_kernel, [(half + BIAS, LANES)], first, peer, left, right, weight)
    parts = totals(sums, SECOND_ORDER)
    second, dots = call(
        functools.partial(second_kernel, group, len(parts)),
        [(half + BIAS, LANES), (8, LANES)],
        *parts,
        first,
        diag,
    )
    peer_second = swap(second)
    devices = n_stu * n_que
    (dots,) = call(form_kernel, [(devices, 1, LANES)], second, peer_second, left, right, weight, dots)
    dots = lax.all_to_all(dots, AXES, 0, 0, tiled=True)
    abilities, discs, icpts = call(
        functools.partial(finish_kernel, group),
        [(size, width), (size, width), (1, size)],
        dots,
        first,
        peer,
        second,
        peer_second,
        whole,
    )
    return abilities, discs, icpts[0]


def solution(mesh):
    placed = (P("stu", "que"), P(("stu", "que"), None), P(("que", "stu"), None), P(("que", "stu")))
    return jax.shard_map(
        functools.partial(shards, mesh.shape["stu"], mesh.shape["que"]),
        mesh=mesh,
        in_specs=placed,
        out_specs=(P(("stu", "que"), None), P(("que", "stu"), None), P(("que", "stu"))),
        check_vma=False,
    )
```

```python
import functools

import jax
import jax.numpy as jnp
from jax import lax
from jax.experimental import pallas as pl
from jax.experimental.pallas import tpu as pltpu
from jax.sharding import PartitionSpec as P

AXES = ("stu", "que")
LANES = 128
GATHER_ORDER = (1, 3, 2)
FIRST_ORDER = (3, 1, 2)
SECOND_ORDER = (1, 2, 3)
BIAS = 8


def halves(value):
    high = value.astype(jnp.bfloat16)
    return high, (value - high.astype(jnp.float32)).astype(jnp.bfloat16)


def product(left, right, dims):
    return lax.dot_general(left, right, (dims, ((), ())), preferred_element_type=jnp.float32)


def dot_nt(left, right):
    left_high, left_low = halves(left)
    right_high, right_low = halves(right)
    dims = ((1,), (1,))
    both = product(
        jnp.concatenate([left_high, left_low], 1), jnp.concatenate([right_high, right_high], 1), dims
    )
    return both + product(left_high, right_low, dims)


def dot_nn(left, right):
    left_high, left_low = halves(left)
    right_high, right_low = halves(right)
    dims = ((1,), (0,))
    both = product(left_high, jnp.concatenate([right_high, right_low], 1), dims)
    width = right.shape[1]
    return both[:, :width] + both[:, width:] + product(left_low, right_high, dims)


def position():
    que = lax.axis_index("que")
    return lax.rem(que, 2), que // 2, lax.axis_index("stu")


def block_of(side, core, line, plane, group):
    return jnp.where(side == 0, line * 2 + core, core * group + plane)


def low_lanes(shape):
    return lax.broadcasted_iota(jnp.int32, shape, 1) < LANES // 2


def turn(value):
    return pltpu.roll(value, LANES // 2, 1)


def pack(value):
    half = value.shape[0] // 2
    low = low_lanes((half, LANES))
    return jnp.where(low, value[:half], turn(value[half:]))


def bias_rows(lanes):
    return jnp.concatenate([lanes[:, :LANES], lanes[:, LANES:]], 0)


def bias_lanes(rows):
    return jnp.concatenate([rows[0:1], rows[1:2]], 1)


def column(rows):
    tall = jnp.concatenate([rows, jnp.zeros((BIAS - 2, LANES), jnp.float32)], 0).T
    return jnp.concatenate([tall[:, 0:1], tall[:, 1:2]], 0)


def arrange_kernel(own_ref, peer_ref, out_ref):
    core, _, _ = position()
    cols = own_ref.shape[1]

    @pl.when(core == 0)
    def _():
        out_ref[:, :cols] = own_ref[...].astype(jnp.float32)
        out_ref[:, cols:] = peer_ref[...].astype(jnp.float32)

    @pl.when(core == 1)
    def _():
        out_ref[:cols, :] = peer_ref[...].astype(jnp.float32).T
        out_ref[cols:, :] = own_ref[...].astype(jnp.float32).T


def pieces(refs, size):
    step = size + BIAS
    return [ref[first : first + step, :] for ref in refs for first in range(0, ref.shape[0], step)]


def place(blocks, dst_ref, side, columns, core, line, plane, group):
    size = dst_ref.shape[0] // (2 * group)
    lane = lax.broadcasted_iota(jnp.int32, (size, LANES), 1)
    half = LANES // 2
    for at, (k, block) in enumerate(blocks):
        for j in range(2):
            value = turn(block[:size]) if j else block[:size]
            last = jnp.where(side == 0, 1.0, columns[j * half : j * half + size, at : at + 1])
            row = block_of(side, core ^ j, line ^ k, plane ^ k, group) * size
            dst_ref[pl.ds(pl.multiple_of(row, size), size), :] = jnp.where(
                lane < half, value, jnp.where(lane == half, last, 0.0)
            )


def gradient_kernel(group, places, parts, *refs):
    code_ref, refs = refs[0], refs[1:]
    sums_ref, left_ref, right_ref, weight_ref, icpt_ref = refs[2 * parts :]
    core, line, plane = position()
    size = left_ref.shape[0] // (2 * group)
    mine = pieces(refs[:parts], size)
    other = pieces(refs[parts : 2 * parts], size)
    rows = [jnp.where(core == 0, there[size : size + 1], here[size : size + 1]) for here, there in zip(mine, other)]
    columns = jnp.concatenate(rows + [jnp.zeros((-group % BIAS, LANES), jnp.float32)] * (group % BIAS > 0), 0).T
    place(list(zip(places, mine)), left_ref, core, columns, core, line, plane, group)
    place(list(zip(places, other)), right_ref, 1 - core, columns, 1 - core, line, plane, group)
    left = left_ref[...]
    right = right_ref[...]
    prob = 1.0 / (1.0 + jnp.exp(-dot_nt(left, right)))
    code = code_ref[...]
    seen = code > 0.0
    resid = jnp.where(seen, prob - jnp.where(code == 2.0, 1.0, 0.0), 0.0)
    weight = jnp.where(seen, prob * (1.0 - prob), 0.0)
    weight_ref[...] = weight
    rows = left.shape[0]
    grad = dot_nn(resid, right)
    diag = dot_nn(weight, right * right)
    sums_ref[:rows, :] = jnp.where(low_lanes((rows, LANES)), grad, turn(diag))
    at = LANES // 2

    @pl.when(core == 0)
    def _():
        sums_ref[rows:, :] = jnp.zeros((BIAS, LANES), jnp.float32)
        icpt_ref[...] = jnp.zeros((BIAS, LANES), jnp.float32)

    @pl.when(core == 1)
    def _():
        lane = lax.broadcasted_iota(jnp.int32, (rows, LANES), 1)
        moved = jnp.where(lane == at + 1, pltpu.roll(diag, 1, 1), pltpu.roll(left, 2, 1))
        lanes = jnp.where(lane == at, grad, moved).T
        spare = jnp.zeros((BIAS - 4, LANES), jnp.float32)
        sums_ref[rows:, :] = jnp.concatenate([bias_rows(lanes[at : at + 1]), bias_rows(lanes[at + 1 : at + 2]), spare], 0)
        spare = jnp.zeros((BIAS - 2, LANES), jnp.float32)
        icpt_ref[...] = jnp.concatenate([bias_rows(lanes[at + 2 : at + 3]), spare], 0)


def start_kernel(group, parts, *refs):
    sum_refs, (left_ref, icpt_ref, send_ref, diag_ref, whole_ref) = refs[:parts], refs[parts:]
    core, line, plane = position()
    total = sum_refs[0][...]
    for ref in sum_refs[1:]:
        total = total + ref[...]
    rows = left_ref.shape[0]
    half = rows // 2
    low = low_lanes((rows, LANES))
    main = total[:rows]
    diag = jnp.where(low, turn(main) + 1.0, 1.0)
    first = jnp.where(low, -(main + left_ref[...]) / diag, 0.0)
    grad_b = total[rows : rows + 2] + icpt_ref[:2]
    diag_b = total[rows + 2 : rows + 4] + 1.0
    first_b = -grad_b / diag_b
    whole_ref[...] = diag
    send_ref[:half, :] = pack(first)
    send_ref[half : half + BIAS, :] = jnp.concatenate(
        [first_b, diag_b, jnp.zeros((BIAS - 4, LANES), jnp.float32)], 0
    )
    diag_ref[:half, :] = pack(diag)
    diag_ref[half:, :] = jnp.concatenate([diag_b, jnp.ones((BIAS - 2, LANES), jnp.float32)], 0)
    size = rows // (2 * group)
    at = block_of(core, 1 - core, line, plane, group) * size
    send_ref[half + BIAS :, :] = whole_ref[pl.ds(pl.multiple_of(at, size), size), :]


def change_of(mine_ref, other_ref, left, right, half):
    low = low_lanes((half, LANES))
    mine = mine_ref[:half, :]
    other = other_ref[:half, :]
    lhs = jnp.concatenate(
        [
            jnp.where(low, mine, turn(left[:half])),
            jnp.where(low, turn(mine), turn(left[half:])),
        ],
        0,
    )
    rhs = jnp.concatenate(
        [
            jnp.where(low, right[:half], turn(other)),
            jnp.where(low, right[half:], other),
        ],
        0,
    )
    return dot_nt(lhs, rhs)


def with_bias(change, mine_ref, other_ref, half, use):
    core, _, _ = position()

    @pl.when(core == 0)
    def _():
        use(change + bias_lanes(other_ref[half : half + 2, :]))

    @pl.when(core == 1)
    def _():
        use(change + column(mine_ref[half : half + 2, :]))


def image_kernel(mine_ref, other_ref, left_ref, right_ref, weight_ref, sums_ref):
    core, _, _ = position()
    half = left_ref.shape[0] // 2
    right = right_ref[...]
    change = change_of(mine_ref, other_ref, left_ref[...], right, half)
    at = LANES // 2

    def use(value):
        sums = dot_nn(weight_ref[...] * value, right)
        sums_ref[:half, :] = pack(sums)
        sums_ref[half:, :] = jnp.zeros((BIAS, LANES), jnp.float32)

        @pl.when(core == 1)
        def _():
            sums_ref[half : half + 2, :] = bias_rows(sums.T[at : at + 1])

    with_bias(change, mine_ref, other_ref, half, use)


def second_kernel(group, parts, *refs):
    sum_refs, (send_ref, diag_ref, second_ref, dots_ref) = refs[:parts], refs[parts:]
    total = sum_refs[0][...]
    for ref in sum_refs[1:]:
        total = total + ref[...]
    half = total.shape[0] - BIAS
    row = lax.broadcasted_iota(jnp.int32, total.shape, 0)
    used = row < half + 2
    first = jnp.where(used, send_ref[: half + BIAS, :], 0.0)
    diag = diag_ref[...]
    lift = jnp.where(used, total + first - diag * first, 0.0)
    second = lift / diag
    second_ref[...] = second
    terms = (first * first * diag, first * lift, second * lift, second * second)
    dots_ref[...] = jnp.concatenate(
        [jnp.sum(term, axis=0, keepdims=True) for term in terms] + [jnp.zeros((8 - len(terms), LANES), jnp.float32)], 0
    ) * (1.0 / group)


def form_kernel(mine_ref, other_ref, left_ref, right_ref, weight_ref, dots_ref, out_ref):
    core, _, _ = position()
    half = left_ref.shape[0] // 2

    def give(terms):
        row = lax.broadcasted_iota(jnp.int32, (8, LANES), 0)
        lane = lax.broadcasted_iota(jnp.int32, (8, LANES), 1)
        sums = jnp.sum(terms, axis=1, keepdims=True)
        dots = jnp.sum(jnp.where(lane == row, sums, 0.0), axis=0, keepdims=True)
        out_ref[...] = jnp.broadcast_to(dots[None], out_ref.shape)

    @pl.when(core == 0)
    def _():
        change = change_of(mine_ref, other_ref, left_ref[...], right_ref[...], half)
        change = change + bias_lanes(other_ref[half : half + 2, :])
        form = jnp.sum(weight_ref[...] * change * change, axis=0, keepdims=True)
        row = lax.broadcasted_iota(jnp.int32, (8, LANES), 0)
        give(dots_ref[...] + jnp.where(row == 3, form[:, :LANES] + form[:, LANES:], 0.0))

    @pl.when(core == 1)
    def _():
        give(dots_ref[...])


def finish_kernel(
    group, dots_ref, send_ref, peer_ref, second_ref, peer_second_ref, whole_ref, theta_ref, disc_ref, icpt_ref
):
    core, line, plane = position()
    dots = jnp.sum(dots_ref[...], axis=0)
    lane = lax.broadcasted_iota(jnp.int32, (8, LANES), 1)
    row = lax.broadcasted_iota(jnp.int32, (8, LANES), 0)
    sums = jnp.sum(jnp.where(lane == row, dots, 0.0), axis=1, keepdims=True)
    a, f, h, d = [sums[at : at + 1] for at in range(4)]
    b = a + f
    e = f + h
    det = b * d - e * e
    s = (a * d - e * f) / det
    t = (f * f - a * h) / det
    rows = whole_ref.shape[0]
    half = rows // 2
    size = rows // (2 * group)

    def direction(first_ref, next_ref, at):
        upper = at // group
        rows_at = pl.ds(pl.multiple_of(lax.rem(at, group) * size, size), size)
        value = s * first_ref[rows_at, :] + t * next_ref[rows_at, :]
        return jnp.where(upper == 1, turn(value), value)

    mine_at = block_of(core, core, line, plane, group)
    other_at = block_of(1 - core, core, line, plane, group)
    mine = direction(send_ref, second_ref, mine_at)
    mine = mine * jnp.sqrt(whole_ref[pl.ds(pl.multiple_of(mine_at * size, size), size), :])
    other = direction(peer_ref, peer_second_ref, other_at) * jnp.sqrt(peer_ref[half + BIAS :, :])
    theta_ref[...] = jnp.where(core == 0, mine, other)[:, : LANES // 2]
    disc_ref[...] = jnp.where(core == 0, other, mine)[:, : LANES // 2]
    ask = jnp.where(core == 0, peer_ref[half : half + BIAS, :], send_ref[half : half + BIAS, :])
    ask_next = jnp.where(core == 0, peer_second_ref[half : half + 2, :], second_ref[half : half + 2, :])
    bias = (s * ask[0:2] + t * ask_next) * jnp.sqrt(ask[2:4])
    disc_at = jnp.where(core == 0, other_at, mine_at)
    row = jnp.where(disc_at // group == 1, bias[1:2], bias[0:1])
    back = lax.rem(LANES - lax.rem(disc_at, group) * size, LANES)
    icpt_ref[...] = pltpu.roll(row, back, 1)[:, :size]


def call(kernel, shapes, *args):
    out = [jax.ShapeDtypeStruct(shape, jnp.float32) for shape in shapes]
    return pl.pallas_call(
        kernel,
        out_shape=out,
        in_specs=[pl.BlockSpec(memory_space=pltpu.VMEM)] * len(args),
        out_specs=[pl.BlockSpec(memory_space=pltpu.VMEM)] * len(out),
        compiler_params=pltpu.CompilerParams(vmem_limit_bytes=32 * 2**20),
    )(*args)


def swap_cores(value, n_stu, n_que):
    return lax.ppermute(value, AXES, [(i, i ^ 1) for i in range(n_stu * n_que)])


def send_over(value, step, n_stu, n_que, crossed=False):
    pairs = []
    for stu in range(n_stu):
        for que in range(n_que):
            there = (stu, que ^ (2 * step)) if (que % 2 == 0) != crossed else (stu ^ step, que)
            pairs.append((stu * n_que + que, there[0] * n_que + there[1]))
    return lax.ppermute(value, AXES, pairs)


def stages(group, order):
    base = 1
    while base < group:
        width = min(4, group // base)
        yield [base * k for k in order if k < width]
        base *= width


def shards(n_stu, n_que, codes, theta, disc, intercept):
    group = n_stu
    assert n_que == 2 * group
    send = functools.partial(send_over, n_stu=n_stu, n_que=n_que)
    swap = functools.partial(swap_cores, n_stu=n_stu, n_que=n_que)
    size, width = theta.shape
    rows = 2 * group * size
    half = rows // 2
    assert width == LANES // 2 and rows == 2 * LANES
    assert disc.shape == theta.shape and codes.shape == (rows, half)
    core = lax.rem(lax.axis_index("que"), 2)
    peer_theta, peer_disc, peer_icpt = swap(theta), swap(disc), swap(intercept)

    def block(own, own_icpt, peers, peers_icpt):
        icpt = jnp.pad(jnp.stack([own_icpt, peers_icpt]), ((0, 0), (0, width - size))).reshape(1, LANES)
        spare = jnp.zeros((BIAS - 1, LANES), jnp.float32)
        return jnp.concatenate([jnp.concatenate([own, peers], 1), icpt, spare], 0)

    def side(students, questions):
        return jnp.where(core == 0, students, questions)

    mine = [block(side(theta, disc), intercept, side(peer_theta, peer_disc), peer_icpt)]
    other = [block(side(peer_disc, peer_theta), peer_icpt, side(disc, theta), intercept)]
    (code,) = call(arrange_kernel, [(rows, rows)], codes, swap(codes))
    places = [0]
    for steps in stages(group, GATHER_ORDER):
        ours, theirs = jnp.concatenate(mine, 0), jnp.concatenate(other, 0)
        for step in steps:
            crossed = step == max(steps)
            piece = send(theirs if crossed else ours, step, crossed=crossed)
            back = swap(piece)
            mine.append(back if crossed else piece)
            other.append(piece if crossed else back)
        places = places + [step + place for step in steps for place in places]

    def totals(value, order):
        parts = [value]
        for number, steps in enumerate(stages(group, order)):
            if number:
                parts = [functools.reduce(jnp.add, parts)]
            parts = parts + [send(parts[0], step) for step in steps]
        return parts

    sums, left, right, weight, icpt = call(
        functools.partial(gradient_kernel, group, tuple(places), len(mine)),
        [(rows + BIAS, LANES), (rows, LANES), (rows, LANES), (rows, rows), (BIAS, LANES)],
        code,
        *mine,
        *other,
    )
    parts = totals(sums, FIRST_ORDER)
    first, diag, whole = call(
        functools.partial(start_kernel, group, len(parts)),
        [(half + BIAS + size, LANES), (half + BIAS, LANES), (rows, LANES)],
        *parts,
        left,
        icpt,
    )
    peer = swap(first)
    (sums,) = call(image_kernel, [(half + BIAS, LANES)], first, peer, left, right, weight)
    parts = totals(sums, SECOND_ORDER)
    second, dots = call(
        functools.partial(second_kernel, group, len(parts)),
        [(half + BIAS, LANES), (8, LANES)],
        *parts,
        first,
        diag,
    )
    peer_second = swap(second)
    devices = n_stu * n_que
    (dots,) = call(form_kernel, [(devices, 1, LANES)], second, peer_second, left, right, weight, dots)
    dots = lax.all_to_all(dots, AXES, 0, 0, tiled=True)
    abilities, discs, icpts = call(
        functools.partial(finish_kernel, group),
        [(size, width), (size, width), (1, size)],
        dots,
        first,
        peer,
        second,
        peer_second,
        whole,
    )
    return abilities, discs, icpts[0]


def solution(mesh):
    placed = (P("stu", "que"), P(("stu", "que"), None), P(("que", "stu"), None), P(("que", "stu")))
    return jax.shard_map(
        functools.partial(shards, mesh.shape["stu"], mesh.shape["que"]),
        mesh=mesh,
        in_specs=placed,
        out_specs=(P(("stu", "que"), None), P(("que", "stu"), None), P(("que", "stu"))),
        check_vma=False,
    )
```

```python
import functools

import jax
import jax.numpy as jnp
from jax import lax
from jax.experimental import pallas as pl
from jax.experimental.pallas import tpu as pltpu
from jax.sharding import PartitionSpec as P

AXES = ("stu", "que")
LANES = 128
GATHER_ORDER = (3, 2, 1)
FIRST_ORDER = (3, 1, 2)
SECOND_ORDER = (1, 2, 3)
BIAS = 8


def halves(value):
    high = value.astype(jnp.bfloat16)
    return high, (value - high.astype(jnp.float32)).astype(jnp.bfloat16)


def product(left, right, dims):
    return lax.dot_general(left, right, (dims, ((), ())), preferred_element_type=jnp.float32)


def dot_nt(left, right):
    left_high, left_low = halves(left)
    right_high, right_low = halves(right)
    dims = ((1,), (1,))
    both = product(
        jnp.concatenate([left_high, left_low], 1), jnp.concatenate([right_high, right_high], 1), dims
    )
    return both + product(left_high, right_low, dims)


def dot_nn(left, right):
    left_high, left_low = halves(left)
    right_high, right_low = halves(right)
    dims = ((1,), (0,))
    both = product(left_high, jnp.concatenate([right_high, right_low], 1), dims)
    width = right.shape[1]
    return both[:, :width] + both[:, width:] + product(left_low, right_high, dims)


def position():
    que = lax.axis_index("que")
    return lax.rem(que, 2), que // 2, lax.axis_index("stu")


def block_of(side, core, line, plane, group):
    return jnp.where(side == 0, line * 2 + core, core * group + plane)


def low_lanes(shape):
    return lax.broadcasted_iota(jnp.int32, shape, 1) < LANES // 2


def turn(value):
    return pltpu.roll(value, LANES // 2, 1)


def pack(value):
    half = value.shape[0] // 2
    low = low_lanes((half, LANES))
    return jnp.where(low, value[:half], turn(value[half:]))


def bias_rows(lanes):
    return jnp.concatenate([lanes[:, :LANES], lanes[:, LANES:]], 0)


def bias_lanes(rows):
    return jnp.concatenate([rows[0:1], rows[1:2]], 1)


def column(rows):
    tall = jnp.concatenate([rows, jnp.zeros((BIAS - 2, LANES), jnp.float32)], 0).T
    return jnp.concatenate([tall[:, 0:1], tall[:, 1:2]], 0)


def arrange_kernel(own_ref, peer_ref, out_ref):
    core, _, _ = position()
    cols = own_ref.shape[1]

    @pl.when(core == 0)
    def _():
        out_ref[:, :cols] = own_ref[...].astype(jnp.float32)
        out_ref[:, cols:] = peer_ref[...].astype(jnp.float32)

    @pl.when(core == 1)
    def _():
        out_ref[:cols, :] = peer_ref[...].astype(jnp.float32).T
        out_ref[cols:, :] = own_ref[...].astype(jnp.float32).T


def pieces(refs, size):
    step = size + BIAS
    return [ref[first : first + step, :] for ref in refs for first in range(0, ref.shape[0], step)]


def place(blocks, dst_ref, side, columns, core, line, plane, group):
    size = dst_ref.shape[0] // (2 * group)
    lane = lax.broadcasted_iota(jnp.int32, (size, LANES), 1)
    half = LANES // 2
    for at, (k, block) in enumerate(blocks):
        for j in range(2):
            value = turn(block[:size]) if j else block[:size]
            last = jnp.where(side == 0, 1.0, columns[j * half : j * half + size, at : at + 1])
            row = block_of(side, core ^ j, line ^ k, plane ^ k, group) * size
            dst_ref[pl.ds(pl.multiple_of(row, size), size), :] = jnp.where(
                lane < half, value, jnp.where(lane == half, last, 0.0)
            )


def gradient_kernel(group, places, parts, *refs):
    code_ref, sums_ref, left_ref, right_ref, weight_ref, icpt_ref = refs[2 * parts :]
    core, line, plane = position()
    size = left_ref.shape[0] // (2 * group)
    mine = pieces(refs[:parts], size)
    other = pieces(refs[parts : 2 * parts], size)
    rows = [jnp.where(core == 0, there[size : size + 1], here[size : size + 1]) for here, there in zip(mine, other)]
    columns = jnp.concatenate(rows + [jnp.zeros((-group % BIAS, LANES), jnp.float32)] * (group % BIAS > 0), 0).T
    place(list(zip(places, mine)), left_ref, core, columns, core, line, plane, group)
    place(list(zip(places, other)), right_ref, 1 - core, columns, 1 - core, line, plane, group)
    left = left_ref[...]
    right = right_ref[...]
    prob = 1.0 / (1.0 + jnp.exp(-dot_nt(left, right)))
    code = code_ref[...]
    seen = code > 0.0
    resid = jnp.where(seen, prob - jnp.where(code == 2.0, 1.0, 0.0), 0.0)
    weight = jnp.where(seen, prob * (1.0 - prob), 0.0)
    weight_ref[...] = weight
    rows = left.shape[0]
    grad = dot_nn(resid, right)
    diag = dot_nn(weight, right * right)
    sums_ref[:rows, :] = jnp.where(low_lanes((rows, LANES)), grad, turn(diag))
    at = LANES // 2

    @pl.when(core == 0)
    def _():
        sums_ref[rows:, :] = jnp.zeros((BIAS, LANES), jnp.float32)
        icpt_ref[...] = jnp.zeros((BIAS, LANES), jnp.float32)

    @pl.when(core == 1)
    def _():
        lane = lax.broadcasted_iota(jnp.int32, (rows, LANES), 1)
        moved = jnp.where(lane == at + 1, pltpu.roll(diag, 1, 1), pltpu.roll(left, 2, 1))
        lanes = jnp.where(lane == at, grad, moved).T
        spare = jnp.zeros((BIAS - 4, LANES), jnp.float32)
        sums_ref[rows:, :] = jnp.concatenate([bias_rows(lanes[at : at + 1]), bias_rows(lanes[at + 1 : at + 2]), spare], 0)
        spare = jnp.zeros((BIAS - 2, LANES), jnp.float32)
        icpt_ref[...] = jnp.concatenate([bias_rows(lanes[at + 2 : at + 3]), spare], 0)


def start_kernel(group, parts, *refs):
    sum_refs, (left_ref, icpt_ref, send_ref, diag_ref, whole_ref) = refs[:parts], refs[parts:]
    core, line, plane = position()
    total = sum_refs[0][...]
    for ref in sum_refs[1:]:
        total = total + ref[...]
    rows = left_ref.shape[0]
    half = rows // 2
    low = low_lanes((rows, LANES))
    main = total[:rows]
    diag = jnp.where(low, turn(main) + 1.0, 1.0)
    first = jnp.where(low, -(main + left_ref[...]) / diag, 0.0)
    grad_b = total[rows : rows + 2] + icpt_ref[:2]
    diag_b = total[rows + 2 : rows + 4] + 1.0
    first_b = -grad_b / diag_b
    whole_ref[...] = diag
    send_ref[:half, :] = pack(first)
    send_ref[half : half + BIAS, :] = jnp.concatenate(
        [first_b, diag_b, jnp.zeros((BIAS - 4, LANES), jnp.float32)], 0
    )
    diag_ref[:half, :] = pack(diag)
    diag_ref[half:, :] = jnp.concatenate([diag_b, jnp.ones((BIAS - 2, LANES), jnp.float32)], 0)
    size = rows // (2 * group)
    at = block_of(core, 1 - core, line, plane, group) * size
    send_ref[half + BIAS :, :] = whole_ref[pl.ds(pl.multiple_of(at, size), size), :]


def change_of(mine_ref, other_ref, left, right, half):
    low = low_lanes((half, LANES))
    mine = mine_ref[:half, :]
    other = other_ref[:half, :]
    lhs = jnp.concatenate(
        [
            jnp.where(low, mine, turn(left[:half])),
            jnp.where(low, turn(mine), turn(left[half:])),
        ],
        0,
    )
    rhs = jnp.concatenate(
        [
            jnp.where(low, right[:half], turn(other)),
            jnp.where(low, right[half:], other),
        ],
        0,
    )
    return dot_nt(lhs, rhs)


def with_bias(change, mine_ref, other_ref, half, use):
    core, _, _ = position()

    @pl.when(core == 0)
    def _():
        use(change + bias_lanes(other_ref[half : half + 2, :]))

    @pl.when(core == 1)
    def _():
        use(change + column(mine_ref[half : half + 2, :]))


def image_kernel(mine_ref, other_ref, left_ref, right_ref, weight_ref, sums_ref):
    core, _, _ = position()
    half = left_ref.shape[0] // 2
    right = right_ref[...]
    change = change_of(mine_ref, other_ref, left_ref[...], right, half)
    at = LANES // 2

    def use(value):
        sums = dot_nn(weight_ref[...] * value, right)
        sums_ref[:half, :] = pack(sums)
        sums_ref[half:, :] = jnp.zeros((BIAS, LANES), jnp.float32)

        @pl.when(core == 1)
        def _():
            sums_ref[half : half + 2, :] = bias_rows(sums.T[at : at + 1])

    with_bias(change, mine_ref, other_ref, half, use)


def second_kernel(group, parts, *refs):
    sum_refs, (send_ref, diag_ref, second_ref, dots_ref) = refs[:parts], refs[parts:]
    total = sum_refs[0][...]
    for ref in sum_refs[1:]:
        total = total + ref[...]
    half = total.shape[0] - BIAS
    row = lax.broadcasted_iota(jnp.int32, total.shape, 0)
    used = row < half + 2
    first = jnp.where(used, send_ref[: half + BIAS, :], 0.0)
    diag = diag_ref[...]
    lift = jnp.where(used, total + first - diag * first, 0.0)
    second = lift / diag
    second_ref[...] = second
    terms = (first * first * diag, first * lift, second * lift, second * second)
    dots_ref[...] = jnp.concatenate(
        [jnp.sum(term, axis=0, keepdims=True) for term in terms] + [jnp.zeros((8 - len(terms), LANES), jnp.float32)], 0
    ) * (1.0 / group)


def form_kernel(mine_ref, other_ref, left_ref, right_ref, weight_ref, dots_ref, out_ref):
    core, _, _ = position()
    half = left_ref.shape[0] // 2

    def give(terms):
        row = lax.broadcasted_iota(jnp.int32, (8, LANES), 0)
        lane = lax.broadcasted_iota(jnp.int32, (8, LANES), 1)
        sums = jnp.sum(terms, axis=1, keepdims=True)
        dots = jnp.sum(jnp.where(lane == row, sums, 0.0), axis=0, keepdims=True)
        out_ref[...] = jnp.broadcast_to(dots[None], out_ref.shape)

    @pl.when(core == 0)
    def _():
        change = change_of(mine_ref, other_ref, left_ref[...], right_ref[...], half)
        change = change + bias_lanes(other_ref[half : half + 2, :])
        form = jnp.sum(weight_ref[...] * change * change, axis=0, keepdims=True)
        row = lax.broadcasted_iota(jnp.int32, (8, LANES), 0)
        give(dots_ref[...] + jnp.where(row == 3, form[:, :LANES] + form[:, LANES:], 0.0))

    @pl.when(core == 1)
    def _():
        give(dots_ref[...])


def finish_kernel(
    group, dots_ref, send_ref, peer_ref, second_ref, peer_second_ref, whole_ref, theta_ref, disc_ref, icpt_ref
):
    core, line, plane = position()
    dots = jnp.sum(dots_ref[...], axis=0)
    lane = lax.broadcasted_iota(jnp.int32, (8, LANES), 1)
    row = lax.broadcasted_iota(jnp.int32, (8, LANES), 0)
    sums = jnp.sum(jnp.where(lane == row, dots, 0.0), axis=1, keepdims=True)
    a, f, h, d = [sums[at : at + 1] for at in range(4)]
    b = a + f
    e = f + h
    det = b * d - e * e
    s = (a * d - e * f) / det
    t = (f * f - a * h) / det
    rows = whole_ref.shape[0]
    half = rows // 2
    size = rows // (2 * group)

    def direction(first_ref, next_ref, at):
        upper = at // group
        rows_at = pl.ds(pl.multiple_of(lax.rem(at, group) * size, size), size)
        value = s * first_ref[rows_at, :] + t * next_ref[rows_at, :]
        return jnp.where(upper == 1, turn(value), value)

    mine_at = block_of(core, core, line, plane, group)
    other_at = block_of(1 - core, core, line, plane, group)
    mine = direction(send_ref, second_ref, mine_at)
    mine = mine * jnp.sqrt(whole_ref[pl.ds(pl.multiple_of(mine_at * size, size), size), :])
    other = direction(peer_ref, peer_second_ref, other_at) * jnp.sqrt(peer_ref[half + BIAS :, :])
    theta_ref[...] = jnp.where(core == 0, mine, other)[:, : LANES // 2]
    disc_ref[...] = jnp.where(core == 0, other, mine)[:, : LANES // 2]
    ask = jnp.where(core == 0, peer_ref[half : half + BIAS, :], send_ref[half : half + BIAS, :])
    ask_next = jnp.where(core == 0, peer_second_ref[half : half + 2, :], second_ref[half : half + 2, :])
    bias = (s * ask[0:2] + t * ask_next) * jnp.sqrt(ask[2:4])
    disc_at = jnp.where(core == 0, other_at, mine_at)
    row = jnp.where(disc_at // group == 1, bias[1:2], bias[0:1])
    back = lax.rem(LANES - lax.rem(disc_at, group) * size, LANES)
    icpt_ref[...] = pltpu.roll(row, back, 1)[:, :size]


def call(kernel, shapes, *args):
    out = [jax.ShapeDtypeStruct(shape, jnp.float32) for shape in shapes]
    return pl.pallas_call(
        kernel,
        out_shape=out,
        in_specs=[pl.BlockSpec(memory_space=pltpu.VMEM)] * len(args),
        out_specs=[pl.BlockSpec(memory_space=pltpu.VMEM)] * len(out),
        compiler_params=pltpu.CompilerParams(vmem_limit_bytes=32 * 2**20),
    )(*args)


def swap_cores(value, n_stu, n_que):
    return lax.ppermute(value, AXES, [(i, i ^ 1) for i in range(n_stu * n_que)])


def send_over(value, step, n_stu, n_que, crossed=False):
    pairs = []
    for stu in range(n_stu):
        for que in range(n_que):
            there = (stu, que ^ (2 * step)) if (que % 2 == 0) != crossed else (stu ^ step, que)
            pairs.append((stu * n_que + que, there[0] * n_que + there[1]))
    return lax.ppermute(value, AXES, pairs)


def stages(group, order):
    base = 1
    while base < group:
        width = min(4, group // base)
        yield [base * k for k in order if k < width]
        base *= width


def shards(n_stu, n_que, codes, theta, disc, intercept):
    group = n_stu
    assert n_que == 2 * group
    send = functools.partial(send_over, n_stu=n_stu, n_que=n_que)
    swap = functools.partial(swap_cores, n_stu=n_stu, n_que=n_que)
    size, width = theta.shape
    rows = 2 * group * size
    half = rows // 2
    assert width == LANES // 2 and rows == 2 * LANES
    assert disc.shape == theta.shape and codes.shape == (rows, half)
    core = lax.rem(lax.axis_index("que"), 2)
    peer_theta, peer_disc, peer_icpt = swap(theta), swap(disc), swap(intercept)

    def block(own, own_icpt, peers, peers_icpt):
        icpt = jnp.pad(jnp.stack([own_icpt, peers_icpt]), ((0, 0), (0, width - size))).reshape(1, LANES)
        spare = jnp.zeros((BIAS - 1, LANES), jnp.float32)
        return jnp.concatenate([jnp.concatenate([own, peers], 1), icpt, spare], 0)

    def side(students, questions):
        return jnp.where(core == 0, students, questions)

    mine = [block(side(theta, disc), intercept, side(peer_theta, peer_disc), peer_icpt)]
    other = [block(side(peer_disc, peer_theta), peer_icpt, side(disc, theta), intercept)]
    (code,) = call(arrange_kernel, [(rows, rows)], codes, swap(codes))
    places = [0]
    for steps in stages(group, GATHER_ORDER):
        ours, theirs = jnp.concatenate(mine, 0), jnp.concatenate(other, 0)
        for step in steps:
            crossed = step == max(steps)
            piece = send(theirs if crossed else ours, step, crossed=crossed)
            back = swap(piece)
            mine.append(back if crossed else piece)
            other.append(piece if crossed else back)
        places = places + [step + place for step in steps for place in places]

    def totals(value, order):
        parts = [value]
        for number, steps in enumerate(stages(group, order)):
            if number:
                parts = [functools.reduce(jnp.add, parts)]
            parts = parts + [send(parts[0], step) for step in steps]
        return parts

    sums, left, right, weight, icpt = call(
        functools.partial(gradient_kernel, group, tuple(places), len(mine)),
        [(rows + BIAS, LANES), (rows, LANES), (rows, LANES), (rows, rows), (BIAS, LANES)],
        *mine,
        *other,
        code,
    )
    parts = totals(sums, FIRST_ORDER)
    first, diag, whole = call(
        functools.partial(start_kernel, group, len(parts)),
        [(half + BIAS + size, LANES), (half + BIAS, LANES), (rows, LANES)],
        *parts,
        left,
        icpt,
    )
    peer = swap(first)
    (sums,) = call(image_kernel, [(half + BIAS, LANES)], first, peer, left, right, weight)
    parts = totals(sums, SECOND_ORDER)
    second, dots = call(
        functools.partial(second_kernel, group, len(parts)),
        [(half + BIAS, LANES), (8, LANES)],
        *parts,
        first,
        diag,
    )
    peer_second = swap(second)
    devices = n_stu * n_que
    (dots,) = call(form_kernel, [(devices, 1, LANES)], second, peer_second, left, right, weight, dots)
    dots = lax.all_to_all(dots, AXES, 0, 0, tiled=True)
    abilities, discs, icpts = call(
        functools.partial(finish_kernel, group),
        [(size, width), (size, width), (1, size)],
        dots,
        first,
        peer,
        second,
        peer_second,
        whole,
    )
    return abilities, discs, icpts[0]


def solution(mesh):
    placed = (P("stu", "que"), P(("stu", "que"), None), P(("que", "stu"), None), P(("que", "stu")))
    return jax.shard_map(
        functools.partial(shards, mesh.shape["stu"], mesh.shape["que"]),
        mesh=mesh,
        in_specs=placed,
        out_specs=(P(("stu", "que"), None), P(("que", "stu"), None), P(("que", "stu"))),
        check_vma=False,
    )
```
